32 devices in a mesh: clip: 16 (over z, x, core), slab: 2 (over y).
Axes of the slice: x: 2, y: 2, z: 4, core: 2. Of those that a mesh axis runs over, the one named last changes fastest.
Arguments:
- inputs: bfloat16 [128, 64, 8, 512], P('clip', 'slab'), may hold values from -6 to 6
- grad_mask: int32 [128, 64, 8], P('clip', 'slab'), may hold values from 0 to 1, as said below
- cotangent: bfloat16 [128, 64, 8, 512], P('clip', 'slab'), may hold values from -6 to 6
- ln1_gain: bfloat16 [512], P(('clip', 'slab')), may hold values from 0.099609375 to 1.8984375
- ln1_bias: bfloat16 [512], P(('clip', 'slab')), may hold values from -3 to 3
- w_qkv: bfloat16 [512, 1536], P(('clip', 'slab')), may hold values from -0.25 to 0.25
- q_bias: bfloat16 [512], P(('clip', 'slab')), may hold values from -3 to 3
- v_bias: bfloat16 [512], P(('clip', 'slab')), may hold values from -3 to 3
- w_proj: bfloat16 [512, 512], P(('clip', 'slab')), may hold values from -1 to 1
- proj_bias: bfloat16 [512], P(('clip', 'slab')), may hold values from -3 to 3
- ln2_gain: bfloat16 [512], P(('clip', 'slab')), may hold values from 0.099609375 to 1.8984375
- ln2_bias: bfloat16 [512], P(('clip', 'slab')), may hold values from -3 to 3
- w_fc1: bfloat16 [512, 2048], P(('clip', 'slab')), may hold values from -0.25 to 0.25
- fc1_bias: bfloat16 [2048], P(('clip', 'slab')), may hold values from -3 to 3
- w_fc2: bfloat16 [2048, 512], P(('clip', 'slab')), may hold values from -0.125 to 0.125
- fc2_bias: bfloat16 [512], P(('clip', 'slab')), may hold values from -3 to 3
- pos_table: float32 [49, 16], replicated, may hold values from -4 to 4
Outputs:
- output: bfloat16 [128, 64, 8, 512], P('clip', 'slab')
- input_grad: bfloat16 [128, 64, 8, 512], P('clip', 'slab')
- ln1_gain_grad: float32 [512], P(('clip', 'slab'))
- ln1_bias_grad: float32 [512], P(('clip', 'slab'))
- w_qkv_grad: float32 [512, 1536], P(('clip', 'slab'))
- q_bias_grad: float32 [512], P(('clip', 'slab'))
- v_bias_grad: float32 [512], P(('clip', 'slab'))
- w_proj_grad: float32 [512, 512], P(('clip', 'slab'))
- proj_bias_grad: float32 [512], P(('clip', 'slab'))
- ln2_gain_grad: float32 [512], P(('clip', 'slab'))
- ln2_bias_grad: float32 [512], P(('clip', 'slab'))
- w_fc1_grad: float32 [512, 2048], P(('clip', 'slab'))
- fc1_bias_grad: float32 [2048], P(('clip', 'slab'))
- w_fc2_grad: float32 [2048, 512], P(('clip', 'slab'))
- fc2_bias_grad: float32 [512], P(('clip', 'slab'))
- pos_table_grad: float32 [49, 16], replicated
The draws below stay inside these ranges and needn't reach their ends.
Inputs may be any that keep to these rules, and one draw needn't show every extreme that they name: grad_mask[c, t, f] is 1 where patch (t, f) of clip c receives a gradient; each clip's patches are 1 independently with a chance of that clip's own between 0.70 and 0.90.
All inputs are finite; a program needn't handle non-finite values.
Results may differ from the reference program's by a relative error of at most 0.011.
Values may be sent and summed in bfloat16 or wider, within the bound.
A program may use at most 256 MiB of HBM per device.

```python
import math
import jax
import jax.numpy as jnp
from jax import lax

D = 512
HEADS = 16
FF = 2048
HEAD_DIM = 32
GRID_T = 64
GRID_F = 8
WIN = 4
SHIFT = 2
CLIPS = 128
TABLE = 49


def draw_grad_mask(key, part):
    rate_key, patch_key = jax.random.split(key)
    rates = jax.random.randint(rate_key, (CLIPS, 1, 1), 70, 91)
    patches = jax.random.randint(patch_key, (CLIPS, GRID_T, GRID_F), 0, 100)
    return (patches < rates).astype(jnp.int32)


def levels(rng, extent, cuts, smallest, top_value):
    factor_of, own = 1.0, jax.random.fold_in(rng, 6)
    for dim, shards_of in cuts:
        heights = jnp.exp(jax.random.uniform(jax.random.fold_in(own, dim), (shards_of,), jnp.float32, smallest / len(cuts), top_value / len(cuts)))
        factor_of = factor_of * jnp.repeat(heights, extent[dim] // shards_of).reshape([-1 if axis == dim else 1 for axis in range(len(extent))])
    return factor_of


def scatter_about(rng, extent, scale, bound, cuts=(), held_as=jnp.bfloat16):
    array = jax.random.normal(rng, extent, jnp.float32) * scale
    if len(cuts) > 0:
        array = levels(rng, extent, cuts, -0.22, 0.18) * array
    return jnp.clip(array, min=-bound, max=bound).astype(held_as)


def setup_inputs(seed: int = 0) -> dict:
    key_of = jax.random.split(jax.random.key(seed), 18)
    inputs = scatter_about(key_of[0], (CLIPS, GRID_T, GRID_F, D), 1.0, 6.0, ((0, 16), (1, 2)))
    grad_mask = draw_grad_mask(jax.random.fold_in(key_of[17], 71), 0)
    cotangent = scatter_about(key_of[2], (CLIPS, GRID_T, GRID_F, D), 1.0, 6.0, ((0, 16), (1, 2)))
    ln1_gain = jnp.clip(1.0 + 0.18 * jax.random.normal(key_of[3], (D,), jnp.float32), 0.099609375, 1.8984375).astype(jnp.bfloat16)
    ln1_bias = scatter_about(key_of[4], (D,), 0.5, 3.0, ((0, 32),))
    w_qkv = scatter_about(key_of[5], (D, 3 * D), D ** -0.5, 0.25, ((0, 32),))
    q_bias = scatter_about(key_of[6], (D,), 0.5, 3.0, ((0, 32),))
    v_bias = scatter_about(key_of[7], (D,), 0.5, 3.0, ((0, 32),))
    w_proj = scatter_about(key_of[8], (D, D), (D // 16) ** -0.5, 1.0, ((0, 32),))
    proj_bias = scatter_about(key_of[9], (D,), 0.5, 3.0, ((0, 32),))
    ln2_gain = jnp.clip(1.0 + 0.18 * jax.random.normal(key_of[10], (D,), jnp.float32), 0.099609375, 1.8984375).astype(jnp.bfloat16)
    ln2_bias = scatter_about(key_of[11], (D,), 0.5, 3.0, ((0, 32),))
    w_fc1 = scatter_about(key_of[12], (D, FF), D ** -0.5, 0.25, ((0, 32),))
    fc1_bias = scatter_about(key_of[13], (FF,), 0.5, 3.0, ((0, 32),))
    w_fc2 = scatter_about(key_of[14], (FF, D), FF ** -0.5, 0.125, ((0, 32),))
    fc2_bias = scatter_about(key_of[15], (D,), 0.5, 3.0, ((0, 32),))
    pos_table = scatter_about(key_of[16], (TABLE, HEADS), 1.0, 4.0, (), jnp.float32)
    return {"inputs": inputs, "grad_mask": grad_mask, "cotangent": cotangent, "ln1_gain": ln1_gain, "ln1_bias": ln1_bias, "w_qkv": w_qkv, "q_bias": q_bias, "v_bias": v_bias, "w_proj": w_proj, "proj_bias": proj_bias, "ln2_gain": ln2_gain, "ln2_bias": ln2_bias, "w_fc1": w_fc1, "fc1_bias": fc1_bias, "w_fc2": w_fc2, "fc2_bias": fc2_bias, "pos_table": pos_table}


epsilon = 1e-06
highest = lax.Precision.HIGHEST

@jax.custom_vjp
def low(v):
    return lax.optimization_barrier(v.astype(jnp.bfloat16)).astype(jnp.float32)

@jax.custom_vjp
def low_back(v):
    return v

def low_keep(v):
    return (low(v), None)

def low_pass(kept, grad):
    return (grad,)

def back_keep(v):
    return (v, None)

def back_low(kept, grad):
    return (low(grad),)
low.defvjp(low_keep, low_pass)
low_back.defvjp(back_keep, back_low)

def normalize(values, gain_row, bias_row):
    average = lax.optimization_barrier(jnp.mean(values, -1, keepdims=True))
    centred = values - average
    variance = lax.optimization_barrier(jnp.mean(centred * centred, -1, keepdims=True))
    return centred * lax.rsqrt(variance + epsilon) * gain_row + bias_row

def table_onehot():
    positions = jnp.arange(WIN * WIN)
    row_of = positions // WIN
    column_of = positions % WIN
    table_index = (row_of[:, None] - row_of[None, :] + WIN - 1) * (2 * WIN - 1) + column_of[:, None] - column_of[None, :] + WIN - 1
    return (table_index.reshape(-1)[:, None] == jnp.arange(TABLE)[None, :]).astype(jnp.float32)

def to_windows(field_grid):
    clip_count, row_count, column_count, feature_width = field_grid.shape
    blocks = field_grid.reshape(clip_count, row_count // WIN, WIN, column_count // WIN, WIN, feature_width)
    return blocks.transpose(0, 1, 3, 2, 4, 5).reshape(-1, WIN * WIN, feature_width)

def from_windows(windows, clip_count, row_count, column_count):
    feature_width = windows.shape[-1]
    blocks = windows.reshape(clip_count, row_count // WIN, column_count // WIN, WIN, WIN, feature_width)
    return blocks.transpose(0, 1, 3, 2, 4, 5).reshape(clip_count, row_count, column_count, feature_width)

def forward(inputs, params):
    ln1_gain, ln1_bias, w_qkv, q_bias, v_bias, w_proj, proj_bias, ln2_gain, ln2_bias, w_fc1, fc1_bias, w_fc2, fc2_bias, pos_table = params
    clip_count, row_count, column_count, feature_width = inputs.shape
    score_scale = 1.0 / math.sqrt(HEAD_DIM)
    normed = low(normalize(inputs, ln1_gain, ln1_bias))
    windows = to_windows(jnp.roll(normed, (-SHIFT, -SHIFT), axis=(1, 2)))
    window_count = windows.shape[0]
    head_shape = (window_count, WIN * WIN, HEADS, HEAD_DIM)
    projected = jnp.einsum('wtd,de->wte', windows, w_qkv, precision=highest)
    query_heads = low_back(low(projected[..., :D] + q_bias)).reshape(head_shape)
    key_heads = low_back(low(projected[..., D:2 * D])).reshape(head_shape)
    value_heads = low_back(low(projected[..., 2 * D:] + v_bias)).reshape(head_shape)
    position_bias = jnp.dot(table_onehot(), pos_table, precision=highest).reshape(WIN * WIN, WIN * WIN, HEADS).transpose(2, 0, 1)
    raw_scores = jnp.einsum('wqhc,wkhc->whqk', query_heads, key_heads, precision=highest) * score_scale
    scores = low_back(raw_scores + position_bias[None])
    attention = low(jax.nn.softmax(scores, axis=-1))
    context = jnp.einsum('whqk,wkhc->wqhc', attention, value_heads, precision=highest).reshape(window_count, WIN * WIN, D)
    context = low_back(low(context))
    context_grid = jnp.roll(from_windows(context, clip_count, row_count, column_count), (SHIFT, SHIFT), axis=(1, 2))
    branch = jnp.einsum('ctfd,de->ctfe', context_grid, w_proj, precision=highest) + proj_bias
    middle = inputs + low_back(branch)
    second = low(normalize(middle, ln2_gain, ln2_bias))
    pre_act = low_back(jnp.einsum('ctfd,de->ctfe', second, w_fc1, precision=highest) + fc1_bias)
    hidden = low(jax.nn.gelu(pre_act, approximate=False))
    return middle + jnp.einsum('ctfe,ed->ctfd', hidden, w_fc2, precision=highest) + fc2_bias

def reference(inputs, grad_mask, cotangent, ln1_gain, ln1_bias, w_qkv, q_bias, v_bias, w_proj, proj_bias, ln2_gain, ln2_bias, w_fc1, fc1_bias, w_fc2, fc2_bias, pos_table):
    params = tuple((member.astype(jnp.float32) for member in (ln1_gain, ln1_bias, w_qkv, q_bias, v_bias, w_proj, proj_bias, ln2_gain, ln2_bias, w_fc1, fc1_bias, w_fc2, fc2_bias, pos_table)))
    group_size = math.gcd(CLIPS, 8)
    group_count = CLIPS // group_size

    def one_group(running, batch):
        group_inputs, group_mask, group_cotangent = batch
        result, pullback = jax.vjp(forward, group_inputs.astype(jnp.float32), params)
        incoming = group_cotangent.astype(jnp.float32) * group_mask.astype(jnp.float32)[..., None]
        group_input_grad, param_grads = pullback(incoming)
        running = tuple((total_now + update for total_now, update in zip(running, param_grads)))
        return (running, (result.astype(jnp.bfloat16), group_input_grad.astype(jnp.bfloat16)))

    def grouped(array_in):
        return array_in.reshape((group_count, group_size) + array_in.shape[1:])
    zeros = tuple((jnp.zeros(member.shape, jnp.float32) for member in params))
    totals, (output, input_grad) = lax.scan(one_group, zeros, (grouped(inputs), grouped(grad_mask), grouped(cotangent)))
    output = output.reshape(inputs.shape)
    input_grad = input_grad.reshape(inputs.shape)
    return (output, input_grad, totals[0], totals[1], totals[2], totals[3], totals[4], totals[5], totals[6], totals[7], totals[8], totals[9], totals[10], totals[11], totals[12], totals[13])
```

```python
import functools
import math

import jax
import jax.numpy as jnp
from jax import lax
from jax.experimental import pallas as pl
from jax.experimental.pallas import tpu as pltpu
from jax.sharding import PartitionSpec as P

F32 = jnp.float32
BF = jnp.bfloat16
MESH = pl.DeviceIdType.MESH
SCALE = 1.0 / math.sqrt(32.0)
NT = (((1,), (1,)), ((), ()))
TN = (((0,), (0,)), ((), ()))
VM = pl.BlockSpec(memory_space=pltpu.VMEM)
HB = pl.BlockSpec(memory_space=pl.ANY)
UNROLL = 16


def dot(a, b, dims=(((1,), (0,)), ((), ()))):
    return lax.dot_general(a, b, dims, preferred_element_type=F32)


def tree(xs, op=lambda a, b: a + b):
    xs = list(xs)
    while len(xs) > 1:
        xs = [op(xs[i], xs[i + 1]) if i + 1 < len(xs) else xs[i] for i in range(0, len(xs), 2)]
    return xs[0]


def tile(ref, i):
    return ref[pl.ds(pl.multiple_of(i * 16, 16), 16), :]


def row(ref, i):
    return jnp.broadcast_to(ref[pl.ds(i, 1), :], (16, 128))


def pair_products(a_ref, a0, b_ref, b0):
    def body(d, acc):
        ad = tile(a_ref, a0 + d)
        return tuple(acc[q] + ad * row(b_ref, (b0 + d) * 16 + q) for q in range(16))

    return lax.fori_loop(
        0, 32, body, tuple(jnp.zeros((16, 128), F32) for _ in range(16)), unroll=UNROLL
    )


def weighted(ws, b_ref, b0, o_ref, o0, scale):
    def body(d, carry):
        parts = []
        for k in range(4):
            t = ws[4 * k] * row(b_ref, (b0 + d) * 16 + 4 * k)
            for q in range(4 * k + 1, 4 * k + 4):
                t = t + ws[q] * row(b_ref, (b0 + d) * 16 + q)
            parts.append(t)
        s = (parts[0] + parts[1]) + (parts[2] + parts[3])
        if scale is not None:
            s = s * scale
        o_ref[pl.ds(pl.multiple_of((o0 + d) * 16, 16), 16), :] = s.astype(BF).astype(F32)
        return carry

    lax.fori_loop(0, 32, body, 0, unroll=UNROLL)


class Place:
    def __init__(self):
        self.clip = lax.axis_index("clip")
        self.y = lax.axis_index("slab")
        self.c = self.clip % 2
        self.x = (self.clip // 2) % 2
        self.z = self.clip // 4
        self.rank8 = self.x * 4 + self.c * 2 + self.y
        base = self.x * 2 + self.c
        self.along_z = [(((self.z + d) % 4) * 4 + base, self.y) for d in (1, 2, 3)]
        self.over_x = (self.clip + 2 - 4 * self.x, self.y)
        self.over_y = (self.clip, 1 - self.y)
        self.over_core = (self.clip + 1 - 2 * self.c, self.y)

    def greet(self):
        barrier = pltpu.get_barrier_semaphore()
        others = self.along_z + [self.over_x, self.over_y, self.over_core]
        for other in others:
            pl.semaphore_signal(barrier, inc=1, device_id=other, device_id_type=MESH)
        pl.semaphore_wait(barrier, len(others))


def remote(src, dst, ssem, rsem, to):
    return pltpu.make_async_remote_copy(
        src_ref=src, dst_ref=dst, send_sem=ssem, recv_sem=rsem, device_id=to, device_id_type=MESH
    )


class Gather:
    def __init__(self, place, pieces, ssem, rsem):
        self.copies = []
        z, x, c, y = place.z, place.x, place.c, place.y
        for k, (buf, c0, n, first_x) in enumerate(pieces):
            cols = pl.ds(c0, n)

            def cp(ix, s, to, k=k, buf=buf, cols=cols):
                ref = buf.at[ix + (slice(None), cols)]
                return remote(ref, ref, ssem.at[k, s], rsem.at[k, s], to)

            al = slice(None)
            steps = [[cp((z, x, c, y), d, place.along_z[d]) for d in range(3)]]
            if first_x:
                steps.append([cp((al, x, c, y), 3, place.over_x)])
                steps.append([cp((al, al, c, y), 4, place.over_y)])
            else:
                steps.append([cp((al, x, c, y), 3, place.over_y)])
                steps.append([cp((al, x, c, al), 4, place.over_x)])
            steps.append([cp((al, al, c, al), 5, place.over_core)])
            self.copies.append(steps)

    def start(self, k, s):
        for copy in self.copies[k][s]:
            copy.start()

    def advance(self, k, s):
        for copy in self.copies[k][s]:
            copy.wait_recv()
        if s < 3:
            self.start(k, s + 1)

    def close(self):
        for steps in self.copies:
            for step in steps:
                for copy in step:
                    copy.wait_send()


def spots(p):
    i, j = p // 4, p % 4
    return (i * 8 + (j + 2) % 8, i * 8 + (j + 6) % 8)


def gathered(ref, lo, hi):
    return jnp.concatenate([ref[pl.ds(lo, 64, stride=32), :], ref[pl.ds(hi, 64, stride=32), :]], axis=0)


def small_block(place, small_refs, fc1b_ref, scr):
    scr[...] = jnp.zeros_like(scr)
    for k, ref in enumerate(small_refs):
        scr[k : k + 1, 0:16] = ref[...].astype(F32)
    lane = lax.broadcasted_iota(jnp.int32, (128, 128), 1)
    src = lax.broadcasted_iota(jnp.int32, (128, 128), 0)
    sel = ((lane == place.rank8 * 16 + src) & (src < 16)).astype(F32).astype(BF)
    vectors = dot(scr[...].astype(BF), sel)
    scr[0:1, 0:64] = fc1b_ref[...].astype(F32)
    half = ((lane == place.y * 64 + src) & (src < 64)).astype(F32).astype(BF)
    wide = dot(scr[0:1, :].astype(BF), half)
    r = lax.broadcasted_iota(jnp.int32, (16, 128), 0)
    return jnp.where(
        r < 8,
        vectors,
        jnp.where(r == 8 + place.x * 2 + place.c, jnp.broadcast_to(wide, (16, 128)), 0.0),
    ).astype(BF)


def k1_body(
    x_ref, wq_ref, wp_ref, w1_ref, w2_ref, s0, s1, s2, s3, s4, s5, s6, s7, fb_ref, bt_ref,
    ctx_ref, wqb, wpb, w1b, w2b, par_ref, qkv_save, att_save, ctxt_ref, normt_ref, nt_ref, rs_ref,
    xs, ntf, g_ref, ct_ref, cs_ref, a_ref, qb, halo, chalo, gains, scr,
    ssem, rsem, hss, hrs, lsem, osem,
):
    me = Place()
    z, x, c, y = me.z, me.x, me.c, me.y
    own = [
        pltpu.make_async_copy(src, buf.at[z, x, c, y], osem.at[i])
        for i, (src, buf) in enumerate(((wp_ref, wpb), (w1_ref, w1b), (w2_ref, w2b)))
    ]
    for cp in own:
        cp.start()
    wqb[z, x, c, y, :, 0:128] = small_block(me, (s0, s1, s2, s3, s4, s5, s6, s7), fb_ref, scr)
    for g in range(4):
        for k in range(3):
            wqb[z, x, c, y, :, 128 + g * 384 + k * 128 : 256 + g * 384 + k * 128] = wq_ref[
                :, k * 512 + g * 128 : k * 512 + g * 128 + 128
            ]
    pieces = [(wqb, 0, 512, True)] + [(wqb, 128 + g * 384, 384, g % 2 == 0) for g in (1, 2, 3)]
    pieces += [(wpb, 0, 256, True), (wpb, 256, 256, False)]
    pieces += [(w1b, 0, 1024, True), (w1b, 1024, 1024, False)]
    pieces += [(w2b, 0, 256, True), (w2b, 256, 256, False)]
    gat = Gather(me, pieces, ssem, rsem)
    me.greet()
    for k in range(4):
        gat.start(k, 0)
    xhalo = remote(x_ref.at[:, 0:16, :], halo, hss.at[4], hrs.at[4], me.over_y)
    xhalo.start()
    for b in range(8):
        for k in range(4):
            xs[k, b * 256 : b * 256 + 240, :] = x_ref[b, 16:256, k * 128 : k * 128 + 128].astype(F32)
    gat.advance(0, 0)
    gat.advance(1, 0)
    xhalo.wait_recv()
    for b in range(8):
        for k in range(4):
            xs[k, b * 256 + 240 : b * 256 + 256, :] = halo[b, :, k * 128 : k * 128 + 128].astype(F32)

    def norm_block(p):
        lo, hi = spots(p)
        turned = jnp.concatenate([gathered(xs.at[k], lo, hi).T for k in range(4)], axis=0)
        mean = jnp.mean(turned, 0, keepdims=True)
        cen = turned - mean
        rs = lax.rsqrt(jnp.mean(cen * cen, 0, keepdims=True) + 1e-6)
        ntf[:, p * 128 : (p + 1) * 128] = cen * rs
        rs_ref[p : p + 1, :] = rs

    todo = [(2, 0), (0, 1), (1, 1), (3, 0), (0, 2), (2, 1), (1, 2)]
    for p in range(16):
        norm_block(p)
        if p % 2 == 1 and todo:
            gat.advance(*todo.pop(0))
    for step in todo:
        gat.advance(*step)
    for cp in own:
        cp.wait()
    for k in (4, 5, 6):
        gat.start(k, 0)
    gat.advance(0, 3)
    for zz in range(4):
        total = jnp.sum(wqb[zz, :, :, :, :, 0:128].astype(F32).reshape(8, 16, 128), axis=0)
        par_ref[0:8, zz * 128 : (zz + 1) * 128] = total[0:8]
        for k in range(4):
            par_ref[8 + zz : 9 + zz, k * 128 : (k + 1) * 128] = total[8 + k : 9 + k]
    par_ref[12:16, :] = jnp.zeros((4, 512), F32)
    scr2 = par_ref[...].T
    gains[0] = jnp.broadcast_to(scr2[:, 0:1], (512, 128))
    gains[1] = jnp.broadcast_to(scr2[:, 1:2], (512, 128))
    gains[2] = jnp.broadcast_to(scr2[:, 2:3], (512, 128))
    gains[3] = jnp.broadcast_to(scr2[:, 3:4], (512, 128))

    def finish_norm(p, carry):
        cols = pl.ds(pl.multiple_of(p * 128, 128), 128)
        n = ntf[:, cols]
        normt_ref[:, cols] = (n * gains[0] + gains[1]).astype(BF)
        nt_ref[:, cols] = n.astype(BF)
        return carry

    lax.fori_loop(0, 16, finish_norm, 0)

    plan = [
        [(2, 2), (3, 1), (1, 3)],
        [(3, 2), (4, 0), (5, 0), ("s", 7)],
        [(2, 3), (4, 1), (6, 0), ("s", 8)],
        [(3, 3), (5, 1), (4, 2), (7, 0), ("s", 9)],
        [(6, 1), (5, 2)],
        [(7, 1), (8, 0), (4, 3)],
        [(6, 2), (5, 3)],
        [(8, 1), (9, 0)],
        [(7, 2)],
        [(9, 1), (6, 3)],
        [(8, 2)],
        [(7, 3)],
    ]

    def progress():
        if plan:
            for k, s in plan.pop(0):
                if k == "s":
                    gat.start(s, 0)
                else:
                    gat.advance(k, s)

    saves = []
    chs = []
    for g in range(4):
        w = wqb[:, :, :, :, :, 128 + g * 384 : 512 + g * 384].reshape(512, 384)
        wt = w.astype(F32).T.astype(BF)
        fs = slice(g * 128, (g + 1) * 128)
        if g > 0:
            saves[-1].wait()

        def project(t, carry):
            out = dot(wt, normt_ref[:, pl.ds(pl.multiple_of(t * 512, 512), 512)])
            for k in range(4):
                block = out[:, k * 128 : (k + 1) * 128]
                block = jnp.concatenate(
                    [block[0:128] + gains[2, fs, :], block[128:256], block[256:384] + gains[3, fs, :]],
                    axis=0,
                )
                g_ref[pl.ds(t * 4 + k, 384, stride=16), :] = block.astype(BF).astype(F32)
            return carry

        lax.fori_loop(0, 4, project, 0)

        def keep(i, carry):
            rows = pl.ds(pl.multiple_of(i * 512, 512), 512)
            qb[rows, :] = g_ref[rows, :].astype(BF)
            return carry

        lax.fori_loop(0, 12, keep, 0)
        save = pltpu.make_async_copy(qb, qkv_save.at[g], lsem.at[g])
        save.start()
        saves.append(save)
        progress()

        def head(h, carry, g=g):
            acc = pair_products(g_ref, h * 32, g_ref, 128 + h * 32)
            bt = bt_ref[g * 4 + h]
            s = [
                acc[q] * SCALE + jnp.broadcast_to(bt[:, q : q + 1], (16, 128)) for q in range(16)
            ]
            m = tree(s, jnp.maximum)
            e = [jnp.exp(v - m) for v in s]
            inv = 1.0 / tree(e)
            low = []
            for q in range(16):
                a = e[q] * inv
                a_ref[pl.ds(pl.multiple_of((g * 4 + h) * 256 + q * 16, 16), 16), :] = a
                low.append(a.astype(BF).astype(F32))
            weighted(low, g_ref, 256 + h * 32, ct_ref, h * 32, None)
            return carry

        lax.fori_loop(0, 2, head, 0)
        progress()
        lax.fori_loop(2, 4, head, 0)
        asave = pltpu.make_async_copy(
            a_ref.at[pl.ds(g * 1024, 1024), :], att_save.at[pl.ds(g * 1024, 1024), :], lsem.at[4 + g]
        )
        asave.start()
        chs.append(asave)
        for p in range(16):
            block = ct_ref[pl.ds(p, 128, stride=16), :]
            ctxt_ref[fs, p * 128 : (p + 1) * 128] = block.astype(BF)
            turned = block.T
            lo, hi = spots(p)
            cs_ref[pl.ds(lo, 64, stride=32), :] = turned[0:64]
            cs_ref[pl.ds(hi, 64, stride=32), :] = turned[64:128]
        for b in range(8):
            ctx_ref[b, 16:256, fs] = cs_ref[b * 256 : b * 256 + 240, :].astype(BF)
            chalo[g, b] = cs_ref[b * 256 + 240 : b * 256 + 256, :].astype(BF)
        send = remote(chalo.at[g], ctx_ref.at[:, 0:16, pl.ds(g * 128, 128)], hss.at[g], hrs.at[g], me.over_y)
        send.start()
        chs.append(send)
        progress()
    while plan:
        progress()
    gat.advance(8, 3)
    gat.advance(9, 2)
    gat.advance(9, 3)
    saves[-1].wait()
    for cp in chs:
        cp.wait()
    xhalo.wait_send()
    gat.close()


def k1_call(x, wq, wp, w1, w2, smalls, fb, bt):
    S = jax.ShapeDtypeStruct
    lead = (4, 2, 2, 2)
    outs = [
        (S((8, 256, 512), BF), VM),
        (S(lead + (16, 1664), BF), VM),
        (S(lead + (16, 512), BF), HB),
        (S(lead + (16, 2048), BF), HB),
        (S(lead + (64, 512), BF), HB),
        (S((16, 512), F32), VM),
        (S((4, 6144, 128), BF), HB),
        (S((4096, 128), F32), HB),
        (S((512, 2048), BF), VM),
        (S((512, 2048), BF), VM),
        (S((512, 2048), BF), VM),
        (S((16, 128), F32), VM),
    ]
    V = pltpu.VMEM
    return pl.pallas_call(
        k1_body,
        out_shape=[o[0] for o in outs],
        in_specs=[VM, VM, HB, HB, HB] + [VM] * 10,
        out_specs=[o[1] for o in outs],
        scratch_shapes=[
            V((4, 2048, 128), F32), V((512, 2048), F32), V((6144, 128), F32), V((2048, 128), F32),
            V((2048, 128), F32), V((4096, 128), F32), V((6144, 128), BF), V((8, 16, 512), BF),
            V((4, 8, 16, 128), BF), V((4, 512, 128), F32), V((16, 128), F32),
            pltpu.SemaphoreType.DMA((10, 6)), pltpu.SemaphoreType.DMA((10, 6)),
            pltpu.SemaphoreType.DMA((5,)), pltpu.SemaphoreType.DMA((5,)),
            pltpu.SemaphoreType.DMA((8,)), pltpu.SemaphoreType.DMA((3,)),
        ],
        compiler_params=pltpu.CompilerParams(
            collective_id=1, has_side_effects=True, vmem_limit_bytes=60 << 20
        ),
        name="gather_attend",
    )(x, wq, wp, w1, w2, *smalls, fb, bt)


HEADS = 16
HEAD_DIM = 32
WIN = 4
SHIFT = 2
TABLE = 49


epsilon = 1e-06
highest = lax.Precision.HIGHEST


def from_behind(block, axis, distance):
    devices = range(lax.axis_size(axis))
    route = [((i - distance) % len(devices), i) for i in devices]
    return lax.ppermute(block, axis, route)


def normalize(values, gain_row, bias_row):
    average = jnp.mean(values, -1, keepdims=True)
    centred = values - average
    variance = jnp.mean(centred * centred, -1, keepdims=True)
    return centred * lax.rsqrt(variance + epsilon) * gain_row + bias_row


def exact_gelu(values):
    return jax.nn.gelu(values, approximate=False)


def table_onehot():
    positions = jnp.arange(WIN * WIN)
    row_of = positions // WIN
    column_of = positions % WIN
    table_index = (
        (row_of[:, None] - row_of[None, :] + WIN - 1) * (2 * WIN - 1)
        + column_of[:, None]
        - column_of[None, :]
        + WIN
        - 1
    )
    return (table_index.reshape(-1)[:, None] == jnp.arange(TABLE)[None, :]).astype(jnp.float32)


def to_windows(field_grid):
    clip_count, row_count, column_count, feature_width = field_grid.shape
    blocks = field_grid.reshape(
        clip_count, row_count // WIN, WIN, column_count // WIN, WIN, feature_width
    )
    return blocks.transpose(0, 1, 3, 2, 4, 5).reshape(-1, WIN * WIN, feature_width)


def from_windows(windows, clip_count, row_count, column_count):
    feature_width = windows.shape[-1]
    blocks = windows.reshape(
        clip_count, row_count // WIN, column_count // WIN, WIN, WIN, feature_width
    )
    return blocks.transpose(0, 1, 3, 2, 4, 5).reshape(
        clip_count, row_count, column_count, feature_width
    )


def times_transposed(left, right):
    return lax.dot_general(
        left, right, (((1,), (1,)), ((), ())), preferred_element_type=jnp.float32
    )


def outer_sum(left, right):
    return lax.dot_general(
        left, right, (((0,), (0,)), ((), ())), preferred_element_type=jnp.float32
    )


def per_device(
    inputs,
    grad_mask,
    cotangent,
    ln1_gain,
    ln1_bias,
    w_qkv,
    q_bias,
    v_bias,
    w_proj,
    proj_bias,
    ln2_gain,
    ln2_bias,
    w_fc1,
    fc1_bias,
    w_fc2,
    fc2_bias,
    pos_table,
):
    (
        gain_one,
        bias_one,
        qkv_full,
        qbias_full,
        vbias_full,
        proj_full,
        pbias_full,
        gain_two,
        bias_two,
        fc1_full,
        fc1b_full,
        fc2_full,
        fc2b_full,
    ) = (
        lax.all_gather(ln1_gain, ("clip", "slab"), axis=0, tiled=True),
        lax.all_gather(ln1_bias, ("clip", "slab"), axis=0, tiled=True),
        lax.all_gather(w_qkv, ("clip", "slab"), axis=0, tiled=True),
        lax.all_gather(q_bias, ("clip", "slab"), axis=0, tiled=True),
        lax.all_gather(v_bias, ("clip", "slab"), axis=0, tiled=True),
        lax.all_gather(w_proj, ("clip", "slab"), axis=0, tiled=True),
        lax.all_gather(proj_bias, ("clip", "slab"), axis=0, tiled=True),
        lax.all_gather(ln2_gain, ("clip", "slab"), axis=0, tiled=True),
        lax.all_gather(ln2_bias, ("clip", "slab"), axis=0, tiled=True),
        lax.all_gather(w_fc1, ("clip", "slab"), axis=0, tiled=True),
        lax.all_gather(fc1_bias, ("clip", "slab"), axis=0, tiled=True),
        lax.all_gather(w_fc2, ("clip", "slab"), axis=0, tiled=True),
        lax.all_gather(fc2_bias, ("clip", "slab"), axis=0, tiled=True),
    )
    clip_count, row_count, column_count, feature_width = inputs.shape
    score_scale = 1.0 / math.sqrt(HEAD_DIM)
    float_type = jnp.float32
    half_type = jnp.bfloat16
    ahead = from_behind(inputs[:, :SHIFT], "slab", -1)
    window_rows = jnp.concatenate([inputs[:, SHIFT:], ahead], axis=1).astype(float_type)
    normed, first_pull = jax.vjp(
        normalize, window_rows, gain_one.astype(float_type), bias_one.astype(float_type)
    )
    windows = to_windows(jnp.roll(normed.astype(half_type), -SHIFT, axis=2))
    window_count = windows.shape[0]
    token_count = window_count * WIN * WIN
    head_shape = (window_count, WIN * WIN, HEADS, HEAD_DIM)
    flat_windows = windows.reshape(token_count, feature_width)
    projected = jnp.dot(flat_windows, qkv_full, preferred_element_type=float_type)
    query_heads = (
        (projected[:, :feature_width] + qbias_full.astype(float_type))
        .astype(half_type)
        .reshape(head_shape)
    )
    key_heads = (
        projected[:, feature_width : 2 * feature_width].astype(half_type).reshape(head_shape)
    )
    value_heads = (
        (projected[:, 2 * feature_width :] + vbias_full.astype(float_type))
        .astype(half_type)
        .reshape(head_shape)
    )
    onehot = table_onehot()
    position_bias = (
        jnp.dot(onehot, pos_table, precision=highest)
        .reshape(WIN * WIN, WIN * WIN, HEADS)
        .transpose(2, 0, 1)
    )
    scores = (
        jnp.einsum("wqhc,wkhc->whqk", query_heads, key_heads, preferred_element_type=float_type)
        * score_scale
        + position_bias[None]
    )
    attention = jax.nn.softmax(scores, axis=-1)
    attention_low = attention.astype(half_type)
    context = jnp.einsum(
        "whqk,wkhc->wqhc", attention_low, value_heads, preferred_element_type=float_type
    )
    context = context.astype(half_type).reshape(window_count, WIN * WIN, feature_width)
    context_grid = jnp.roll(
        from_windows(context, clip_count, row_count, column_count), SHIFT, axis=2
    )
    returned = from_behind(context_grid[:, row_count - SHIFT :], "slab", 1)
    own_flat = jnp.concatenate([returned, context_grid[:, : row_count - SHIFT]], axis=1).reshape(
        -1, feature_width
    )
    input_flat = inputs.reshape(-1, feature_width).astype(float_type)
    middle = (
        input_flat
        + jnp.dot(own_flat, proj_full, preferred_element_type=float_type)
        + pbias_full.astype(float_type)
    )
    second, second_pull = jax.vjp(
        normalize, middle, gain_two.astype(float_type), bias_two.astype(float_type)
    )
    second_low = second.astype(half_type)
    pre_act = jnp.dot(second_low, fc1_full, preferred_element_type=float_type) + fc1b_full.astype(
        float_type
    )
    hidden, gelu_pull = jax.vjp(exact_gelu, pre_act)
    hidden_low = hidden.astype(half_type)
    output = (
        middle
        + jnp.dot(hidden_low, fc2_full, preferred_element_type=float_type)
        + fc2b_full.astype(float_type)
    )
    incoming = (cotangent.astype(float_type) * grad_mask.astype(float_type)[..., None]).reshape(
        -1, feature_width
    )
    incoming_low = incoming.astype(half_type)
    fc2_grad = outer_sum(hidden_low, incoming_low)
    fc2b_grad = jnp.sum(incoming, axis=0)
    hidden_grad = times_transposed(incoming_low, fc2_full)
    pre_grad = gelu_pull(hidden_grad)[0].astype(half_type)
    fc1_grad = outer_sum(second_low, pre_grad)
    fc1b_grad = jnp.sum(pre_grad.astype(float_type), axis=0)
    second_grad = times_transposed(pre_grad, fc1_full)
    middle_part, gain_two_grad, bias_two_grad = second_pull(second_grad)
    middle_grad = incoming + middle_part
    branch_low = middle_grad.astype(half_type)
    proj_grad = outer_sum(own_flat, branch_low)
    pbias_grad = jnp.sum(branch_low.astype(float_type), axis=0)
    context_grad = (
        times_transposed(branch_low, proj_full)
        .astype(half_type)
        .reshape(clip_count, row_count, column_count, feature_width)
    )
    sent_back = from_behind(context_grad[:, :SHIFT], "slab", -1)
    window_context_grad = jnp.concatenate([context_grad[:, SHIFT:], sent_back], axis=1)
    context_heads = to_windows(jnp.roll(window_context_grad, -SHIFT, axis=2)).reshape(head_shape)
    value_grad = jnp.einsum(
        "whqk,wqhc->wkhc", attention_low, context_heads, preferred_element_type=float_type
    ).astype(half_type)
    attention_grad = jnp.einsum(
        "wqhc,wkhc->whqk", context_heads, value_heads, preferred_element_type=float_type
    )
    score_grad = (
        attention * (attention_grad - jnp.sum(attention_grad * attention, -1, keepdims=True))
    ).astype(half_type)
    bias_cells = (
        jnp.sum(score_grad.astype(float_type), axis=0)
        .transpose(1, 2, 0)
        .reshape(WIN * WIN * WIN * WIN, HEADS)
    )
    table_grad = lax.dot_general(onehot, bias_cells, (((0,), (0,)), ((), ())), precision=highest)
    query_grad = (
        jnp.einsum("whqk,wkhc->wqhc", score_grad, key_heads, preferred_element_type=float_type)
        * score_scale
    ).astype(half_type)
    key_grad = (
        jnp.einsum("whqk,wqhc->wkhc", score_grad, query_heads, preferred_element_type=float_type)
        * score_scale
    ).astype(half_type)
    query_flat = query_grad.reshape(token_count, feature_width)
    value_flat = value_grad.reshape(token_count, feature_width)
    qkv_grad_low = jnp.concatenate(
        [query_flat, key_grad.reshape(token_count, feature_width), value_flat], axis=1
    )
    qkv_grad = outer_sum(flat_windows, qkv_grad_low)
    qbias_grad = jnp.sum(query_flat.astype(float_type), axis=0)
    vbias_grad = jnp.sum(value_flat.astype(float_type), axis=0)
    normed_grad = times_transposed(qkv_grad_low, qkv_full).reshape(
        window_count, WIN * WIN, feature_width
    )
    normed_grid_grad = jnp.roll(
        from_windows(normed_grad, clip_count, row_count, column_count), SHIFT, axis=2
    )
    rows_part, gain_one_grad, bias_one_grad = first_pull(normed_grid_grad)
    halo_back = from_behind(
        rows_part[:, row_count - SHIFT :].astype(jnp.bfloat16), "slab", 1
    ).astype(jnp.float32)
    input_grad = middle_grad.reshape(
        clip_count, row_count, column_count, feature_width
    ) + jnp.concatenate([halo_back, rows_part[:, : row_count - SHIFT]], axis=1)
    shares = (
        lax.psum_scatter(gain_one_grad, ("clip", "slab"), scatter_dimension=0, tiled=True),
        lax.psum_scatter(bias_one_grad, ("clip", "slab"), scatter_dimension=0, tiled=True),
        lax.psum_scatter(qkv_grad, ("clip", "slab"), scatter_dimension=0, tiled=True),
        lax.psum_scatter(qbias_grad, ("clip", "slab"), scatter_dimension=0, tiled=True),
        lax.psum_scatter(vbias_grad, ("clip", "slab"), scatter_dimension=0, tiled=True),
        lax.psum_scatter(proj_grad, ("clip", "slab"), scatter_dimension=0, tiled=True),
        lax.psum_scatter(pbias_grad, ("clip", "slab"), scatter_dimension=0, tiled=True),
        lax.psum_scatter(gain_two_grad, ("clip", "slab"), scatter_dimension=0, tiled=True),
        lax.psum_scatter(bias_two_grad, ("clip", "slab"), scatter_dimension=0, tiled=True),
        lax.psum_scatter(fc1_grad, ("clip", "slab"), scatter_dimension=0, tiled=True),
        lax.psum_scatter(fc1b_grad, ("clip", "slab"), scatter_dimension=0, tiled=True),
        lax.psum_scatter(fc2_grad, ("clip", "slab"), scatter_dimension=0, tiled=True),
        lax.psum_scatter(fc2b_grad, ("clip", "slab"), scatter_dimension=0, tiled=True),
    )
    table_total = lax.psum(table_grad, ("clip", "slab"))
    output = output.reshape(clip_count, row_count, column_count, feature_width).astype(half_type)
    return (
        output,
        input_grad.astype(half_type),
        shares[0],
        shares[1],
        shares[2],
        shares[3],
        shares[4],
        shares[5],
        shares[6],
        shares[7],
        shares[8],
        shares[9],
        shares[10],
        shares[11],
        shares[12],
        table_total,
    )


def per_device_fast(
    inputs,
    grad_mask,
    cotangent,
    ln1_gain,
    ln1_bias,
    w_qkv,
    q_bias,
    v_bias,
    w_proj,
    proj_bias,
    ln2_gain,
    ln2_bias,
    w_fc1,
    fc1_bias,
    w_fc2,
    fc2_bias,
    pos_table,
):
    bt = (
        jnp.dot(table_onehot(), pos_table, precision=highest)
        .reshape(16, 16, 16)
        .transpose(2, 0, 1)
    )
    smalls = [
        v.reshape(1, 16)
        for v in (ln1_gain, ln1_bias, q_bias, v_bias, proj_bias, ln2_gain, ln2_bias, fc2_bias)
    ]
    ctx, wqb, wpb, w1b, w2b, par, qs, asv, ctxt, normt, nt, rs = k1_call(
        inputs.reshape(8, 256, 512), w_qkv, w_proj, w_fc1, w_fc2, smalls, fc1_bias.reshape(1, 64), bt
    )
    gain_one, bias_one, qbias_full, vbias_full, pbias_full, gain_two, bias_two, fc2b_full = (
        par[i] for i in range(8)
    )
    fc1b_full = par[8:12].reshape(2048)
    qkv_full = (
        wqb.reshape(512, 1664)[:, 128:].reshape(512, 4, 3, 128).transpose(0, 2, 1, 3).reshape(512, 1536)
    )
    proj_full, fc1_full, fc2_full = wpb.reshape(512, 512), w1b.reshape(512, 2048), w2b.reshape(2048, 512)
    clip_count, row_count, column_count, feature_width = inputs.shape
    score_scale = 1.0 / math.sqrt(HEAD_DIM)
    float_type = jnp.float32
    half_type = jnp.bfloat16
    ahead = from_behind(inputs[:, :SHIFT], "slab", -1)
    window_rows = jnp.concatenate([inputs[:, SHIFT:], ahead], axis=1).astype(float_type)
    normed, first_pull = jax.vjp(
        normalize, window_rows, gain_one.astype(float_type), bias_one.astype(float_type)
    )
    windows = to_windows(jnp.roll(normed.astype(half_type), -SHIFT, axis=2))
    window_count = windows.shape[0]
    token_count = window_count * WIN * WIN
    head_shape = (window_count, WIN * WIN, HEADS, HEAD_DIM)
    flat_windows = windows.reshape(token_count, feature_width)
    projected = jnp.dot(flat_windows, qkv_full, preferred_element_type=float_type)
    query_heads = (
        (projected[:, :feature_width] + qbias_full.astype(float_type))
        .astype(half_type)
        .reshape(head_shape)
    )
    key_heads = (
        projected[:, feature_width : 2 * feature_width].astype(half_type).reshape(head_shape)
    )
    value_heads = (
        (projected[:, 2 * feature_width :] + vbias_full.astype(float_type))
        .astype(half_type)
        .reshape(head_shape)
    )
    onehot = table_onehot()
    position_bias = (
        jnp.dot(onehot, pos_table, precision=highest)
        .reshape(WIN * WIN, WIN * WIN, HEADS)
        .transpose(2, 0, 1)
    )
    scores = (
        jnp.einsum("wqhc,wkhc->whqk", query_heads, key_heads, preferred_element_type=float_type)
        * score_scale
        + position_bias[None]
    )
    attention = jax.nn.softmax(scores, axis=-1)
    attention_low = attention.astype(half_type)
    context = jnp.einsum(
        "whqk,wkhc->wqhc", attention_low, value_heads, preferred_element_type=float_type
    )
    context = context.astype(half_type).reshape(window_count, WIN * WIN, feature_width)
    context_grid = jnp.roll(
        from_windows(context, clip_count, row_count, column_count), SHIFT, axis=2
    )
    returned = from_behind(context_grid[:, row_count - SHIFT :], "slab", 1)
    own_flat = jnp.concatenate([returned, context_grid[:, : row_count - SHIFT]], axis=1).reshape(
        -1, feature_width
    )
    own_flat = ctx.reshape(-1, feature_width)
    input_flat = inputs.reshape(-1, feature_width).astype(float_type)
    middle = (
        input_flat
        + jnp.dot(own_flat, proj_full, preferred_element_type=float_type)
        + pbias_full.astype(float_type)
    )
    second, second_pull = jax.vjp(
        normalize, middle, gain_two.astype(float_type), bias_two.astype(float_type)
    )
    second_low = second.astype(half_type)
    pre_act = jnp.dot(second_low, fc1_full, preferred_element_type=float_type) + fc1b_full.astype(
        float_type
    )
    hidden, gelu_pull = jax.vjp(exact_gelu, pre_act)
    hidden_low = hidden.astype(half_type)
    output = (
        middle
        + jnp.dot(hidden_low, fc2_full, preferred_element_type=float_type)
        + fc2b_full.astype(float_type)
    )
    incoming = (cotangent.astype(float_type) * grad_mask.astype(float_type)[..., None]).reshape(
        -1, feature_width
    )
    incoming_low = incoming.astype(half_type)
    fc2_grad = outer_sum(hidden_low, incoming_low)
    fc2b_grad = jnp.sum(incoming, axis=0)
    hidden_grad = times_transposed(incoming_low, fc2_full)
    pre_grad = gelu_pull(hidden_grad)[0].astype(half_type)
    fc1_grad = outer_sum(second_low, pre_grad)
    fc1b_grad = jnp.sum(pre_grad.astype(float_type), axis=0)
    second_grad = times_transposed(pre_grad, fc1_full)
    middle_part, gain_two_grad, bias_two_grad = second_pull(second_grad)
    middle_grad = incoming + middle_part
    branch_low = middle_grad.astype(half_type)
    proj_grad = outer_sum(own_flat, branch_low)
    pbias_grad = jnp.sum(branch_low.astype(float_type), axis=0)
    context_grad = (
        times_transposed(branch_low, proj_full)
        .astype(half_type)
        .reshape(clip_count, row_count, column_count, feature_width)
    )
    sent_back = from_behind(context_grad[:, :SHIFT], "slab", -1)
    window_context_grad = jnp.concatenate([context_grad[:, SHIFT:], sent_back], axis=1)
    context_heads = to_windows(jnp.roll(window_context_grad, -SHIFT, axis=2)).reshape(head_shape)
    value_grad = jnp.einsum(
        "whqk,wqhc->wkhc", attention_low, context_heads, preferred_element_type=float_type
    ).astype(half_type)
    attention_grad = jnp.einsum(
        "wqhc,wkhc->whqk", context_heads, value_heads, preferred_element_type=float_type
    )
    score_grad = (
        attention * (attention_grad - jnp.sum(attention_grad * attention, -1, keepdims=True))
    ).astype(half_type)
    bias_cells = (
        jnp.sum(score_grad.astype(float_type), axis=0)
        .transpose(1, 2, 0)
        .reshape(WIN * WIN * WIN * WIN, HEADS)
    )
    table_grad = lax.dot_general(onehot, bias_cells, (((0,), (0,)), ((), ())), precision=highest)
    query_grad = (
        jnp.einsum("whqk,wkhc->wqhc", score_grad, key_heads, preferred_element_type=float_type)
        * score_scale
    ).astype(half_type)
    key_grad = (
        jnp.einsum("whqk,wqhc->wkhc", score_grad, query_heads, preferred_element_type=float_type)
        * score_scale
    ).astype(half_type)
    query_flat = query_grad.reshape(token_count, feature_width)
    value_flat = value_grad.reshape(token_count, feature_width)
    qkv_grad_low = jnp.concatenate(
        [query_flat, key_grad.reshape(token_count, feature_width), value_flat], axis=1
    )
    qkv_grad = outer_sum(flat_windows, qkv_grad_low)
    qbias_grad = jnp.sum(query_flat.astype(float_type), axis=0)
    vbias_grad = jnp.sum(value_flat.astype(float_type), axis=0)
    normed_grad = times_transposed(qkv_grad_low, qkv_full).reshape(
        window_count, WIN * WIN, feature_width
    )
    normed_grid_grad = jnp.roll(
        from_windows(normed_grad, clip_count, row_count, column_count), SHIFT, axis=2
    )
    rows_part, gain_one_grad, bias_one_grad = first_pull(normed_grid_grad)
    halo_back = from_behind(
        rows_part[:, row_count - SHIFT :].astype(jnp.bfloat16), "slab", 1
    ).astype(jnp.float32)
    input_grad = middle_grad.reshape(
        clip_count, row_count, column_count, feature_width
    ) + jnp.concatenate([halo_back, rows_part[:, : row_count - SHIFT]], axis=1)
    shares = (
        lax.psum_scatter(gain_one_grad, ("clip", "slab"), scatter_dimension=0, tiled=True),
        lax.psum_scatter(bias_one_grad, ("clip", "slab"), scatter_dimension=0, tiled=True),
        lax.psum_scatter(qkv_grad, ("clip", "slab"), scatter_dimension=0, tiled=True),
        lax.psum_scatter(qbias_grad, ("clip", "slab"), scatter_dimension=0, tiled=True),
        lax.psum_scatter(vbias_grad, ("clip", "slab"), scatter_dimension=0, tiled=True),
        lax.psum_scatter(proj_grad, ("clip", "slab"), scatter_dimension=0, tiled=True),
        lax.psum_scatter(pbias_grad, ("clip", "slab"), scatter_dimension=0, tiled=True),
        lax.psum_scatter(gain_two_grad, ("clip", "slab"), scatter_dimension=0, tiled=True),
        lax.psum_scatter(bias_two_grad, ("clip", "slab"), scatter_dimension=0, tiled=True),
        lax.psum_scatter(fc1_grad, ("clip", "slab"), scatter_dimension=0, tiled=True),
        lax.psum_scatter(fc1b_grad, ("clip", "slab"), scatter_dimension=0, tiled=True),
        lax.psum_scatter(fc2_grad, ("clip", "slab"), scatter_dimension=0, tiled=True),
        lax.psum_scatter(fc2b_grad, ("clip", "slab"), scatter_dimension=0, tiled=True),
    )
    table_total = lax.psum(table_grad, ("clip", "slab"))
    output = output.reshape(clip_count, row_count, column_count, feature_width).astype(half_type)
    return (
        output,
        input_grad.astype(half_type),
        shares[0],
        shares[1],
        shares[2],
        shares[3],
        shares[4],
        shares[5],
        shares[6],
        shares[7],
        shares[8],
        shares[9],
        shares[10],
        shares[11],
        shares[12],
        table_total,
    )


def solution(mesh):
    in_specs = (
        P("clip", "slab", None, None),
        P("clip", "slab", None),
        P("clip", "slab", None, None),
        P(("clip", "slab")),
        P(("clip", "slab")),
        P(("clip", "slab"), None),
        P(("clip", "slab")),
        P(("clip", "slab")),
        P(("clip", "slab"), None),
        P(("clip", "slab")),
        P(("clip", "slab")),
        P(("clip", "slab")),
        P(("clip", "slab"), None),
        P(("clip", "slab")),
        P(("clip", "slab"), None),
        P(("clip", "slab")),
        P(),
    )
    out_specs = (
        P("clip", "slab", None, None),
        P("clip", "slab", None, None),
        P(("clip", "slab")),
        P(("clip", "slab")),
        P(("clip", "slab"), None),
        P(("clip", "slab")),
        P(("clip", "slab")),
        P(("clip", "slab"), None),
        P(("clip", "slab")),
        P(("clip", "slab")),
        P(("clip", "slab")),
        P(("clip", "slab"), None),
        P(("clip", "slab")),
        P(("clip", "slab"), None),
        P(("clip", "slab")),
        P(),
    )
    fits = mesh.shape["clip"] == 16 and mesh.shape["slab"] == 2
    return jax.shard_map(
        per_device_fast if fits else per_device, mesh=mesh, in_specs=in_specs, out_specs=out_specs, check_vma=False
    )
```

```python
import functools
import math

import jax
import jax.numpy as jnp
from jax import lax
from jax.experimental import pallas as pl
from jax.experimental.pallas import tpu as pltpu
from jax.sharding import PartitionSpec as P

F32 = jnp.float32
BF = jnp.bfloat16
MESH = pl.DeviceIdType.MESH
SCALE = 1.0 / math.sqrt(32.0)
NT = (((1,), (1,)), ((), ()))
TN = (((0,), (0,)), ((), ()))
VM = pl.BlockSpec(memory_space=pltpu.VMEM)
HB = pl.BlockSpec(memory_space=pl.ANY)
UNROLL = 16


def dot(a, b, dims=(((1,), (0,)), ((), ()))):
    return lax.dot_general(a, b, dims, preferred_element_type=F32)


def tree(xs, op=lambda a, b: a + b):
    xs = list(xs)
    while len(xs) > 1:
        xs = [op(xs[i], xs[i + 1]) if i + 1 < len(xs) else xs[i] for i in range(0, len(xs), 2)]
    return xs[0]


def tile(ref, i):
    return ref[pl.ds(pl.multiple_of(i * 16, 16), 16), :]


def row(ref, i):
    return jnp.broadcast_to(ref[pl.ds(i, 1), :], (16, 128))


def pair_products(a_ref, a0, b_ref, b0):
    def body(d, acc):
        ad = tile(a_ref, a0 + d)
        return tuple(acc[q] + ad * row(b_ref, (b0 + d) * 16 + q) for q in range(16))

    return lax.fori_loop(
        0, 32, body, tuple(jnp.zeros((16, 128), F32) for _ in range(16)), unroll=UNROLL
    )


def weighted(ws, b_ref, b0, o_ref, o0, scale):
    def body(d, carry):
        parts = []
        for k in range(4):
            t = ws[4 * k] * row(b_ref, (b0 + d) * 16 + 4 * k)
            for q in range(4 * k + 1, 4 * k + 4):
                t = t + ws[q] * row(b_ref, (b0 + d) * 16 + q)
            parts.append(t)
        s = (parts[0] + parts[1]) + (parts[2] + parts[3])
        if scale is not None:
            s = s * scale
        o_ref[pl.ds(pl.multiple_of((o0 + d) * 16, 16), 16), :] = s.astype(BF).astype(F32)
        return carry

    lax.fori_loop(0, 32, body, 0, unroll=UNROLL)


class Place:
    def __init__(self):
        self.clip = lax.axis_index("clip")
        self.y = lax.axis_index("slab")
        self.c = self.clip % 2
        self.x = (self.clip // 2) % 2
        self.z = self.clip // 4
        self.rank8 = self.x * 4 + self.c * 2 + self.y
        base = self.x * 2 + self.c
        self.along_z = [(((self.z + d) % 4) * 4 + base, self.y) for d in (1, 2, 3)]
        self.over_x = (self.clip + 2 - 4 * self.x, self.y)
        self.over_y = (self.clip, 1 - self.y)
        self.over_core = (self.clip + 1 - 2 * self.c, self.y)

    def greet(self):
        barrier = pltpu.get_barrier_semaphore()
        others = self.along_z + [self.over_x, self.over_y, self.over_core]
        for other in others:
            pl.semaphore_signal(barrier, inc=1, device_id=other, device_id_type=MESH)
        pl.semaphore_wait(barrier, len(others))


def remote(src, dst, ssem, rsem, to):
    return pltpu.make_async_remote_copy(
        src_ref=src, dst_ref=dst, send_sem=ssem, recv_sem=rsem, device_id=to, device_id_type=MESH
    )


class Gather:
    def __init__(self, place, pieces, ssem, rsem):
        self.copies = []
        z, x, c, y = place.z, place.x, place.c, place.y
        for k, (buf, c0, n, first_x) in enumerate(pieces):
            cols = pl.ds(c0, n)

            def cp(ix, s, to, k=k, buf=buf, cols=cols):
                ref = buf.at[ix + (slice(None), cols)]
                return remote(ref, ref, ssem.at[k, s], rsem.at[k, s], to)

            al = slice(None)
            steps = [[cp((z, x, c, y), d, place.along_z[d]) for d in range(3)]]
            if first_x:
                steps.append([cp((al, x, c, y), 3, place.over_x)])
                steps.append([cp((al, al, c, y), 4, place.over_y)])
            else:
                steps.append([cp((al, x, c, y), 3, place.over_y)])
                steps.append([cp((al, x, c, al), 4, place.over_x)])
            steps.append([cp((al, al, c, al), 5, place.over_core)])
            self.copies.append(steps)

    def start(self, k, s):
        for copy in self.copies[k][s]:
            copy.start()

    def advance(self, k, s):
        for copy in self.copies[k][s]:
            copy.wait_recv()
        if s < 3:
            self.start(k, s + 1)

    def close(self):
        for steps in self.copies:
            for step in steps:
                for copy in step:
                    copy.wait_send()


def spots(p):
    i, j = p // 4, p % 4
    return (i * 8 + (j + 2) % 8, i * 8 + (j + 6) % 8)


def gathered(ref, lo, hi):
    return jnp.concatenate([ref[pl.ds(lo, 64, stride=32), :], ref[pl.ds(hi, 64, stride=32), :]], axis=0)


def small_block(place, small_refs, fc1b_ref, scr):
    scr[...] = jnp.zeros_like(scr)
    for k, ref in enumerate(small_refs):
        scr[k : k + 1, 0:16] = ref[...].astype(F32)
    lane = lax.broadcasted_iota(jnp.int32, (128, 128), 1)
    src = lax.broadcasted_iota(jnp.int32, (128, 128), 0)
    sel = ((lane == place.rank8 * 16 + src) & (src < 16)).astype(F32).astype(BF)
    vectors = dot(scr[...].astype(BF), sel)
    scr[0:1, 0:64] = fc1b_ref[...].astype(F32)
    half = ((lane == place.y * 64 + src) & (src < 64)).astype(F32).astype(BF)
    wide = dot(scr[0:1, :].astype(BF), half)
    r = lax.broadcasted_iota(jnp.int32, (16, 128), 0)
    return jnp.where(
        r < 8,
        vectors,
        jnp.where(r == 8 + place.x * 2 + place.c, jnp.broadcast_to(wide, (16, 128)), 0.0),
    ).astype(BF)


def k1_body(
    x_ref, wq_ref, wp_ref, w1_ref, w2_ref, s0, s1, s2, s3, s4, s5, s6, s7, fb_ref, bt_ref,
    ctx_ref, wqb, wpb, w1b, w2b, par_ref, qkv_save, att_save, ctxt_ref, normt_ref, nt_ref, rs_ref,
    xs, ntf, g_ref, ct_ref, cs_ref, a_ref, qb, halo, chalo, gains, scr,
    ssem, rsem, hss, hrs, lsem, osem,
):
    me = Place()
    z, x, c, y = me.z, me.x, me.c, me.y
    own = [
        pltpu.make_async_copy(src, buf.at[z, x, c, y], osem.at[i])
        for i, (src, buf) in enumerate(((wp_ref, wpb), (w1_ref, w1b), (w2_ref, w2b)))
    ]
    for cp in own:
        cp.start()
    wqb[z, x, c, y, :, 0:128] = small_block(me, (s0, s1, s2, s3, s4, s5, s6, s7), fb_ref, scr)
    for g in range(4):
        for k in range(3):
            wqb[z, x, c, y, :, 128 + g * 384 + k * 128 : 256 + g * 384 + k * 128] = wq_ref[
                :, k * 512 + g * 128 : k * 512 + g * 128 + 128
            ]
    pieces = [(wqb, 0, 512, True)] + [(wqb, 128 + g * 384, 384, g % 2 == 0) for g in (1, 2, 3)]
    pieces += [(wpb, 0, 256, True), (wpb, 256, 256, False)]
    pieces += [(w1b, 0, 1024, True), (w1b, 1024, 1024, False)]
    pieces += [(w2b, 0, 256, True), (w2b, 256, 256, False)]
    gat = Gather(me, pieces, ssem, rsem)
    me.greet()
    for k in range(4):
        gat.start(k, 0)
    xhalo = remote(x_ref.at[:, 0:16, :], halo, hss.at[4], hrs.at[4], me.over_y)
    xhalo.start()
    for b in range(8):
        for k in range(4):
            xs[k, b * 256 : b * 256 + 240, :] = x_ref[b, 16:256, k * 128 : k * 128 + 128].astype(F32)
    gat.advance(0, 0)
    gat.advance(1, 0)
    xhalo.wait_recv()
    for b in range(8):
        for k in range(4):
            xs[k, b * 256 + 240 : b * 256 + 256, :] = halo[b, :, k * 128 : k * 128 + 128].astype(F32)

    def norm_block(p):
        lo, hi = spots(p)
        turned = jnp.concatenate([gathered(xs.at[k], lo, hi).T for k in range(4)], axis=0)
        mean = jnp.mean(turned, 0, keepdims=True)
        cen = turned - mean
        rs = lax.rsqrt(jnp.mean(cen * cen, 0, keepdims=True) + 1e-6)
        ntf[:, p * 128 : (p + 1) * 128] = cen * rs
        rs_ref[p : p + 1, :] = rs

    todo = [(2, 0), (0, 1), (1, 1), (3, 0), (0, 2), (2, 1), (1, 2)]
    for p in range(16):
        norm_block(p)
        if p % 2 == 1 and todo:
            gat.advance(*todo.pop(0))
    for step in todo:
        gat.advance(*step)
    for cp in own:
        cp.wait()
    for k in (4, 5, 6):
        gat.start(k, 0)
    gat.advance(0, 3)
    for zz in range(4):
        total = jnp.sum(wqb[zz, :, :, :, :, 0:128].astype(F32).reshape(8, 16, 128), axis=0)
        par_ref[0:8, zz * 128 : (zz + 1) * 128] = total[0:8]
        for k in range(4):
            par_ref[8 + zz : 9 + zz, k * 128 : (k + 1) * 128] = total[8 + k : 9 + k]
    par_ref[12:16, :] = jnp.zeros((4, 512), F32)
    scr2 = par_ref[...].T
    gains[0] = jnp.broadcast_to(scr2[:, 0:1], (512, 128))
    gains[1] = jnp.broadcast_to(scr2[:, 1:2], (512, 128))
    gains[2] = jnp.broadcast_to(scr2[:, 2:3], (512, 128))
    gains[3] = jnp.broadcast_to(scr2[:, 3:4], (512, 128))

    def finish_norm(p, carry):
        cols = pl.ds(pl.multiple_of(p * 128, 128), 128)
        n = ntf[:, cols]
        normt_ref[:, cols] = (n * gains[0] + gains[1]).astype(BF)
        nt_ref[:, cols] = n.astype(BF)
        return carry

    lax.fori_loop(0, 16, finish_norm, 0)

    plan = [
        [(2, 2), (3, 1), (1, 3)],
        [(3, 2), (4, 0), (5, 0), ("s", 7)],
        [(2, 3), (4, 1), (6, 0), ("s", 8)],
        [(3, 3), (5, 1), (4, 2), (7, 0), ("s", 9)],
        [(6, 1), (5, 2)],
        [(7, 1), (8, 0), (4, 3)],
        [(6, 2), (5, 3)],
        [(8, 1), (9, 0)],
        [(7, 2)],
        [(9, 1), (6, 3)],
        [(8, 2)],
        [(7, 3)],
    ]

    def progress():
        if plan:
            for k, s in plan.pop(0):
                if k == "s":
                    gat.start(s, 0)
                else:
                    gat.advance(k, s)

    saves = []
    chs = []
    for g in range(4):
        w = wqb[:, :, :, :, :, 128 + g * 384 : 512 + g * 384].reshape(512, 384)
        wt = w.astype(F32).T.astype(BF)
        fs = slice(g * 128, (g + 1) * 128)
        if g > 0:
            saves[-1].wait()

        def project(t, carry):
            out = dot(wt, normt_ref[:, pl.ds(pl.multiple_of(t * 512, 512), 512)])
            for k in range(4):
                block = out[:, k * 128 : (k + 1) * 128]
                block = jnp.concatenate(
                    [block[0:128] + gains[2, fs, :], block[128:256], block[256:384] + gains[3, fs, :]],
                    axis=0,
                )
                g_ref[pl.ds(t * 4 + k, 384, stride=16), :] = block.astype(BF).astype(F32)
            return carry

        lax.fori_loop(0, 4, project, 0)

        def keep(i, carry):
            rows = pl.ds(pl.multiple_of(i * 512, 512), 512)
            qb[rows, :] = g_ref[rows, :].astype(BF)
            return carry

        lax.fori_loop(0, 12, keep, 0)
        save = pltpu.make_async_copy(qb, qkv_save.at[g], lsem.at[g])
        save.start()
        saves.append(save)
        progress()

        def head(h, carry, g=g):
            acc = pair_products(g_ref, h * 32, g_ref, 128 + h * 32)
            bt = bt_ref[g * 4 + h]
            s = [
                acc[q] * SCALE + jnp.broadcast_to(bt[:, q : q + 1], (16, 128)) for q in range(16)
            ]
            m = tree(s, jnp.maximum)
            e = [jnp.exp(v - m) for v in s]
            inv = 1.0 / tree(e)
            low = []
            for q in range(16):
                a = e[q] * inv
                a_ref[pl.ds(pl.multiple_of((g * 4 + h) * 256 + q * 16, 16), 16), :] = a
                low.append(a.astype(BF).astype(F32))
            weighted(low, g_ref, 256 + h * 32, ct_ref, h * 32, None)
            return carry

        lax.fori_loop(0, 2, head, 0)
        progress()
        lax.fori_loop(2, 4, head, 0)
        asave = pltpu.make_async_copy(
            a_ref.at[pl.ds(g * 1024, 1024), :], att_save.at[pl.ds(g * 1024, 1024), :], lsem.at[4 + g]
        )
        asave.start()
        chs.append(asave)
        for p in range(16):
            block = ct_ref[pl.ds(p, 128, stride=16), :]
            ctxt_ref[fs, p * 128 : (p + 1) * 128] = block.astype(BF)
            turned = block.T
            lo, hi = spots(p)
            cs_ref[pl.ds(lo, 64, stride=32), :] = turned[0:64]
            cs_ref[pl.ds(hi, 64, stride=32), :] = turned[64:128]
        for b in range(8):
            ctx_ref[b, 16:256, fs] = cs_ref[b * 256 : b * 256 + 240, :].astype(BF)
            chalo[g, b] = cs_ref[b * 256 + 240 : b * 256 + 256, :].astype(BF)
        send = remote(chalo.at[g], ctx_ref.at[:, 0:16, pl.ds(g * 128, 128)], hss.at[g], hrs.at[g], me.over_y)
        send.start()
        chs.append(send)
        progress()
    while plan:
        progress()
    gat.advance(8, 3)
    gat.advance(9, 2)
    gat.advance(9, 3)
    saves[-1].wait()
    for cp in chs:
        cp.wait()
    xhalo.wait_send()
    gat.close()


def k1_call(x, wq, wp, w1, w2, smalls, fb, bt):
    S = jax.ShapeDtypeStruct
    lead = (4, 2, 2, 2)
    outs = [
        (S((8, 256, 512), BF), VM),
        (S(lead + (16, 1664), BF), VM),
        (S(lead + (16, 512), BF), HB),
        (S(lead + (16, 2048), BF), HB),
        (S(lead + (64, 512), BF), HB),
        (S((16, 512), F32), VM),
        (S((4, 6144, 128), BF), HB),
        (S((4096, 128), F32), HB),
        (S((512, 2048), BF), VM),
        (S((512, 2048), BF), VM),
        (S((512, 2048), BF), VM),
        (S((16, 128), F32), VM),
    ]
    V = pltpu.VMEM
    return pl.pallas_call(
        k1_body,
        out_shape=[o[0] for o in outs],
        in_specs=[VM, VM, HB, HB, HB] + [VM] * 10,
        out_specs=[o[1] for o in outs],
        scratch_shapes=[
            V((4, 2048, 128), F32), V((512, 2048), F32), V((6144, 128), F32), V((2048, 128), F32),
            V((2048, 128), F32), V((4096, 128), F32), V((6144, 128), BF), V((8, 16, 512), BF),
            V((4, 8, 16, 128), BF), V((4, 512, 128), F32), V((16, 128), F32),
            pltpu.SemaphoreType.DMA((10, 6)), pltpu.SemaphoreType.DMA((10, 6)),
            pltpu.SemaphoreType.DMA((5,)), pltpu.SemaphoreType.DMA((5,)),
            pltpu.SemaphoreType.DMA((8,)), pltpu.SemaphoreType.DMA((3,)),
        ],
        compiler_params=pltpu.CompilerParams(
            collective_id=1, has_side_effects=True, vmem_limit_bytes=60 << 20
        ),
        name="gather_attend",
    )(x, wq, wp, w1, w2, *smalls, fb, bt)


def gelu_parts(a):
    z = jnp.abs(a) * 0.7071067811865476
    t = 1.0 / (1.0 + 0.3275911 * z)
    e = jnp.exp(a * a * -0.5)
    p = 0.5307027145 * t - 0.7265760135
    p = p * t + 0.7107068705
    p = p * t - 0.142248368
    p = p * t + 0.127414796
    tail = p * t * e
    return jnp.where(a >= 0, 1.0 - tail, tail), e * 0.3989422804014327


CH = 512
FJ = 512


def k2_body(
    x_ref, ctx_ref, cot_ref, mask_ref, par_ref, wp_ref, w1_ref, w2_ref,
    out_ref, mg_ref, br_ref, g1_ref, g2_ref, small_ref, hid_ref, pg_ref, sec_ref, inc_ref,
):
    pb, g2, b2, fb2 = (par_ref[k : k + 1, :] for k in (4, 5, 6, 7))
    small_ref[...] = jnp.zeros_like(small_ref)
    rsel = (
        lax.broadcasted_iota(jnp.int32, (256, 32), 0) // 8
        == lax.broadcasted_iota(jnp.int32, (256, 32), 1)
    ).astype(F32).astype(BF)
    csel = lax.broadcasted_iota(jnp.int32, (256, 8), 0) % 8 == lax.broadcasted_iota(
        jnp.int32, (256, 8), 1
    )

    def chunk(i, carry):
        rows = pl.ds(pl.multiple_of(i * CH, CH), CH)
        mid = x_ref[rows, :].astype(F32) + dot(ctx_ref[rows, :], wp_ref[...]) + pb
        cen = mid - jnp.mean(mid, 1, keepdims=True)
        rs = lax.rsqrt(jnp.mean(cen * cen, 1, keepdims=True) + 1e-6)
        n2 = cen * rs
        sec = (n2 * g2 + b2).astype(BF)
        sec_ref[rows, :] = sec
        marks = []
        for k in range(CH // 256):
            spread = dot(rsel, mask_ref[i * (CH // 256) + k].astype(F32).astype(BF))
            marks.append(jnp.sum(jnp.where(csel, spread, 0.0), 1, keepdims=True))
        inc = cot_ref[rows, :].astype(F32) * jnp.concatenate(marks, 0)
        low = inc.astype(BF)
        inc_ref[rows, :] = low
        small_ref[7:8, :] += jnp.sum(inc, 0, keepdims=True)
        total = back = None
        for j in range(2048 // FJ):
            cols = slice(j * FJ, (j + 1) * FJ)
            pre = dot(sec, w1_ref[:, cols]) + par_ref[8 + j : 9 + j, :]
            hg = dot(low, w2_ref[cols, :], NT)
            cdf, pdf = gelu_parts(pre)
            hid = (pre * cdf).astype(BF)
            hid_ref[rows, cols] = hid
            pg = (hg * (cdf + pre * pdf)).astype(BF)
            pg_ref[rows, cols] = pg
            small_ref[8 + j : 9 + j, :] += jnp.sum(pg.astype(F32), 0, keepdims=True)
            o = dot(hid, w2_ref[cols, :])
            s = dot(pg, w1_ref[:, cols], NT)
            total = o if total is None else total + o
            back = s if back is None else back + s
        out_ref[rows, :] = (mid + total + fb2).astype(BF)
        small_ref[5:6, :] += jnp.sum(back * n2, 0, keepdims=True)
        small_ref[6:7, :] += jnp.sum(back, 0, keepdims=True)
        eg = back * g2
        r = (eg - jnp.mean(eg, 1, keepdims=True) - n2 * jnp.mean(eg * n2, 1, keepdims=True)) * rs
        mg = inc + r
        mg_ref[rows, :] = mg
        br = mg.astype(BF)
        br_ref[rows, :] = br
        small_ref[4:5, :] += jnp.sum(br.astype(F32), 0, keepdims=True)
        return carry

    lax.fori_loop(0, 2048 // CH, chunk, 0)

    def grads_one(j, carry):
        cols = pl.ds(pl.multiple_of(j * 256, 256), 256)
        g1_ref[:, cols] = dot(sec_ref[...], pg_ref[:, cols], TN).astype(BF)
        return carry

    lax.fori_loop(0, 8, grads_one, 0)

    def grads_two(j, carry):
        cols = pl.ds(pl.multiple_of(j * 256, 256), 256)
        g2_ref[cols, :] = dot(hid_ref[:, cols], inc_ref[...], TN).astype(BF)
        return carry

    lax.fori_loop(0, 8, grads_two, 0)


def k2_call(x, ctx, cot, mask, par, wp, w1, w2):
    S = jax.ShapeDtypeStruct
    V = pltpu.VMEM
    return pl.pallas_call(
        k2_body,
        out_shape=[
            S((2048, 512), BF), S((2048, 512), F32), S((2048, 512), BF),
            S((512, 2048), BF), S((2048, 512), BF), S((16, 512), F32),
        ],
        in_specs=[VM] * 8,
        out_specs=[VM] * 6,
        scratch_shapes=[V((2048, 2048), BF)] * 2 + [V((2048, 512), BF)] * 2,
        compiler_params=pltpu.CompilerParams(vmem_limit_bytes=60 << 20),
        name="feed_forward",
    )(x, ctx, cot, mask, par, wp, w1, w2)


class Scatter:
    def __init__(self, place, pieces, ssem, rsem):
        self.me = place
        self.pieces = pieces
        self.steps = []
        z, x, c, y = place.z, place.x, place.c, place.y
        al = slice(None)
        for k, (src, c0, n, first_y, own, s, r1, r2, r3, r4, done) in enumerate(pieces):
            cols = pl.ds(c0, n)

            def cp(a, b, i, to, k=k):
                return remote(a, b, ssem.at[k, i], rsem.at[k, i], to)

            steps = [[cp(src.at[:, :, 1 - c, :, :, cols], r1, 0, place.over_core)]]
            if first_y:
                steps.append([cp(s.at[:, :, 1 - y], r2, 1, place.over_y)])
                steps.append([cp(s.at[:, 1 - x, y], r3, 2, place.over_x)])
            else:
                steps.append([cp(s.at[:, 1 - x], r2, 1, place.over_x)])
                steps.append([cp(s.at[:, x, 1 - y], r3, 2, place.over_y)])
            steps.append(
                [
                    cp(s.at[(z + 1 + d) % 4, x, y], r4.at[d], 3 + d, place.along_z[d])
                    for d in range(3)
                ]
            )
            self.steps.append(steps)

    def start(self, k, i):
        for copy in self.steps[k][i]:
            copy.start()

    def advance(self, k, i):
        me = self.me
        z, x, c, y = me.z, me.x, me.c, me.y
        src, c0, n, first_y, own, s, r1, r2, r3, r4, done = self.pieces[k]
        cols = pl.ds(c0, n)
        for copy in self.steps[k][i]:
            copy.wait_recv()
        if i == 0:
            if own is not None:
                own.wait()

            def add(zz, carry):
                held = s[zz] if own is not None else src[zz, :, c, :, :, cols]
                s[zz] = (held.astype(F32) + r1[zz].astype(F32)).astype(BF)
                return carry

            lax.fori_loop(0, 4, add, 0)
        elif i == 1 and first_y:
            s[:, :, y] = (s[:, :, y].astype(F32) + r2[...].astype(F32)).astype(BF)
        elif i == 1:
            s[:, x] = (s[:, x].astype(F32) + r2[...].astype(F32)).astype(BF)
        elif i == 2:
            s[:, x, y] = (s[:, x, y].astype(F32) + r3[...].astype(F32)).astype(BF)
        else:
            done(tree([s[z, x, y].astype(F32)] + [r4[d].astype(F32) for d in range(3)]))
        if i < 3:
            self.start(k, i + 1)

    def close(self):
        for steps in self.steps:
            for step in steps:
                for copy in step:
                    copy.wait_send()


def k3_body(
    br_ref, mg_h, g1_ref, g2_ref, small_ref, wqb_h, wp_h, qkv_save, att_save, ctxt_h, normt_h, nt_h, rs_ref,
    ig_ref, gq_ref, gp_ref, gf1_ref, gf2_ref, v0, v1, v2, v3, v4, v5, v6, v7, fb_ref, tab_ref,
    bs, bp, mg, wq, wp, qb, g_ref, dg, dc, a_ref, dqt, ctxt, normt, nt, ds_ref, low_ref,
    gacc, pgrad, qgrad, bhalo, rhalo, rout, cells, ar, arr, arz,
    s4, r14, r24, r34, r44, sp, r1p, r2p, r3p, r4p, sq, r1q, r2q, r3q, r4q,
    ssem, rsem, hss, hrs, lsem, asems, aremr,
):
    me = Place()
    z, x, c, y = me.z, me.x, me.c, me.y
    me.greet()

    def local(src, dst, i):
        cp = pltpu.make_async_copy(src, dst, lsem.at[i])
        cp.start()
        return cp

    pieces = []
    owns = []
    for k, (src, rows, n) in enumerate(((g2_ref, 64, 256), (g1_ref, 16, 1024))):
        for half in range(2):
            j = k * 2 + half
            own = local(
                src.at[:, :, c, :, :, pl.ds(half * n, n)], s4[j], 10 + j
            )
            out = gf2_ref if k == 0 else gf1_ref

            def done(v, out=out, c0=half * n, n=n):
                out[:, c0 : c0 + n] = v

            pieces.append((src, half * n, n, half == 0, own, s4[j], r14[j], r24[j], r34[j], r44[j], done))
    for half in range(2):

        def done(v, c0=half * 256):
            gp_ref[:, c0 : c0 + 256] = v

        pieces.append(
            (pgrad, half * 256, 256, half == 0, None, sp.at[half], r1p.at[half], r2p.at[half], r3p.at[half], r4p.at[half], done)
        )
    for g in range(4):

        def done(v, g=g):
            for k in range(3):
                gq_ref[:, k * 512 + g * 128 : k * 512 + g * 128 + 128] = v[:, k * 128 : k * 128 + 128]

        pieces.append(
            (qgrad.at[g], 0, 384, g % 2 == 0, None, sq.at[g], r1q.at[g], r2q.at[g], r3q.at[g], r4q.at[g], done)
        )
    sca = Scatter(me, pieces, ssem, rsem)
    bh = remote(br_ref.at[:, 0:16, :], bhalo, hss.at[0], hrs.at[0], me.over_y)
    bh.start()
    for k in range(4):
        sca.start(k, 0)
    load_c = local(ctxt_h, ctxt, 0)
    load_p = local(wp_h, wp, 1)
    load_q = local(qkv_save.at[0], qb, 2)
    load_a = local(att_save, a_ref, 3)
    load_n = local(normt_h, normt, 4)
    load_t = local(nt_h, nt, 5)
    load_w = local(wqb_h, wq, 6)
    load_m = local(mg_h, mg, 7)
    for b in range(8):
        for k in range(4):
            bs[k, b * 256 : b * 256 + 240, :] = br_ref[b, 16:256, k * 128 : k * 128 + 128].astype(F32)
    bh.wait_recv()
    for b in range(8):
        for k in range(4):
            bs[k, b * 256 + 240 : b * 256 + 256, :] = bhalo[b, :, k * 128 : k * 128 + 128].astype(F32)
    for p in range(16):
        lo, hi = spots(p)
        for k in range(4):
            bp[p * 128 : p * 128 + 128, k * 128 : k * 128 + 128] = gathered(bs.at[k], lo, hi).astype(BF)
    sca.advance(0, 0)
    sca.advance(1, 0)
    load_c.wait()
    pgrad[...] = dot(ctxt[...], bp[...]).astype(BF).reshape(4, 2, 2, 2, 16, 512)
    sca.start(4, 0)
    sca.start(5, 0)
    load_p.wait()
    load_a.wait()
    cells[...] = jnp.zeros_like(cells)
    plan = [
        [(2, 0), (3, 0)],
        [(0, 1), (1, 1)],
        [(4, 0), (5, 0)],
        [(2, 1), (3, 1)],
        [(0, 2), (1, 2)],
        [(6, 0), (4, 1), (5, 1)],
        [(2, 2), (3, 2)],
        [(0, 3), (1, 3)],
        [(6, 1), (7, 0), (4, 2), (5, 2)],
        [(6, 2), (7, 1)],
        [(2, 3), (3, 3), (4, 3), (5, 3)],
        [(6, 3), (7, 2), (8, 0)],
        [(8, 1), (7, 3)],
        [(9, 0)],
        [(8, 2), (9, 1)],
        [(8, 3), (9, 2)],
        [(9, 3)],
    ]

    def progress():
        if plan:
            for k, s in plan.pop(0):
                sca.advance(k, s)

    lanes = lax.broadcasted_iota(jnp.int32, (16, 128), 1)
    for g in range(4):
        fs = slice(g * 128, (g + 1) * 128)

        def context_grad(t, carry, fs=fs):
            out = dot(wp[fs, :], bp[pl.ds(pl.multiple_of(t * 512, 512), 512), :], NT)
            for k in range(4):
                dc[pl.ds(t * 4 + k, 128, stride=16), :] = (
                    out[:, k * 128 : (k + 1) * 128].astype(BF).astype(F32)
                )
            return carry

        lax.fori_loop(0, 4, context_grad, 0)
        load_q.wait()

        def widen(i, carry):
            rows = pl.ds(pl.multiple_of(i * 512, 512), 512)
            g_ref[rows, :] = qb[rows, :].astype(F32)
            return carry

        lax.fori_loop(0, 12, widen, 0)
        if g < 3:
            load_q = local(qkv_save.at[g + 1], qb, 2)
        progress()

        def head(h, carry, g=g):
            da = pair_products(dc, h * 32, g_ref, 256 + h * 32)
            a0 = (g * 4 + h) * 16
            at = [tile(a_ref, a0 + q) for q in range(16)]
            tot = tree([da[q] * at[q] for q in range(16)])
            ds = []
            mine = lanes == g * 4 + h
            for q in range(16):
                low_ref[q * 16 : q * 16 + 16, :] = at[q].astype(BF).astype(F32)
                d = (at[q] * (da[q] - tot)).astype(BF).astype(F32)
                ds_ref[q * 16 : q * 16 + 16, :] = d
                ds.append(d)
                cell = jnp.sum(d, axis=1, keepdims=True)
                cells[q * 16 : q * 16 + 16, :] += jnp.where(mine, cell, 0.0)
            weighted(ds, g_ref, 128 + h * 32, dg, h * 32, SCALE)
            turned = [ds_ref[pl.ds(p, 16, stride=16), :] for p in range(16)]
            weighted(turned, g_ref, h * 32, dg, 128 + h * 32, SCALE)
            turned = [low_ref[pl.ds(p, 16, stride=16), :] for p in range(16)]
            weighted(turned, dc, h * 32, dg, 256 + h * 32, None)
            return carry

        lax.fori_loop(0, 2, head, 0)
        progress()
        lax.fori_loop(2, 4, head, 0)
        sums = jnp.zeros((384, 128), F32)
        for p in range(16):
            v = dg[pl.ds(p, 384, stride=16), :]
            sums = sums + v
            dqt[g * 384 : (g + 1) * 384, p * 128 : (p + 1) * 128] = v.astype(BF)
        ar[g, 2:3, :] = jnp.sum(sums[0:128].T, 0, keepdims=True)
        ar[g, 3:4, :] = jnp.sum(sums[256:384].T, 0, keepdims=True)
        if g == 0:
            load_n.wait()
        for k in range(3):
            rows = slice(g * 384 + k * 128, g * 384 + k * 128 + 128)
            qgrad[g, :, :, :, :, :, k * 128 : k * 128 + 128] = (
                dot(normt[...], dqt[rows, :], NT).astype(BF).reshape(4, 2, 2, 2, 16, 128)
            )
        sca.start(6 + g, 0)
        progress()
    load_w.wait()
    load_t.wait()
    wall = wq[:, :, :, :, :, 128:1664].reshape(512, 1536)
    gain = jnp.broadcast_to(wq_gain(wq), (512, 128))
    gacc[...] = jnp.zeros_like(gacc)

    def norm_back(t, carry):
        e4 = dot(wall, dqt[:, pl.ds(pl.multiple_of(t * 512, 512), 512)])
        for k in range(4):
            p = t * 4 + k
            e = e4[:, k * 128 : (k + 1) * 128]
            n = nt[:, pl.ds(pl.multiple_of(p * 128, 128), 128)].astype(F32)
            gacc[0] += e * n
            gacc[1] += e
            eg = e * gain
            m2 = jnp.mean(eg * n, 0, keepdims=True)
            r = (eg - jnp.mean(eg, 0, keepdims=True) - n * m2) * rs_ref[pl.ds(p, 1), :]
            lo = t * 8 + (k + 2) % 8
            hi = t * 8 + (k + 6) % 8
            for q in range(4):
                turned = r[q * 128 : q * 128 + 128].T
                bs[q, pl.ds(lo, 64, stride=32), :] = turned[0:64]
                bs[q, pl.ds(hi, 64, stride=32), :] = turned[64:128]
        return carry

    for t in range(4):
        lax.fori_loop(t, t + 1, norm_back, 0)
        progress()
    for b in range(8):
        for k in range(4):
            rout[b, :, k * 128 : k * 128 + 128] = bs[k, b * 256 + 240 : b * 256 + 256, :].astype(BF)
    rh = remote(rout, rhalo, hss.at[1], hrs.at[1], me.over_y)
    rh.start()
    for zz in range(4):
        ls = slice(zz * 128, zz * 128 + 128)
        for k in range(2):
            ar[zz, k : k + 1, :] = jnp.sum(gacc[k, ls, :].T, 0, keepdims=True)
        ar[zz, 4:8, :] = small_ref[4:8, ls]
        for k in range(4):
            ar[zz, 8 + k : 9 + k, :] = small_ref[8 + zz : 9 + zz, k * 128 : k * 128 + 128]
        ar[zz, 12:16, :] = jnp.zeros((4, 128), F32)
    pair = lax.broadcasted_iota(jnp.int32, (64, 256), 1)
    entry = lax.broadcasted_iota(jnp.int32, (64, 256), 0)
    qi, pi = pair // 16, pair % 16
    index = (pi // 4 - qi // 4 + 3) * 7 + pi % 4 - qi % 4 + 3
    table = lax.dot_general(
        (index == entry).astype(F32), cells[...], (((1,), (0,)), ((), ())),
        precision=lax.Precision.HIGHEST, preferred_element_type=F32,
    )
    packed = table[0:8]
    for k in range(1, 8):
        packed = packed + pltpu.roll(table[8 * k : 8 * k + 8], 16 * k, 1)
    ar[4, 0:8, :] = packed
    ar[4, 8:16, :] = jnp.zeros((8, 128), F32)
    progress()
    small = [
        remote(ar, arr.at[0], asems.at[0], aremr.at[0], me.over_core),
        remote(ar, arr.at[1], asems.at[1], aremr.at[1], me.over_x),
        remote(ar, arr.at[2], asems.at[2], aremr.at[2], me.over_y),
    ]
    small[0].start()
    load_m.wait()

    def finish(half):
        for b in range(half * 4, half * 4 + 4):
            for k in range(4):
                ls = slice(k * 128, k * 128 + 128)
                ig_ref[b, 16:256, ls] = (mg[b, 16:256, ls] + bs[k, b * 256 : b * 256 + 240, :]).astype(BF)

    finish(0)
    small[0].wait()
    ar[...] = ar[...] + arr[0]
    small[1].start()
    progress()
    finish(1)
    small[1].wait()
    ar[...] = ar[...] + arr[1]
    small[2].start()
    progress()
    rh.wait()
    for b in range(8):
        ig_ref[b, 0:16, :] = (mg[b, 0:16, :] + rhalo[b].astype(F32)).astype(BF)
    small[2].wait()
    ar[...] = ar[...] + arr[2]
    last = []
    for d in range(3):
        to = (z + 1 + d) % 4
        last.append(remote(ar.at[to], arz.at[z, 0], asems.at[3 + d], aremr.at[3 + d], me.along_z[d]))
        last.append(remote(ar.at[4], arz.at[z, 1], asems.at[6 + d], aremr.at[6 + d], me.along_z[d]))
    for cp in last:
        cp.start()
    arz[z, 0] = ar[z]
    arz[z, 1] = ar[4]
    while plan:
        progress()
    for cp in last:
        cp.wait()
    total = (arz[0] + arz[1]) + (arz[2] + arz[3])
    tab_ref[...] = total[1, 0:8]
    ar[0] = total[0]
    mine = pltpu.roll(total[0], (8 - me.rank8) * 16 % 128, 1)
    for k, ref in enumerate((v0, v1, v2, v3, v4, v5, v6, v7)):
        ref[...] = mine[k : k + 1, 0:16]
    fb = ar[0, pl.ds(8 + x * 2 + c, 1), :]
    fb_ref[...] = jnp.where(y == 0, fb[:, 0:64], fb[:, 64:128])
    bh.wait_send()
    sca.close()


def wq_gain(wq):
    parts = []
    for zz in range(4):
        total = jnp.sum(wq[zz, :, :, :, :, 0:128].astype(F32).reshape(8, 16, 128), axis=0)
        parts.append(total.T[:, 0:1])
    return jnp.concatenate(parts, 0)


def k3_call(br, mg, g1, g2, small, wqb, wp, qs, asv, ctxt, normt, nt, rs):
    S = jax.ShapeDtypeStruct
    V = pltpu.VMEM
    lead = (4, 2, 2, 2)
    half = (4, 2, 2)
    outs = [S((8, 256, 512), BF), S((16, 1536), F32), S((16, 512), F32), S((16, 2048), F32), S((64, 512), F32)]
    outs += [S((1, 16), F32)] * 8 + [S((1, 64), F32), S((8, 128), F32)]

    def four(shape):
        return [V(shape + (64, 256), BF)] * 2 + [V(shape + (16, 1024), BF)] * 2

    fours = [four(half), four(half), four((4, 2)), four((4,)), four((3,))]
    rest = []
    for count, n in ((2, 256), (4, 384)):
        for shape in (half, half, (4, 2), (4,), (3,)):
            rest.append(V((count,) + shape + (16, n), BF))
    scratch = [
        V((4, 2048, 128), F32), V((2048, 512), BF), V((8, 256, 512), F32), V(lead + (16, 1664), BF),
        V((512, 512), BF), V((6144, 128), BF), V((6144, 128), F32), V((6144, 128), F32),
        V((2048, 128), F32), V((4096, 128), F32), V((1536, 2048), BF), V((512, 2048), BF),
        V((512, 2048), BF), V((512, 2048), BF), V((256, 128), F32), V((256, 128), F32),
        V((2, 512, 128), F32), V(lead + (16, 512), BF), V((4,) + lead + (16, 384), BF),
        V((8, 16, 512), BF), V((8, 16, 512), BF), V((8, 16, 512), BF), V((256, 128), F32),
        V((5, 16, 128), F32), V((3, 5, 16, 128), F32), V((4, 2, 16, 128), F32),
    ]
    sems = [
        pltpu.SemaphoreType.DMA((10, 6)), pltpu.SemaphoreType.DMA((10, 6)),
        pltpu.SemaphoreType.DMA((2,)), pltpu.SemaphoreType.DMA((2,)), pltpu.SemaphoreType.DMA((14,)),
        pltpu.SemaphoreType.DMA((9,)), pltpu.SemaphoreType.DMA((9,)),
    ]

    def body(*refs):
        n = 13 + len(outs) + len(scratch)
        flat = refs[n : n + 20]
        groups = [flat[i * 4 : i * 4 + 4] for i in range(5)]
        k3_body(*refs[:n], *groups, *refs[n + 20 :])

    return pl.pallas_call(
        body,
        out_shape=outs,
        in_specs=[VM, HB, HB, HB, VM, HB, HB, HB, HB, HB, HB, HB, VM],
        out_specs=[VM] * len(outs),
        scratch_shapes=scratch + sum(fours, []) + rest + sems,
        compiler_params=pltpu.CompilerParams(
            collective_id=2, has_side_effects=True, vmem_limit_bytes=62 << 20
        ),
        name="attend_back_scatter",
    )(br, mg, g1, g2, small, wqb, wp, qs, asv, ctxt, normt, nt, rs)


HEADS = 16
HEAD_DIM = 32
WIN = 4
SHIFT = 2
TABLE = 49


epsilon = 1e-06
highest = lax.Precision.HIGHEST


def from_behind(block, axis, distance):
    devices = range(lax.axis_size(axis))
    route = [((i - distance) % len(devices), i) for i in devices]
    return lax.ppermute(block, axis, route)


def normalize(values, gain_row, bias_row):
    average = jnp.mean(values, -1, keepdims=True)
    centred = values - average
    variance = jnp.mean(centred * centred, -1, keepdims=True)
    return centred * lax.rsqrt(variance + epsilon) * gain_row + bias_row


def exact_gelu(values):
    return jax.nn.gelu(values, approximate=False)


def table_onehot():
    positions = jnp.arange(WIN * WIN)
    row_of = positions // WIN
    column_of = positions % WIN
    table_index = (
        (row_of[:, None] - row_of[None, :] + WIN - 1) * (2 * WIN - 1)
        + column_of[:, None]
        - column_of[None, :]
        + WIN
        - 1
    )
    return (table_index.reshape(-1)[:, None] == jnp.arange(TABLE)[None, :]).astype(jnp.float32)


def to_windows(field_grid):
    clip_count, row_count, column_count, feature_width = field_grid.shape
    blocks = field_grid.reshape(
        clip_count, row_count // WIN, WIN, column_count // WIN, WIN, feature_width
    )
    return blocks.transpose(0, 1, 3, 2, 4, 5).reshape(-1, WIN * WIN, feature_width)


def from_windows(windows, clip_count, row_count, column_count):
    feature_width = windows.shape[-1]
    blocks = windows.reshape(
        clip_count, row_count // WIN, column_count // WIN, WIN, WIN, feature_width
    )
    return blocks.transpose(0, 1, 3, 2, 4, 5).reshape(
        clip_count, row_count, column_count, feature_width
    )


def times_transposed(left, right):
    return lax.dot_general(
        left, right, (((1,), (1,)), ((), ())), preferred_element_type=jnp.float32
    )


def outer_sum(left, right):
    return lax.dot_general(
        left, right, (((0,), (0,)), ((), ())), preferred_element_type=jnp.float32
    )


def per_device(
    inputs,
    grad_mask,
    cotangent,
    ln1_gain,
    ln1_bias,
    w_qkv,
    q_bias,
    v_bias,
    w_proj,
    proj_bias,
    ln2_gain,
    ln2_bias,
    w_fc1,
    fc1_bias,
    w_fc2,
    fc2_bias,
    pos_table,
):
    (
        gain_one,
        bias_one,
        qkv_full,
        qbias_full,
        vbias_full,
        proj_full,
        pbias_full,
        gain_two,
        bias_two,
        fc1_full,
        fc1b_full,
        fc2_full,
        fc2b_full,
    ) = (
        lax.all_gather(ln1_gain, ("clip", "slab"), axis=0, tiled=True),
        lax.all_gather(ln1_bias, ("clip", "slab"), axis=0, tiled=True),
        lax.all_gather(w_qkv, ("clip", "slab"), axis=0, tiled=True),
        lax.all_gather(q_bias, ("clip", "slab"), axis=0, tiled=True),
        lax.all_gather(v_bias, ("clip", "slab"), axis=0, tiled=True),
        lax.all_gather(w_proj, ("clip", "slab"), axis=0, tiled=True),
        lax.all_gather(proj_bias, ("clip", "slab"), axis=0, tiled=True),
        lax.all_gather(ln2_gain, ("clip", "slab"), axis=0, tiled=True),
        lax.all_gather(ln2_bias, ("clip", "slab"), axis=0, tiled=True),
        lax.all_gather(w_fc1, ("clip", "slab"), axis=0, tiled=True),
        lax.all_gather(fc1_bias, ("clip", "slab"), axis=0, tiled=True),
        lax.all_gather(w_fc2, ("clip", "slab"), axis=0, tiled=True),
        lax.all_gather(fc2_bias, ("clip", "slab"), axis=0, tiled=True),
    )
    clip_count, row_count, column_count, feature_width = inputs.shape
    score_scale = 1.0 / math.sqrt(HEAD_DIM)
    float_type = jnp.float32
    half_type = jnp.bfloat16
    ahead = from_behind(inputs[:, :SHIFT], "slab", -1)
    window_rows = jnp.concatenate([inputs[:, SHIFT:], ahead], axis=1).astype(float_type)
    normed, first_pull = jax.vjp(
        normalize, window_rows, gain_one.astype(float_type), bias_one.astype(float_type)
    )
    windows = to_windows(jnp.roll(normed.astype(half_type), -SHIFT, axis=2))
    window_count = windows.shape[0]
    token_count = window_count * WIN * WIN
    head_shape = (window_count, WIN * WIN, HEADS, HEAD_DIM)
    flat_windows = windows.reshape(token_count, feature_width)
    projected = jnp.dot(flat_windows, qkv_full, preferred_element_type=float_type)
    query_heads = (
        (projected[:, :feature_width] + qbias_full.astype(float_type))
        .astype(half_type)
        .reshape(head_shape)
    )
    key_heads = (
        projected[:, feature_width : 2 * feature_width].astype(half_type).reshape(head_shape)
    )
    value_heads = (
        (projected[:, 2 * feature_width :] + vbias_full.astype(float_type))
        .astype(half_type)
        .reshape(head_shape)
    )
    onehot = table_onehot()
    position_bias = (
        jnp.dot(onehot, pos_table, precision=highest)
        .reshape(WIN * WIN, WIN * WIN, HEADS)
        .transpose(2, 0, 1)
    )
    scores = (
        jnp.einsum("wqhc,wkhc->whqk", query_heads, key_heads, preferred_element_type=float_type)
        * score_scale
        + position_bias[None]
    )
    attention = jax.nn.softmax(scores, axis=-1)
    attention_low = attention.astype(half_type)
    context = jnp.einsum(
        "whqk,wkhc->wqhc", attention_low, value_heads, preferred_element_type=float_type
    )
    context = context.astype(half_type).reshape(window_count, WIN * WIN, feature_width)
    context_grid = jnp.roll(
        from_windows(context, clip_count, row_count, column_count), SHIFT, axis=2
    )
    returned = from_behind(context_grid[:, row_count - SHIFT :], "slab", 1)
    own_flat = jnp.concatenate([returned, context_grid[:, : row_count - SHIFT]], axis=1).reshape(
        -1, feature_width
    )
    input_flat = inputs.reshape(-1, feature_width).astype(float_type)
    middle = (
        input_flat
        + jnp.dot(own_flat, proj_full, preferred_element_type=float_type)
        + pbias_full.astype(float_type)
    )
    second, second_pull = jax.vjp(
        normalize, middle, gain_two.astype(float_type), bias_two.astype(float_type)
    )
    second_low = second.astype(half_type)
    pre_act = jnp.dot(second_low, fc1_full, preferred_element_type=float_type) + fc1b_full.astype(
        float_type
    )
    hidden, gelu_pull = jax.vjp(exact_gelu, pre_act)
    hidden_low = hidden.astype(half_type)
    output = (
        middle
        + jnp.dot(hidden_low, fc2_full, preferred_element_type=float_type)
        + fc2b_full.astype(float_type)
    )
    incoming = (cotangent.astype(float_type) * grad_mask.astype(float_type)[..., None]).reshape(
        -1, feature_width
    )
    incoming_low = incoming.astype(half_type)
    fc2_grad = outer_sum(hidden_low, incoming_low)
    fc2b_grad = jnp.sum(incoming, axis=0)
    hidden_grad = times_transposed(incoming_low, fc2_full)
    pre_grad = gelu_pull(hidden_grad)[0].astype(half_type)
    fc1_grad = outer_sum(second_low, pre_grad)
    fc1b_grad = jnp.sum(pre_grad.astype(float_type), axis=0)
    second_grad = times_transposed(pre_grad, fc1_full)
    middle_part, gain_two_grad, bias_two_grad = second_pull(second_grad)
    middle_grad = incoming + middle_part
    branch_low = middle_grad.astype(half_type)
    proj_grad = outer_sum(own_flat, branch_low)
    pbias_grad = jnp.sum(branch_low.astype(float_type), axis=0)
    context_grad = (
        times_transposed(branch_low, proj_full)
        .astype(half_type)
        .reshape(clip_count, row_count, column_count, feature_width)
    )
    sent_back = from_behind(context_grad[:, :SHIFT], "slab", -1)
    window_context_grad = jnp.concatenate([context_grad[:, SHIFT:], sent_back], axis=1)
    context_heads = to_windows(jnp.roll(window_context_grad, -SHIFT, axis=2)).reshape(head_shape)
    value_grad = jnp.einsum(
        "whqk,wqhc->wkhc", attention_low, context_heads, preferred_element_type=float_type
    ).astype(half_type)
    attention_grad = jnp.einsum(
        "wqhc,wkhc->whqk", context_heads, value_heads, preferred_element_type=float_type
    )
    score_grad = (
        attention * (attention_grad - jnp.sum(attention_grad * attention, -1, keepdims=True))
    ).astype(half_type)
    bias_cells = (
        jnp.sum(score_grad.astype(float_type), axis=0)
        .transpose(1, 2, 0)
        .reshape(WIN * WIN * WIN * WIN, HEADS)
    )
    table_grad = lax.dot_general(onehot, bias_cells, (((0,), (0,)), ((), ())), precision=highest)
    query_grad = (
        jnp.einsum("whqk,wkhc->wqhc", score_grad, key_heads, preferred_element_type=float_type)
        * score_scale
    ).astype(half_type)
    key_grad = (
        jnp.einsum("whqk,wqhc->wkhc", score_grad, query_heads, preferred_element_type=float_type)
        * score_scale
    ).astype(half_type)
    query_flat = query_grad.reshape(token_count, feature_width)
    value_flat = value_grad.reshape(token_count, feature_width)
    qkv_grad_low = jnp.concatenate(
        [query_flat, key_grad.reshape(token_count, feature_width), value_flat], axis=1
    )
    qkv_grad = outer_sum(flat_windows, qkv_grad_low)
    qbias_grad = jnp.sum(query_flat.astype(float_type), axis=0)
    vbias_grad = jnp.sum(value_flat.astype(float_type), axis=0)
    normed_grad = times_transposed(qkv_grad_low, qkv_full).reshape(
        window_count, WIN * WIN, feature_width
    )
    normed_grid_grad = jnp.roll(
        from_windows(normed_grad, clip_count, row_count, column_count), SHIFT, axis=2
    )
    rows_part, gain_one_grad, bias_one_grad = first_pull(normed_grid_grad)
    halo_back = from_behind(
        rows_part[:, row_count - SHIFT :].astype(jnp.bfloat16), "slab", 1
    ).astype(jnp.float32)
    input_grad = middle_grad.reshape(
        clip_count, row_count, column_count, feature_width
    ) + jnp.concatenate([halo_back, rows_part[:, : row_count - SHIFT]], axis=1)
    shares = (
        lax.psum_scatter(gain_one_grad, ("clip", "slab"), scatter_dimension=0, tiled=True),
        lax.psum_scatter(bias_one_grad, ("clip", "slab"), scatter_dimension=0, tiled=True),
        lax.psum_scatter(qkv_grad, ("clip", "slab"), scatter_dimension=0, tiled=True),
        lax.psum_scatter(qbias_grad, ("clip", "slab"), scatter_dimension=0, tiled=True),
        lax.psum_scatter(vbias_grad, ("clip", "slab"), scatter_dimension=0, tiled=True),
        lax.psum_scatter(proj_grad, ("clip", "slab"), scatter_dimension=0, tiled=True),
        lax.psum_scatter(pbias_grad, ("clip", "slab"), scatter_dimension=0, tiled=True),
        lax.psum_scatter(gain_two_grad, ("clip", "slab"), scatter_dimension=0, tiled=True),
        lax.psum_scatter(bias_two_grad, ("clip", "slab"), scatter_dimension=0, tiled=True),
        lax.psum_scatter(fc1_grad, ("clip", "slab"), scatter_dimension=0, tiled=True),
        lax.psum_scatter(fc1b_grad, ("clip", "slab"), scatter_dimension=0, tiled=True),
        lax.psum_scatter(fc2_grad, ("clip", "slab"), scatter_dimension=0, tiled=True),
        lax.psum_scatter(fc2b_grad, ("clip", "slab"), scatter_dimension=0, tiled=True),
    )
    table_total = lax.psum(table_grad, ("clip", "slab"))
    output = output.reshape(clip_count, row_count, column_count, feature_width).astype(half_type)
    return (
        output,
        input_grad.astype(half_type),
        shares[0],
        shares[1],
        shares[2],
        shares[3],
        shares[4],
        shares[5],
        shares[6],
        shares[7],
        shares[8],
        shares[9],
        shares[10],
        shares[11],
        shares[12],
        table_total,
    )


def per_device_fast(
    inputs,
    grad_mask,
    cotangent,
    ln1_gain,
    ln1_bias,
    w_qkv,
    q_bias,
    v_bias,
    w_proj,
    proj_bias,
    ln2_gain,
    ln2_bias,
    w_fc1,
    fc1_bias,
    w_fc2,
    fc2_bias,
    pos_table,
):
    bt = (
        jnp.dot(table_onehot(), pos_table, precision=highest)
        .reshape(16, 16, 16)
        .transpose(2, 0, 1)
    )
    smalls = [
        v.reshape(1, 16)
        for v in (ln1_gain, ln1_bias, q_bias, v_bias, proj_bias, ln2_gain, ln2_bias, fc2_bias)
    ]
    shape = inputs.shape
    x = inputs.reshape(8, 256, 512)
    ctx, wqb, wpb, w1b, w2b, par, qs, asv, ctxt, normt, nt, rs = k1_call(
        x, w_qkv, w_proj, w_fc1, w_fc2, smalls, fc1_bias.reshape(1, 64), bt
    )
    wp = wpb.reshape(512, 512)
    output, mg, br, g1, g2, small = k2_call(
        x.reshape(2048, 512), ctx.reshape(2048, 512), cotangent.reshape(2048, 512), grad_mask, par,
        wp, w1b.reshape(512, 2048), w2b.reshape(2048, 512)
    )
    lead = (4, 2, 2, 2)
    input_grad, gq, gp, gf1, gf2, *vectors, fb, tab = k3_call(
        br.reshape(8, 256, 512), mg.reshape(8, 256, 512), g1.reshape(lead + (16, 2048)),
        g2.reshape(lead + (64, 512)), small, wqb, wp, qs, asv, ctxt, normt, nt, rs
    )
    v = [r.reshape(16) for r in vectors]
    table = tab.reshape(8, 8, 16).transpose(1, 0, 2).reshape(64, 16)[:TABLE]
    return (
        output.reshape(shape), input_grad.reshape(shape), v[0], v[1], gq, v[2], v[3], gp, v[4], v[5],
        v[6], gf1, fb.reshape(64), gf2, v[7], table,
    )


def solution(mesh):
    in_specs = (
        P("clip", "slab", None, None),
        P("clip", "slab", None),
        P("clip", "slab", None, None),
        P(("clip", "slab")),
        P(("clip", "slab")),
        P(("clip", "slab"), None),
        P(("clip", "slab")),
        P(("clip", "slab")),
        P(("clip", "slab"), None),
        P(("clip", "slab")),
        P(("clip", "slab")),
        P(("clip", "slab")),
        P(("clip", "slab"), None),
        P(("clip", "slab")),
        P(("clip", "slab"), None),
        P(("clip", "slab")),
        P(),
    )
    out_specs = (
        P("clip", "slab", None, None),
        P("clip", "slab", None, None),
        P(("clip", "slab")),
        P(("clip", "slab")),
        P(("clip", "slab"), None),
        P(("clip", "slab")),
        P(("clip", "slab")),
        P(("clip", "slab"), None),
        P(("clip", "slab")),
        P(("clip", "slab")),
        P(("clip", "slab")),
        P(("clip", "slab"), None),
        P(("clip", "slab")),
        P(("clip", "slab"), None),
        P(("clip", "slab")),
        P(),
    )
    fits = mesh.shape["clip"] == 16 and mesh.shape["slab"] == 2
    return jax.shard_map(
        per_device_fast if fits else per_device, mesh=mesh, in_specs=in_specs, out_specs=out_specs, check_vma=False
    )
```

```python
import functools
import math

import jax
import jax.numpy as jnp
from jax import lax
from jax.experimental import pallas as pl
from jax.experimental.pallas import tpu as pltpu
from jax.sharding import PartitionSpec as P

F32 = jnp.float32
BF = jnp.bfloat16
MESH = pl.DeviceIdType.MESH
SCALE = 1.0 / math.sqrt(32.0)
NT = (((1,), (1,)), ((), ()))
TN = (((0,), (0,)), ((), ()))
VM = pl.BlockSpec(memory_space=pltpu.VMEM)
HB = pl.BlockSpec(memory_space=pl.ANY)
UNROLL = 16
TABLE = 49


def dot(a, b, dims=(((1,), (0,)), ((), ()))):
    return lax.dot_general(a, b, dims, preferred_element_type=F32)


def tree(xs, op=lambda a, b: a + b):
    xs = list(xs)
    while len(xs) > 1:
        xs = [op(xs[i], xs[i + 1]) if i + 1 < len(xs) else xs[i] for i in range(0, len(xs), 2)]
    return xs[0]


def tile(ref, i):
    return ref[pl.ds(pl.multiple_of(i * 16, 16), 16), :]


def row(ref, i):
    return jnp.broadcast_to(ref[pl.ds(i, 1), :], (16, 128))


def pair_products(a_ref, a0, b_ref, b0):
    def body(d, acc):
        ad = tile(a_ref, a0 + d)
        return tuple(acc[q] + ad * row(b_ref, (b0 + d) * 16 + q) for q in range(16))

    return lax.fori_loop(
        0, 32, body, tuple(jnp.zeros((16, 128), F32) for _ in range(16)), unroll=UNROLL
    )


def weighted(ws, b_ref, b0, o_ref, o0, scale):
    def body(d, carry):
        parts = []
        for k in range(4):
            t = ws[4 * k] * row(b_ref, (b0 + d) * 16 + 4 * k)
            for q in range(4 * k + 1, 4 * k + 4):
                t = t + ws[q] * row(b_ref, (b0 + d) * 16 + q)
            parts.append(t)
        s = (parts[0] + parts[1]) + (parts[2] + parts[3])
        if scale is not None:
            s = s * scale
        o_ref[pl.ds(pl.multiple_of((o0 + d) * 16, 16), 16), :] = s.astype(BF).astype(F32)
        return carry

    lax.fori_loop(0, 32, body, 0, unroll=UNROLL)


class Place:
    def __init__(self):
        self.clip = lax.axis_index("clip")
        self.y = lax.axis_index("slab")
        self.c = self.clip % 2
        self.x = (self.clip // 2) % 2
        self.z = self.clip // 4
        self.rank8 = self.x * 4 + self.c * 2 + self.y
        base = self.x * 2 + self.c
        self.along_z = [(((self.z + d) % 4) * 4 + base, self.y) for d in (1, 2, 3)]
        self.over_x = (self.clip + 2 - 4 * self.x, self.y)
        self.over_y = (self.clip, 1 - self.y)
        self.over_core = (self.clip + 1 - 2 * self.c, self.y)

    def greet(self):
        barrier = pltpu.get_barrier_semaphore()
        others = self.along_z + [self.over_x, self.over_y, self.over_core]
        for other in others:
            pl.semaphore_signal(barrier, inc=1, device_id=other, device_id_type=MESH)

    def met(self):
        pl.semaphore_wait(pltpu.get_barrier_semaphore(), 6)


def remote(src, dst, ssem, rsem, to):
    return pltpu.make_async_remote_copy(
        src_ref=src, dst_ref=dst, send_sem=ssem, recv_sem=rsem, device_id=to, device_id_type=MESH
    )


class Gather:
    def __init__(self, place, pieces, ssem, rsem):
        self.copies = []
        z, x, c, y = place.z, place.x, place.c, place.y
        for k, (buf, c0, n, first_x, first) in enumerate(pieces):
            cols = pl.ds(c0, n)

            def cp(ix, s, to, k=k, buf=buf, cols=cols):
                ref = buf.at[ix + (slice(None), cols)]
                return remote(ref, ref, ssem.at[k, s], rsem.at[k, s], to)

            al = slice(None)
            mine = buf.at[z, x, c, y, :, cols]
            steps = [
                [
                    remote(
                        mine if first is None else first.at[:, cols],
                        mine,
                        ssem.at[k, d],
                        rsem.at[k, d],
                        place.along_z[d],
                    )
                    for d in range(3)
                ]
            ]
            if first_x:
                steps.append([cp((al, x, c, y), 3, place.over_x)])
                steps.append([cp((al, al, c, y), 4, place.over_y)])
            else:
                steps.append([cp((al, x, c, y), 3, place.over_y)])
                steps.append([cp((al, x, c, al), 4, place.over_x)])
            steps.append([cp((al, al, c, al), 5, place.over_core)])
            self.copies.append(steps)

    def start(self, k, s):
        for copy in self.copies[k][s]:
            copy.start()

    def advance(self, k, s):
        for copy in self.copies[k][s]:
            copy.wait_recv()
        if s < 3:
            self.start(k, s + 1)

    def close(self):
        for steps in self.copies:
            for step in steps:
                for copy in step:
                    copy.wait_send()


PLAN_GATHER = (
    (), (), ((0, 0),), (),
    ((1, 0), (2, 0), (0, 1), (3, 0), (1, 1), (4, 0), (2, 1), (5, 0), (6, 0), (0, 2), (1, 2), (3, 1), (0, 3), (1, 3)),
    ((4, 1),), ((6, 1), (7, 0)), ((2, 2),), (),
    ((2, 3), (5, 1)), ((3, 2),), ((4, 2), (8, 0)), ((3, 3),), ((4, 3), (5, 2), (6, 2)), ((9, 0),), ((5, 3), (6, 3)),
    (), ((7, 1), (8, 1)), ((10, 0),), (), (), ((9, 1),), (),
    (), (), (), (), ((7, 2),), ((8, 2),), (),
    ((7, 3),), ((8, 3), (10, 1)), (), (), (), (), (),
    ((9, 2), (9, 3), (10, 2), (10, 3)),
)


def spots(p):
    i, j = p // 4, p % 4
    return (i * 8 + (j + 2) % 8, i * 8 + (j + 6) % 8)


def gathered(ref, lo, hi):
    return jnp.concatenate([ref[pl.ds(lo, 64, stride=32), :], ref[pl.ds(hi, 64, stride=32), :]], axis=0)


def position_bias(tab_ref, bt_ref):
    for p in range(0, 16, 4):
        entry = lax.broadcasted_iota(jnp.int32, (TABLE, 512), 0)
        lane = lax.broadcasted_iota(jnp.int32, (TABLE, 512), 1)
        pi = lane // 128 + p
        qi = lane % 128
        index = (pi // 4 - qi // 4 + 3) * 7 + pi % 4 - qi % 4 + 3
        one = ((index == entry) & (qi < 16)).astype(F32)
        res = jnp.dot(
            tab_ref[...], one, precision=lax.Precision.HIGHEST, preferred_element_type=F32
        )
        for k in range(4):
            bt_ref[pl.ds(p + k, 16, stride=16), :] = res[:, k * 128 : (k + 1) * 128]


def small_block(place, small_refs, fc1b_ref, scr):
    scr[...] = jnp.zeros_like(scr)
    for k, ref in enumerate(small_refs):
        scr[k : k + 1, 0:16] = ref[...].astype(F32)
    lane = lax.broadcasted_iota(jnp.int32, (128, 128), 1)
    src = lax.broadcasted_iota(jnp.int32, (128, 128), 0)
    sel = ((lane == place.rank8 * 16 + src) & (src < 16)).astype(F32).astype(BF)
    vectors = dot(scr[...].astype(BF), sel)
    scr[0:1, 0:64] = fc1b_ref[...].astype(F32)
    half = ((lane == place.y * 64 + src) & (src < 64)).astype(F32).astype(BF)
    wide = dot(scr[0:1, :].astype(BF), half)
    r = lax.broadcasted_iota(jnp.int32, (16, 128), 0)
    return jnp.where(
        r < 8,
        vectors,
        jnp.where(r == 8 + place.x * 2 + place.c, jnp.broadcast_to(wide, (16, 128)), 0.0),
    ).astype(BF)


def k1_body(
    x_h, wq_ref, wp_ref, w1_ref, w2_ref, s0, s1, s2, s3, s4, s5, s6, s7, fb_ref, tab_ref,
    ctx_ref, wqb_h, wpb, w1b, w2b, par_ref, qkv_save, att_save, ctxt_h, normt_h, nt_h, rs_ref,
    x_ref, xs, ntf, g_ref, ct_ref, cs_ref, a_ref, qb, halo, chalo, gains, scr,
    wqb, ctxt_ref, normt_ref, nt_ref, bt_ref, ssem, rsem, hss, hrs, lsem, osem,
):
    me = Place()
    z, x, c, y = me.z, me.x, me.c, me.y
    own = [
        pltpu.make_async_copy(src, buf.at[z, x, c, y], osem.at[i])
        for i, (src, buf) in enumerate(((wp_ref, wpb), (w1_ref, w1b), (w2_ref, w2b)))
    ]
    for cp in own:
        cp.start()
    xload = pltpu.make_async_copy(x_h, x_ref, osem.at[3])
    xload.start()
    me.greet()
    for g in range(4):
        for k in range(3):
            wqb[z, x, c, y, :, 128 + g * 384 + k * 128 : 256 + g * 384 + k * 128] = wq_ref[
                :, k * 512 + g * 128 : k * 512 + g * 128 + 128
            ]
    wqb[z, x, c, y, :, 0:128] = small_block(me, (s0, s1, s2, s3, s4, s5, s6, s7), fb_ref, scr)
    pieces = [(wqb, 0, 256, True, None), (wqb, 256, 256, False, None)]
    pieces += [(wqb, 128 + g * 384, 384, g % 2 == 1, None) for g in (1, 2, 3)]
    pieces += [(wpb, 0, 256, False, wp_ref), (wpb, 256, 256, True, wp_ref)]
    pieces += [(w1b, 0, 1024, False, w1_ref), (w1b, 1024, 1024, True, w1_ref)]
    pieces += [(w2b, 0, 256, False, w2_ref), (w2b, 256, 256, True, w2_ref)]
    gat = Gather(me, pieces, ssem, rsem)
    me.met()
    for k in range(5):
        gat.start(k, 0)
    xhalo = remote(x_h.at[:, 0:16, :], halo, hss.at[4], hrs.at[4], me.over_y)
    xhalo.start()
    plan = [list(part) for part in PLAN_GATHER]

    def progress():
        for k, s in plan.pop(0):
            gat.advance(k, s)

    xload.wait()
    for b in range(8):
        for k in range(4):
            xs[k, b * 256 : b * 256 + 240, :] = x_ref[b, 16:256, k * 128 : k * 128 + 128].astype(F32)
    for k in range(5, 11):
        gat.start(k, 0)
    xhalo.wait_recv()
    for b in range(8):
        for k in range(4):
            xs[k, b * 256 + 240 : b * 256 + 256, :] = halo[b, :, k * 128 : k * 128 + 128].astype(F32)

    def norm_block(p):
        lo, hi = spots(p)
        turned = jnp.concatenate([gathered(xs.at[k], lo, hi).T for k in range(4)], axis=0)
        mean = jnp.mean(turned, 0, keepdims=True)
        cen = turned - mean
        rs = lax.rsqrt(jnp.mean(cen * cen, 0, keepdims=True) + 1e-6)
        ntf[:, p * 128 : (p + 1) * 128] = cen * rs
        rs_ref[p : p + 1, :] = rs

    position_bias(tab_ref, bt_ref)
    for p in range(16):
        norm_block(p)
        if p % 4 == 3:
            progress()
    for cp in own:
        cp.wait()
    progress()
    for zz in range(4):
        total = jnp.sum(wqb[zz, :, :, :, :, 0:128].astype(F32).reshape(8, 16, 128), axis=0)
        par_ref[0:8, zz * 128 : (zz + 1) * 128] = total[0:8]
        for k in range(4):
            par_ref[8 + zz : 9 + zz, k * 128 : (k + 1) * 128] = total[8 + k : 9 + k]
    par_ref[12:16, :] = jnp.zeros((4, 512), F32)
    turned = par_ref[...].T
    for k in range(4):
        gains[k] = jnp.broadcast_to(turned[:, k : k + 1], (512, 128))

    def finish_norm(p, carry):
        cols = pl.ds(pl.multiple_of(p * 128, 128), 128)
        n = ntf[:, cols]
        normt_ref[:, cols] = (n * gains[0] + gains[1]).astype(BF)
        nt_ref[:, cols] = n.astype(BF)
        return carry

    for t in range(4):
        lax.fori_loop(t * 4, t * 4 + 4, finish_norm, 0)
        progress()

    outs = []

    def out(src, dst, i):
        cp = pltpu.make_async_copy(src, dst, lsem.at[i])
        cp.start()
        outs.append(cp)

    out(normt_ref, normt_h, 8)
    out(nt_ref, nt_h, 9)
    save = None
    for g in range(4):
        w = wqb[:, :, :, :, :, 128 + g * 384 : 512 + g * 384].reshape(512, 384)
        wt = w.astype(F32).T.astype(BF)
        fs = slice(g * 128, (g + 1) * 128)
        if save is not None:
            save.wait()
        for t in range(2):
            res = dot(wt, normt_ref[:, t * 1024 : t * 1024 + 1024])
            for k in range(8):
                block = res[:, k * 128 : (k + 1) * 128]
                block = jnp.concatenate(
                    [block[0:128] + gains[2, fs, :], block[128:256], block[256:384] + gains[3, fs, :]],
                    axis=0,
                )
                g_ref[pl.ds(t * 8 + k, 384, stride=16), :] = block.astype(BF).astype(F32)
            if t == 0:
                progress()

        def keep(i, carry):
            rows = pl.ds(pl.multiple_of(i * 512, 512), 512)
            qb[rows, :] = g_ref[rows, :].astype(BF)
            return carry

        lax.fori_loop(0, 12, keep, 0)
        save = pltpu.make_async_copy(qb, qkv_save.at[g], lsem.at[g])
        save.start()
        if g == 3:
            out(wqb, wqb_h, 10)
        progress()

        def head(h, carry, g=g):
            acc = pair_products(g_ref, h * 32, g_ref, 128 + h * 32)
            bt = tile(bt_ref, g * 4 + h)
            s = [
                acc[q] * SCALE + jnp.broadcast_to(bt[:, q : q + 1], (16, 128)) for q in range(16)
            ]
            m = tree(s, jnp.maximum)
            e = [jnp.exp(v - m) for v in s]
            inv = 1.0 / tree(e)
            low = []
            for q in range(16):
                a = e[q] * inv
                a_ref[pl.ds(pl.multiple_of((g * 4 + h) * 256 + q * 16, 16), 16), :] = a
                low.append(a.astype(BF).astype(F32))
            weighted(low, g_ref, 256 + h * 32, ct_ref, h * 32, None)
            return carry

        for h in range(4):
            lax.fori_loop(h, h + 1, head, 0)
            progress()
        out(a_ref.at[pl.ds(g * 1024, 1024), :], att_save.at[pl.ds(g * 1024, 1024), :], 4 + g)
        for p in range(16):
            block = ct_ref[pl.ds(p, 128, stride=16), :]
            ctxt_ref[fs, p * 128 : (p + 1) * 128] = block.astype(BF)
            turned = block.T
            lo, hi = spots(p)
            cs_ref[pl.ds(lo, 64, stride=32), :] = turned[0:64]
            cs_ref[pl.ds(hi, 64, stride=32), :] = turned[64:128]
        for b in range(8):
            ctx_ref[b, 16:256, fs] = cs_ref[b * 256 : b * 256 + 240, :].astype(BF)
            chalo[g, b] = cs_ref[b * 256 + 240 : b * 256 + 256, :].astype(BF)
        send = remote(chalo.at[g], ctx_ref.at[:, 0:16, pl.ds(g * 128, 128)], hss.at[g], hrs.at[g], me.over_y)
        send.start()
        outs.append(send)
        out(ctxt_ref.at[pl.ds(g * 128, 128), :], ctxt_h.at[pl.ds(g * 128, 128), :], 11 + g)
        progress()
    while plan:
        progress()
    save.wait()
    for cp in outs:
        cp.wait()
    xhalo.wait_send()
    gat.close()


def k1_call(x, wq, wp, w1, w2, smalls, fb, bt):
    S = jax.ShapeDtypeStruct
    lead = (4, 2, 2, 2)
    outs = [
        (S((8, 256, 512), BF), VM),
        (S(lead + (16, 1664), BF), HB),
        (S(lead + (16, 512), BF), HB),
        (S(lead + (16, 2048), BF), HB),
        (S(lead + (64, 512), BF), HB),
        (S((16, 512), F32), VM),
        (S((4, 6144, 128), BF), HB),
        (S((4096, 128), F32), HB),
        (S((512, 2048), BF), HB),
        (S((512, 2048), BF), HB),
        (S((512, 2048), BF), HB),
        (S((16, 128), F32), VM),
    ]
    V = pltpu.VMEM
    return pl.pallas_call(
        k1_body,
        out_shape=[o[0] for o in outs],
        in_specs=[HB] + [VM] * 14,
        out_specs=[o[1] for o in outs],
        scratch_shapes=[
            V((8, 256, 512), BF), V((4, 2048, 128), F32), V((512, 2048), F32), V((6144, 128), F32),
            V((2048, 128), F32), V((2048, 128), F32), V((4096, 128), F32), V((6144, 128), BF),
            V((8, 16, 512), BF), V((4, 8, 16, 128), BF), V((4, 512, 128), F32), V((16, 128), F32),
            V(lead + (16, 1664), BF), V((512, 2048), BF), V((512, 2048), BF), V((512, 2048), BF), V((256, 128), F32),
            pltpu.SemaphoreType.DMA((11, 6)), pltpu.SemaphoreType.DMA((11, 6)),
            pltpu.SemaphoreType.DMA((5,)), pltpu.SemaphoreType.DMA((5,)),
            pltpu.SemaphoreType.DMA((15,)), pltpu.SemaphoreType.DMA((4,)),
        ],
        compiler_params=pltpu.CompilerParams(
            collective_id=1, has_side_effects=True, vmem_limit_bytes=60 << 20
        ),
        name="gather_attend",
    )(x, wq, wp, w1, w2, *smalls, fb, bt)


def gelu_parts(a):
    z = jnp.abs(a) * 0.7071067811865476
    t = 1.0 / (1.0 + 0.3275911 * z)
    e = jnp.exp(a * a * -0.5)
    p = 0.5307027145 * t - 0.7265760135
    p = p * t + 0.7107068705
    p = p * t - 0.142248368
    p = p * t + 0.127414796
    tail = p * t * e
    return jnp.where(a >= 0, 1.0 - tail, tail), e * 0.3989422804014327


CH = 512
FJ = 512


def k2_body(
    x_ref, ctx_ref, cot_ref, mask_ref, par_ref, wp_ref, w1_ref, w2_ref,
    out_ref, mg_ref, br_ref, g1_ref, g2_ref, small_ref, hid_ref, pg_ref, sec_ref, inc_ref,
):
    pb, g2, b2, fb2 = (par_ref[k : k + 1, :] for k in (4, 5, 6, 7))
    small_ref[...] = jnp.zeros_like(small_ref)
    rsel = (
        lax.broadcasted_iota(jnp.int32, (256, 32), 0) // 8
        == lax.broadcasted_iota(jnp.int32, (256, 32), 1)
    ).astype(F32).astype(BF)
    csel = lax.broadcasted_iota(jnp.int32, (256, 8), 0) % 8 == lax.broadcasted_iota(
        jnp.int32, (256, 8), 1
    )

    def chunk(i, carry):
        rows = pl.ds(pl.multiple_of(i * CH, CH), CH)
        mid = x_ref[rows, :].astype(F32) + dot(ctx_ref[rows, :], wp_ref[...]) + pb
        cen = mid - jnp.mean(mid, 1, keepdims=True)
        rs = lax.rsqrt(jnp.mean(cen * cen, 1, keepdims=True) + 1e-6)
        n2 = cen * rs
        sec = (n2 * g2 + b2).astype(BF)
        sec_ref[rows, :] = sec
        marks = []
        for k in range(CH // 256):
            spread = dot(rsel, mask_ref[i * (CH // 256) + k].astype(F32).astype(BF), NT)
            marks.append(jnp.sum(jnp.where(csel, spread, 0.0), 1, keepdims=True))
        inc = cot_ref[rows, :].astype(F32) * jnp.concatenate(marks, 0)
        low = inc.astype(BF)
        inc_ref[rows, :] = low
        small_ref[7:8, :] += jnp.sum(inc, 0, keepdims=True)
        total = back = None
        for j in range(2048 // FJ):
            cols = slice(j * FJ, (j + 1) * FJ)
            pre = dot(sec, w1_ref[:, cols]) + par_ref[8 + j : 9 + j, :]
            hg = dot(low, w2_ref[cols, :], NT)
            cdf, pdf = gelu_parts(pre)
            hid = (pre * cdf).astype(BF)
            hid_ref[rows, cols] = hid
            pg = (hg * (cdf + pre * pdf)).astype(BF)
            pg_ref[rows, cols] = pg
            small_ref[8 + j : 9 + j, :] += jnp.sum(pg.astype(F32), 0, keepdims=True)
            o = dot(hid, w2_ref[cols, :])
            s = dot(pg, w1_ref[:, cols], NT)
            total = o if total is None else total + o
            back = s if back is None else back + s
        out_ref[rows, :] = (mid + total + fb2).astype(BF)
        small_ref[5:6, :] += jnp.sum(back * n2, 0, keepdims=True)
        small_ref[6:7, :] += jnp.sum(back, 0, keepdims=True)
        eg = back * g2
        r = (eg - jnp.mean(eg, 1, keepdims=True) - n2 * jnp.mean(eg * n2, 1, keepdims=True)) * rs
        mg = inc + r
        mg_ref[rows, :] = mg
        br = mg.astype(BF)
        br_ref[rows, :] = br
        small_ref[4:5, :] += jnp.sum(br.astype(F32), 0, keepdims=True)
        return carry

    lax.fori_loop(0, 2048 // CH, chunk, 0)

    def grads_one(j, carry):
        cols = pl.ds(pl.multiple_of(j * 256, 256), 256)
        g1_ref[:, cols] = dot(sec_ref[...], pg_ref[:, cols], TN).astype(BF)
        return carry

    lax.fori_loop(0, 8, grads_one, 0)

    def grads_two(j, carry):
        cols = pl.ds(pl.multiple_of(j * 256, 256), 256)
        g2_ref[cols, :] = dot(hid_ref[:, cols], inc_ref[...], TN).astype(BF)
        return carry

    lax.fori_loop(0, 8, grads_two, 0)


def k2_call(x, ctx, cot, mask, par, wp, w1, w2):
    S = jax.ShapeDtypeStruct
    V = pltpu.VMEM
    return pl.pallas_call(
        k2_body,
        out_shape=[
            S((2048, 512), BF), S((2048, 512), F32), S((2048, 512), BF),
            S((512, 2048), BF), S((2048, 512), BF), S((16, 512), F32),
        ],
        in_specs=[VM] * 8,
        out_specs=[VM] * 6,
        scratch_shapes=[V((2048, 2048), BF)] * 2 + [V((2048, 512), BF)] * 2,
        compiler_params=pltpu.CompilerParams(vmem_limit_bytes=60 << 20),
        name="feed_forward",
    )(x, ctx, cot, mask, par, wp, w1, w2)


PLAN_SCATTER = (((0, 0), (1, 0), (2, 0)), ((3, 0),), (), ((4, 0), (5, 0)), (), (), ((0, 1), (1, 1)), (), (), ((2, 1), (3, 1), (6, 0)), ((4, 1), (5, 1)), (), ((0, 2), (1, 2)), (), ((2, 2), (3, 2)), ((4, 2), (6, 1), (7, 0)), ((0, 3), (5, 2)), ((1, 3), (6, 2)), (), ((2, 3), (7, 1)), (), ((3, 3), (8, 0)), ((4, 3), (5, 3), (7, 2)), ((6, 3),), ((7, 3), (8, 1)), (), ((8, 2), (9, 0)), (), ((8, 3), (9, 1)), (), ((9, 2),), (), (), ((9, 3),))


class Scatter:
    def __init__(self, place, pieces, ssem, rsem):
        self.me = place
        self.pieces = pieces
        self.steps = []
        z, x, c, y = place.z, place.x, place.c, place.y
        al = slice(None)
        for k, (src, c0, n, first_y, own, s, r1, r2, r3, r4, done) in enumerate(pieces):
            cols = pl.ds(c0, n)

            def cp(a, b, i, to, k=k):
                return remote(a, b, ssem.at[k, i], rsem.at[k, i], to)

            steps = [[cp(src.at[:, :, 1 - c, :, :, cols], r1, 0, place.over_core)]]
            if first_y:
                steps.append([cp(s.at[:, :, 1 - y], r2, 1, place.over_y)])
                steps.append([cp(s.at[:, 1 - x, y], r3, 2, place.over_x)])
            else:
                steps.append([cp(s.at[:, 1 - x], r2, 1, place.over_x)])
                steps.append([cp(s.at[:, x, 1 - y], r3, 2, place.over_y)])
            steps.append(
                [
                    cp(s.at[(z + 1 + d) % 4, x, y], r4.at[d], 3 + d, place.along_z[d])
                    for d in range(3)
                ]
            )
            self.steps.append(steps)

    def start(self, k, i):
        for copy in self.steps[k][i]:
            copy.start()

    def advance(self, k, i):
        me = self.me
        z, x, c, y = me.z, me.x, me.c, me.y
        src, c0, n, first_y, own, s, r1, r2, r3, r4, done = self.pieces[k]
        cols = pl.ds(c0, n)
        for copy in self.steps[k][i]:
            copy.wait_recv()
        if i == 0:
            if own is not None:
                own.wait()

            def add(zz, carry):
                held = s[zz] if own is not None else src[zz, :, c, :, :, cols]
                s[zz] = (held.astype(F32) + r1[zz].astype(F32)).astype(BF)
                return carry

            lax.fori_loop(0, 4, add, 0)
        elif i == 1 and first_y:
            s[:, :, y] = (s[:, :, y].astype(F32) + r2[...].astype(F32)).astype(BF)
        elif i == 1:
            s[:, x] = (s[:, x].astype(F32) + r2[...].astype(F32)).astype(BF)
        elif i == 2:
            s[:, x, y] = (s[:, x, y].astype(F32) + r3[...].astype(F32)).astype(BF)
        else:
            done(tree([s[z, x, y].astype(F32)] + [r4[d].astype(F32) for d in range(3)]))
        if i < 3:
            self.start(k, i + 1)

    def close(self):
        for steps in self.steps:
            for step in steps:
                for copy in step:
                    copy.wait_send()


def k3_body(
    br_ref, mg_h, g1_ref, g2_ref, small_ref, wqb_h, wp_h, qkv_save, att_save, ctxt_h, normt_h, nt_h, rs_ref,
    ig_ref, gq_ref, gp_ref, gf1_ref, gf2_ref, vec_ref,
    bs, bp, mg, wq, wp, qb, g_ref, dg, dc, a_ref, dqt, ctxt, normt, nt, ds_ref, low_ref,
    gacc, pgrad, qgrad, bhalo, rhalo, rout, cells, ar, arr, arz,
    s4, r14, r24, r34, r44, sp, r1p, r2p, r3p, r4p, sq, r1q, r2q, r3q, r4q,
    ssem, rsem, hss, hrs, lsem, asems, aremr,
):
    me = Place()
    z, x, c, y = me.z, me.x, me.c, me.y
    me.greet()
    me.met()

    def local(src, dst, i):
        cp = pltpu.make_async_copy(src, dst, lsem.at[i])
        cp.start()
        return cp

    pieces = []
    owns = []
    for k, (src, rows, n) in enumerate(((g2_ref, 64, 256), (g1_ref, 16, 1024))):
        for half in range(2):
            j = k * 2 + half
            own = local(
                src.at[:, :, c, :, :, pl.ds(half * n, n)], s4[j], 10 + j
            )
            out = gf2_ref if k == 0 else gf1_ref

            def done(v, out=out, c0=half * n, n=n):
                out[:, c0 : c0 + n] = v

            pieces.append((src, half * n, n, half == 0, own, s4[j], r14[j], r24[j], r34[j], r44[j], done))
    for half in range(2):

        def done(v, c0=half * 256):
            gp_ref[:, c0 : c0 + 256] = v

        pieces.append(
            (pgrad, half * 256, 256, half == 0, None, sp.at[half], r1p.at[half], r2p.at[half], r3p.at[half], r4p.at[half], done)
        )
    for g in range(4):

        def done(v, g=g):
            for k in range(3):
                gq_ref[:, k * 512 + g * 128 : k * 512 + g * 128 + 128] = v[:, k * 128 : k * 128 + 128]

        pieces.append(
            (qgrad.at[g], 0, 384, g % 2 == 0, None, sq.at[g], r1q.at[g], r2q.at[g], r3q.at[g], r4q.at[g], done)
        )
    sca = Scatter(me, pieces, ssem, rsem)
    bh = remote(br_ref.at[:, 0:16, :], bhalo, hss.at[0], hrs.at[0], me.over_y)
    bh.start()
    for k in range(4):
        sca.start(k, 0)
    load_c = local(ctxt_h, ctxt, 0)
    load_p = local(wp_h, wp, 1)
    load_q = local(qkv_save.at[0], qb, 2)
    load_a = local(att_save, a_ref, 3)
    load_n = local(normt_h, normt, 4)
    load_t = local(nt_h, nt, 5)
    load_w = local(wqb_h, wq, 6)
    load_m = local(mg_h, mg, 7)
    for b in range(8):
        for k in range(4):
            bs[k, b * 256 : b * 256 + 240, :] = br_ref[b, 16:256, k * 128 : k * 128 + 128].astype(F32)
    bh.wait_recv()
    for b in range(8):
        for k in range(4):
            bs[k, b * 256 + 240 : b * 256 + 256, :] = bhalo[b, :, k * 128 : k * 128 + 128].astype(F32)
    for p in range(16):
        lo, hi = spots(p)
        for k in range(4):
            bp[p * 128 : p * 128 + 128, k * 128 : k * 128 + 128] = gathered(bs.at[k], lo, hi).astype(BF)
    plan = [list(part) for part in PLAN_SCATTER]

    def progress():
        if plan:
            for k, s in plan.pop(0):
                sca.advance(k, s)

    progress()
    load_c.wait()
    pgrad[...] = dot(ctxt[...], bp[...]).astype(BF).reshape(4, 2, 2, 2, 16, 512)
    sca.start(4, 0)
    sca.start(5, 0)
    progress()
    load_p.wait()
    load_a.wait()
    cells[...] = jnp.zeros_like(cells)
    lanes = lax.broadcasted_iota(jnp.int32, (16, 128), 1)
    for g in range(4):
        fs = slice(g * 128, (g + 1) * 128)

        def context_grad(t, carry, fs=fs):
            out = dot(wp[fs, :], bp[pl.ds(pl.multiple_of(t * 512, 512), 512), :], NT)
            for k in range(4):
                dc[pl.ds(t * 4 + k, 128, stride=16), :] = (
                    out[:, k * 128 : (k + 1) * 128].astype(BF).astype(F32)
                )
            return carry

        lax.fori_loop(0, 4, context_grad, 0)
        load_q.wait()

        def widen(i, carry):
            rows = pl.ds(pl.multiple_of(i * 512, 512), 512)
            g_ref[rows, :] = qb[rows, :].astype(F32)
            return carry

        lax.fori_loop(0, 12, widen, 0)
        if g < 3:
            load_q = local(qkv_save.at[g + 1], qb, 2)
        progress()

        def head(h, carry, g=g):
            da = pair_products(dc, h * 32, g_ref, 256 + h * 32)
            a0 = (g * 4 + h) * 16
            at = [tile(a_ref, a0 + q) for q in range(16)]
            tot = tree([da[q] * at[q] for q in range(16)])
            ds = []
            mine = lanes == g * 4 + h
            for q in range(16):
                low_ref[q * 16 : q * 16 + 16, :] = at[q].astype(BF).astype(F32)
                d = (at[q] * (da[q] - tot)).astype(BF).astype(F32)
                ds_ref[q * 16 : q * 16 + 16, :] = d
                ds.append(d)
                cell = jnp.sum(d, axis=1, keepdims=True)
                cells[q * 16 : q * 16 + 16, :] += jnp.where(mine, cell, 0.0)
            weighted(ds, g_ref, 128 + h * 32, dg, h * 32, SCALE)
            turned = [ds_ref[pl.ds(p, 16, stride=16), :] for p in range(16)]
            weighted(turned, g_ref, h * 32, dg, 128 + h * 32, SCALE)
            turned = [low_ref[pl.ds(p, 16, stride=16), :] for p in range(16)]
            weighted(turned, dc, h * 32, dg, 256 + h * 32, None)
            return carry

        for h in range(4):
            lax.fori_loop(h, h + 1, head, 0)
            progress()
        sums = jnp.zeros((384, 128), F32)
        for p in range(16):
            v = dg[pl.ds(p, 384, stride=16), :]
            sums = sums + v
            dqt[g * 384 : (g + 1) * 384, p * 128 : (p + 1) * 128] = v.astype(BF)
        ar[g, 2:3, :] = jnp.sum(sums[0:128].T, 0, keepdims=True)
        ar[g, 3:4, :] = jnp.sum(sums[256:384].T, 0, keepdims=True)
        if g == 0:
            load_n.wait()
        rows = slice(g * 384, g * 384 + 384)
        qgrad[g] = dot(normt[...], dqt[rows, :], NT).astype(BF).reshape(4, 2, 2, 2, 16, 384)
        sca.start(6 + g, 0)
        progress()
    load_w.wait()
    load_t.wait()
    wall = wq[:, :, :, :, :, 128:1664].reshape(512, 1536)
    gain = jnp.broadcast_to(wq_gain(wq), (512, 128))
    gacc[...] = jnp.zeros_like(gacc)

    def norm_back(t):
        e4 = dot(wall, dqt[:, t * 512 : t * 512 + 512])
        for k in range(4):
            p = t * 4 + k
            e = e4[:, k * 128 : (k + 1) * 128]
            n = nt[:, p * 128 : p * 128 + 128].astype(F32)
            gacc[0] += e * n
            gacc[1] += e
            eg = e * gain
            m2 = jnp.mean(eg * n, 0, keepdims=True)
            r = (eg - jnp.mean(eg, 0, keepdims=True) - n * m2) * rs_ref[p : p + 1, :]
            lo = t * 8 + (k + 2) % 8
            hi = t * 8 + (k + 6) % 8
            for q in range(4):
                turned = r[q * 128 : q * 128 + 128].T
                bs[q, pl.ds(lo, 64, stride=32), :] = turned[0:64]
                bs[q, pl.ds(hi, 64, stride=32), :] = turned[64:128]

    for t in range(4):
        norm_back(t)
        progress()
    for b in range(8):
        for k in range(4):
            rout[b, :, k * 128 : k * 128 + 128] = bs[k, b * 256 + 240 : b * 256 + 256, :].astype(BF)
    rh = remote(rout, rhalo, hss.at[1], hrs.at[1], me.over_y)
    rh.start()
    for zz in range(4):
        ls = slice(zz * 128, zz * 128 + 128)
        for k in range(2):
            ar[zz, k : k + 1, :] = jnp.sum(gacc[k, ls, :].T, 0, keepdims=True)
        ar[zz, 4:8, :] = small_ref[4:8, ls]
        for k in range(4):
            ar[zz, 8 + k : 9 + k, :] = small_ref[8 + zz : 9 + zz, k * 128 : k * 128 + 128]
        ar[zz, 12:16, :] = jnp.zeros((4, 128), F32)
    pair = lax.broadcasted_iota(jnp.int32, (256, 128), 0)
    entry = lax.broadcasted_iota(jnp.int32, (256, 128), 1)
    qi, pi = pair // 16, pair % 16
    index = (pi // 4 - qi // 4 + 3) * 7 + pi % 4 - qi % 4 + 3
    table = lax.dot_general(
        cells[...], (index == entry).astype(F32), TN,
        precision=lax.Precision.HIGHEST, preferred_element_type=F32,
    )
    ar[4] = table[0:16]
    progress()
    small = [
        remote(ar, arr.at[0], asems.at[0], aremr.at[0], me.over_core),
        remote(ar, arr.at[1], asems.at[1], aremr.at[1], me.over_x),
        remote(ar, arr.at[2], asems.at[2], aremr.at[2], me.over_y),
    ]
    small[0].start()
    load_m.wait()

    def finish(half):
        for b in range(half * 4, half * 4 + 4):
            for k in range(4):
                ls = slice(k * 128, k * 128 + 128)
                ig_ref[b, 16:256, ls] = (mg[b, 16:256, ls] + bs[k, b * 256 : b * 256 + 240, :]).astype(BF)

    finish(0)
    small[0].wait()
    ar[...] = ar[...] + arr[0]
    small[1].start()
    progress()
    finish(1)
    small[1].wait()
    ar[...] = ar[...] + arr[1]
    small[2].start()
    progress()
    rh.wait()
    for b in range(8):
        ig_ref[b, 0:16, :] = (mg[b, 0:16, :] + rhalo[b].astype(F32)).astype(BF)
    small[2].wait()
    ar[...] = ar[...] + arr[2]
    last = []
    for d in range(3):
        to = (z + 1 + d) % 4
        last.append(remote(ar.at[to], arz.at[z, 0], asems.at[3 + d], aremr.at[3 + d], me.along_z[d]))
        last.append(remote(ar.at[4], arz.at[z, 1], asems.at[6 + d], aremr.at[6 + d], me.along_z[d]))
    for cp in last:
        cp.start()
    arz[z, 0] = ar[z]
    arz[z, 1] = ar[4]
    while plan:
        progress()
    for cp in last:
        cp.wait()
    total = (arz[0] + arz[1]) + (arz[2] + arz[3])
    mine = pltpu.roll(total[0], (8 - me.rank8) * 16 % 128, 1)
    ar[0] = total[0]
    fb = ar[0, pl.ds(8 + x * 2 + c, 1), :]
    vec_ref[0:8, :] = mine[0:8]
    vec_ref[8:9, :] = jnp.where(y == 0, fb, pltpu.roll(fb, 64, 1))
    vec_ref[9:16, :] = jnp.zeros((7, 128), F32)
    vec_ref[16:32, :] = total[1]
    bh.wait_send()
    sca.close()


def wq_gain(wq):
    parts = []
    for zz in range(4):
        total = jnp.sum(wq[zz, :, :, :, :, 0:128].astype(F32).reshape(8, 16, 128), axis=0)
        parts.append(total.T[:, 0:1])
    return jnp.concatenate(parts, 0)


def k3_call(br, mg, g1, g2, small, wqb, wp, qs, asv, ctxt, normt, nt, rs):
    S = jax.ShapeDtypeStruct
    V = pltpu.VMEM
    lead = (4, 2, 2, 2)
    half = (4, 2, 2)
    outs = [S((8, 256, 512), BF), S((16, 1536), F32), S((16, 512), F32), S((16, 2048), F32), S((64, 512), F32)]
    outs += [S((32, 128), F32)]

    def four(shape):
        return [V(shape + (64, 256), BF)] * 2 + [V(shape + (16, 1024), BF)] * 2

    fours = [four(half), four(half), four((4, 2)), four((4,)), four((3,))]
    rest = []
    for count, n in ((2, 256), (4, 384)):
        for shape in (half, half, (4, 2), (4,), (3,)):
            rest.append(V((count,) + shape + (16, n), BF))
    scratch = [
        V((4, 2048, 128), F32), V((2048, 512), BF), V((8, 256, 512), F32), V(lead + (16, 1664), BF),
        V((512, 512), BF), V((6144, 128), BF), V((6144, 128), F32), V((6144, 128), F32),
        V((2048, 128), F32), V((4096, 128), F32), V((1536, 2048), BF), V((512, 2048), BF),
        V((512, 2048), BF), V((512, 2048), BF), V((256, 128), F32), V((256, 128), F32),
        V((2, 512, 128), F32), V(lead + (16, 512), BF), V((4,) + lead + (16, 384), BF),
        V((8, 16, 512), BF), V((8, 16, 512), BF), V((8, 16, 512), BF), V((256, 128), F32),
        V((5, 16, 128), F32), V((3, 5, 16, 128), F32), V((4, 2, 16, 128), F32),
    ]
    sems = [
        pltpu.SemaphoreType.DMA((10, 6)), pltpu.SemaphoreType.DMA((10, 6)),
        pltpu.SemaphoreType.DMA((2,)), pltpu.SemaphoreType.DMA((2,)), pltpu.SemaphoreType.DMA((14,)),
        pltpu.SemaphoreType.DMA((9,)), pltpu.SemaphoreType.DMA((9,)),
    ]

    def body(*refs):
        n = 13 + len(outs) + len(scratch)
        flat = refs[n : n + 20]
        groups = [flat[i * 4 : i * 4 + 4] for i in range(5)]
        k3_body(*refs[:n], *groups, *refs[n + 20 :])

    return pl.pallas_call(
        body,
        out_shape=outs,
        in_specs=[VM, HB, HB, HB, VM, HB, HB, HB, HB, HB, HB, HB, VM],
        out_specs=[VM] * len(outs),
        scratch_shapes=scratch + sum(fours, []) + rest + sems,
        compiler_params=pltpu.CompilerParams(
            collective_id=2, has_side_effects=True, vmem_limit_bytes=62 << 20
        ),
        name="attend_back_scatter",
    )(br, mg, g1, g2, small, wqb, wp, qs, asv, ctxt, normt, nt, rs)


def k4_body(ig, gq, gp, g1, g2, vec, ig_o, gq_o, gp_o, g1_o, g2_o, *small):
    for a, b in ((gq, gq_o), (gp, gp_o), (g1, g1_o), (g2, g2_o)):
        b[...] = a[...]
    for b in range(8):
        ig_o[b] = ig[b]
    for k in range(8):
        small[k][...] = vec[k : k + 1, 0:16]
    small[8][...] = vec[8:9, 0:64]
    small[9][...] = vec[16:32, 0:TABLE]


def k4_call(ig, gq, gp, g1, g2, vec):
    S = jax.ShapeDtypeStruct
    outs = [S(a.shape, a.dtype) for a in (ig, gq, gp, g1, g2)]
    outs += [S((1, 16), F32)] * 8 + [S((1, 64), F32), S((16, TABLE), F32)]
    return pl.pallas_call(
        k4_body,
        out_shape=outs,
        in_specs=[VM] * 6,
        out_specs=[VM] * len(outs),
        compiler_params=pltpu.CompilerParams(vmem_limit_bytes=60 << 20),
        name="hand_over",
    )(ig, gq, gp, g1, g2, vec)


HEADS = 16
HEAD_DIM = 32
WIN = 4
SHIFT = 2
TABLE = 49


epsilon = 1e-06
highest = lax.Precision.HIGHEST


def from_behind(block, axis, distance):
    devices = range(lax.axis_size(axis))
    route = [((i - distance) % len(devices), i) for i in devices]
    return lax.ppermute(block, axis, route)


def normalize(values, gain_row, bias_row):
    average = jnp.mean(values, -1, keepdims=True)
    centred = values - average
    variance = jnp.mean(centred * centred, -1, keepdims=True)
    return centred * lax.rsqrt(variance + epsilon) * gain_row + bias_row


def exact_gelu(values):
    return jax.nn.gelu(values, approximate=False)


def table_onehot():
    positions = jnp.arange(WIN * WIN)
    row_of = positions // WIN
    column_of = positions % WIN
    table_index = (
        (row_of[:, None] - row_of[None, :] + WIN - 1) * (2 * WIN - 1)
        + column_of[:, None]
        - column_of[None, :]
        + WIN
        - 1
    )
    return (table_index.reshape(-1)[:, None] == jnp.arange(TABLE)[None, :]).astype(jnp.float32)


def to_windows(field_grid):
    clip_count, row_count, column_count, feature_width = field_grid.shape
    blocks = field_grid.reshape(
        clip_count, row_count // WIN, WIN, column_count // WIN, WIN, feature_width
    )
    return blocks.transpose(0, 1, 3, 2, 4, 5).reshape(-1, WIN * WIN, feature_width)


def from_windows(windows, clip_count, row_count, column_count):
    feature_width = windows.shape[-1]
    blocks = windows.reshape(
        clip_count, row_count // WIN, column_count // WIN, WIN, WIN, feature_width
    )
    return blocks.transpose(0, 1, 3, 2, 4, 5).reshape(
        clip_count, row_count, column_count, feature_width
    )


def times_transposed(left, right):
    return lax.dot_general(
        left, right, (((1,), (1,)), ((), ())), preferred_element_type=jnp.float32
    )


def outer_sum(left, right):
    return lax.dot_general(
        left, right, (((0,), (0,)), ((), ())), preferred_element_type=jnp.float32
    )


def per_device(
    inputs,
    grad_mask,
    cotangent,
    ln1_gain,
    ln1_bias,
    w_qkv,
    q_bias,
    v_bias,
    w_proj,
    proj_bias,
    ln2_gain,
    ln2_bias,
    w_fc1,
    fc1_bias,
    w_fc2,
    fc2_bias,
    pos_table,
):
    (
        gain_one,
        bias_one,
        qkv_full,
        qbias_full,
        vbias_full,
        proj_full,
        pbias_full,
        gain_two,
        bias_two,
        fc1_full,
        fc1b_full,
        fc2_full,
        fc2b_full,
    ) = (
        lax.all_gather(ln1_gain, ("clip", "slab"), axis=0, tiled=True),
        lax.all_gather(ln1_bias, ("clip", "slab"), axis=0, tiled=True),
        lax.all_gather(w_qkv, ("clip", "slab"), axis=0, tiled=True),
        lax.all_gather(q_bias, ("clip", "slab"), axis=0, tiled=True),
        lax.all_gather(v_bias, ("clip", "slab"), axis=0, tiled=True),
        lax.all_gather(w_proj, ("clip", "slab"), axis=0, tiled=True),
        lax.all_gather(proj_bias, ("clip", "slab"), axis=0, tiled=True),
        lax.all_gather(ln2_gain, ("clip", "slab"), axis=0, tiled=True),
        lax.all_gather(ln2_bias, ("clip", "slab"), axis=0, tiled=True),
        lax.all_gather(w_fc1, ("clip", "slab"), axis=0, tiled=True),
        lax.all_gather(fc1_bias, ("clip", "slab"), axis=0, tiled=True),
        lax.all_gather(w_fc2, ("clip", "slab"), axis=0, tiled=True),
        lax.all_gather(fc2_bias, ("clip", "slab"), axis=0, tiled=True),
    )
    clip_count, row_count, column_count, feature_width = inputs.shape
    score_scale = 1.0 / math.sqrt(HEAD_DIM)
    float_type = jnp.float32
    half_type = jnp.bfloat16
    ahead = from_behind(inputs[:, :SHIFT], "slab", -1)
    window_rows = jnp.concatenate([inputs[:, SHIFT:], ahead], axis=1).astype(float_type)
    normed, first_pull = jax.vjp(
        normalize, window_rows, gain_one.astype(float_type), bias_one.astype(float_type)
    )
    windows = to_windows(jnp.roll(normed.astype(half_type), -SHIFT, axis=2))
    window_count = windows.shape[0]
    token_count = window_count * WIN * WIN
    head_shape = (window_count, WIN * WIN, HEADS, HEAD_DIM)
    flat_windows = windows.reshape(token_count, feature_width)
    projected = jnp.dot(flat_windows, qkv_full, preferred_element_type=float_type)
    query_heads = (
        (projected[:, :feature_width] + qbias_full.astype(float_type))
        .astype(half_type)
        .reshape(head_shape)
    )
    key_heads = (
        projected[:, feature_width : 2 * feature_width].astype(half_type).reshape(head_shape)
    )
    value_heads = (
        (projected[:, 2 * feature_width :] + vbias_full.astype(float_type))
        .astype(half_type)
        .reshape(head_shape)
    )
    onehot = table_onehot()
    position_bias = (
        jnp.dot(onehot, pos_table, precision=highest)
        .reshape(WIN * WIN, WIN * WIN, HEADS)
        .transpose(2, 0, 1)
    )
    scores = (
        jnp.einsum("wqhc,wkhc->whqk", query_heads, key_heads, preferred_element_type=float_type)
        * score_scale
        + position_bias[None]
    )
    attention = jax.nn.softmax(scores, axis=-1)
    attention_low = attention.astype(half_type)
    context = jnp.einsum(
        "whqk,wkhc->wqhc", attention_low, value_heads, preferred_element_type=float_type
    )
    context = context.astype(half_type).reshape(window_count, WIN * WIN, feature_width)
    context_grid = jnp.roll(
        from_windows(context, clip_count, row_count, column_count), SHIFT, axis=2
    )
    returned = from_behind(context_grid[:, row_count - SHIFT :], "slab", 1)
    own_flat = jnp.concatenate([returned, context_grid[:, : row_count - SHIFT]], axis=1).reshape(
        -1, feature_width
    )
    input_flat = inputs.reshape(-1, feature_width).astype(float_type)
    middle = (
        input_flat
        + jnp.dot(own_flat, proj_full, preferred_element_type=float_type)
        + pbias_full.astype(float_type)
    )
    second, second_pull = jax.vjp(
        normalize, middle, gain_two.astype(float_type), bias_two.astype(float_type)
    )
    second_low = second.astype(half_type)
    pre_act = jnp.dot(second_low, fc1_full, preferred_element_type=float_type) + fc1b_full.astype(
        float_type
    )
    hidden, gelu_pull = jax.vjp(exact_gelu, pre_act)
    hidden_low = hidden.astype(half_type)
    output = (
        middle
        + jnp.dot(hidden_low, fc2_full, preferred_element_type=float_type)
        + fc2b_full.astype(float_type)
    )
    incoming = (cotangent.astype(float_type) * grad_mask.astype(float_type)[..., None]).reshape(
        -1, feature_width
    )
    incoming_low = incoming.astype(half_type)
    fc2_grad = outer_sum(hidden_low, incoming_low)
    fc2b_grad = jnp.sum(incoming, axis=0)
    hidden_grad = times_transposed(incoming_low, fc2_full)
    pre_grad = gelu_pull(hidden_grad)[0].astype(half_type)
    fc1_grad = outer_sum(second_low, pre_grad)
    fc1b_grad = jnp.sum(pre_grad.astype(float_type), axis=0)
    second_grad = times_transposed(pre_grad, fc1_full)
    middle_part, gain_two_grad, bias_two_grad = second_pull(second_grad)
    middle_grad = incoming + middle_part
    branch_low = middle_grad.astype(half_type)
    proj_grad = outer_sum(own_flat, branch_low)
    pbias_grad = jnp.sum(branch_low.astype(float_type), axis=0)
    context_grad = (
        times_transposed(branch_low, proj_full)
        .astype(half_type)
        .reshape(clip_count, row_count, column_count, feature_width)
    )
    sent_back = from_behind(context_grad[:, :SHIFT], "slab", -1)
    window_context_grad = jnp.concatenate([context_grad[:, SHIFT:], sent_back], axis=1)
    context_heads = to_windows(jnp.roll(window_context_grad, -SHIFT, axis=2)).reshape(head_shape)
    value_grad = jnp.einsum(
        "whqk,wqhc->wkhc", attention_low, context_heads, preferred_element_type=float_type
    ).astype(half_type)
    attention_grad = jnp.einsum(
        "wqhc,wkhc->whqk", context_heads, value_heads, preferred_element_type=float_type
    )
    score_grad = (
        attention * (attention_grad - jnp.sum(attention_grad * attention, -1, keepdims=True))
    ).astype(half_type)
    bias_cells = (
        jnp.sum(score_grad.astype(float_type), axis=0)
        .transpose(1, 2, 0)
        .reshape(WIN * WIN * WIN * WIN, HEADS)
    )
    table_grad = lax.dot_general(onehot, bias_cells, (((0,), (0,)), ((), ())), precision=highest)
    query_grad = (
        jnp.einsum("whqk,wkhc->wqhc", score_grad, key_heads, preferred_element_type=float_type)
        * score_scale
    ).astype(half_type)
    key_grad = (
        jnp.einsum("whqk,wqhc->wkhc", score_grad, query_heads, preferred_element_type=float_type)
        * score_scale
    ).astype(half_type)
    query_flat = query_grad.reshape(token_count, feature_width)
    value_flat = value_grad.reshape(token_count, feature_width)
    qkv_grad_low = jnp.concatenate(
        [query_flat, key_grad.reshape(token_count, feature_width), value_flat], axis=1
    )
    qkv_grad = outer_sum(flat_windows, qkv_grad_low)
    qbias_grad = jnp.sum(query_flat.astype(float_type), axis=0)
    vbias_grad = jnp.sum(value_flat.astype(float_type), axis=0)
    normed_grad = times_transposed(qkv_grad_low, qkv_full).reshape(
        window_count, WIN * WIN, feature_width
    )
    normed_grid_grad = jnp.roll(
        from_windows(normed_grad, clip_count, row_count, column_count), SHIFT, axis=2
    )
    rows_part, gain_one_grad, bias_one_grad = first_pull(normed_grid_grad)
    halo_back = from_behind(
        rows_part[:, row_count - SHIFT :].astype(jnp.bfloat16), "slab", 1
    ).astype(jnp.float32)
    input_grad = middle_grad.reshape(
        clip_count, row_count, column_count, feature_width
    ) + jnp.concatenate([halo_back, rows_part[:, : row_count - SHIFT]], axis=1)
    shares = (
        lax.psum_scatter(gain_one_grad, ("clip", "slab"), scatter_dimension=0, tiled=True),
        lax.psum_scatter(bias_one_grad, ("clip", "slab"), scatter_dimension=0, tiled=True),
        lax.psum_scatter(qkv_grad, ("clip", "slab"), scatter_dimension=0, tiled=True),
        lax.psum_scatter(qbias_grad, ("clip", "slab"), scatter_dimension=0, tiled=True),
        lax.psum_scatter(vbias_grad, ("clip", "slab"), scatter_dimension=0, tiled=True),
        lax.psum_scatter(proj_grad, ("clip", "slab"), scatter_dimension=0, tiled=True),
        lax.psum_scatter(pbias_grad, ("clip", "slab"), scatter_dimension=0, tiled=True),
        lax.psum_scatter(gain_two_grad, ("clip", "slab"), scatter_dimension=0, tiled=True),
        lax.psum_scatter(bias_two_grad, ("clip", "slab"), scatter_dimension=0, tiled=True),
        lax.psum_scatter(fc1_grad, ("clip", "slab"), scatter_dimension=0, tiled=True),
        lax.psum_scatter(fc1b_grad, ("clip", "slab"), scatter_dimension=0, tiled=True),
        lax.psum_scatter(fc2_grad, ("clip", "slab"), scatter_dimension=0, tiled=True),
        lax.psum_scatter(fc2b_grad, ("clip", "slab"), scatter_dimension=0, tiled=True),
    )
    table_total = lax.psum(table_grad, ("clip", "slab"))
    output = output.reshape(clip_count, row_count, column_count, feature_width).astype(half_type)
    return (
        output,
        input_grad.astype(half_type),
        shares[0],
        shares[1],
        shares[2],
        shares[3],
        shares[4],
        shares[5],
        shares[6],
        shares[7],
        shares[8],
        shares[9],
        shares[10],
        shares[11],
        shares[12],
        table_total,
    )


def per_device_fast(
    inputs,
    grad_mask,
    cotangent,
    ln1_gain,
    ln1_bias,
    w_qkv,
    q_bias,
    v_bias,
    w_proj,
    proj_bias,
    ln2_gain,
    ln2_bias,
    w_fc1,
    fc1_bias,
    w_fc2,
    fc2_bias,
    pos_table,
):
    smalls = [
        v.reshape(1, 16)
        for v in (ln1_gain, ln1_bias, q_bias, v_bias, proj_bias, ln2_gain, ln2_bias, fc2_bias)
    ]
    shape = inputs.shape
    x = inputs.reshape(8, 256, 512)
    ctx, wqb, wpb, w1b, w2b, par, qs, asv, ctxt, normt, nt, rs = k1_call(
        x, w_qkv, w_proj, w_fc1, w_fc2, smalls, fc1_bias.reshape(1, 64), pos_table.T
    )
    wp = wpb.reshape(512, 512)
    output, mg, br, g1, g2, small = k2_call(
        x.reshape(2048, 512), ctx.reshape(2048, 512), cotangent.reshape(2048, 512), grad_mask.transpose(0, 2, 1), par,
        wp, w1b.reshape(512, 2048), w2b.reshape(2048, 512)
    )
    lead = (4, 2, 2, 2)
    third = k3_call(
        br.reshape(8, 256, 512), mg.reshape(8, 256, 512), g1.reshape(lead + (16, 2048)),
        g2.reshape(lead + (64, 512)), small, wqb, wp, qs, asv, ctxt, normt, nt, rs
    )
    input_grad, gq, gp, gf1, gf2, *vectors, fb, table = k4_call(*third)
    v = [r.reshape(16) for r in vectors]
    return (
        output.reshape(shape), input_grad.reshape(shape), v[0], v[1], gq, v[2], v[3], gp, v[4], v[5],
        v[6], gf1, fb.reshape(64), gf2, v[7], table.T,
    )


def solution(mesh):
    in_specs = (
        P("clip", "slab", None, None),
        P("clip", "slab", None),
        P("clip", "slab", None, None),
        P(("clip", "slab")),
        P(("clip", "slab")),
        P(("clip", "slab"), None),
        P(("clip", "slab")),
        P(("clip", "slab")),
        P(("clip", "slab"), None),
        P(("clip", "slab")),
        P(("clip", "slab")),
        P(("clip", "slab")),
        P(("clip", "slab"), None),
        P(("clip", "slab")),
        P(("clip", "slab"), None),
        P(("clip", "slab")),
        P(),
    )
    out_specs = (
        P("clip", "slab", None, None),
        P("clip", "slab", None, None),
        P(("clip", "slab")),
        P(("clip", "slab")),
        P(("clip", "slab"), None),
        P(("clip", "slab")),
        P(("clip", "slab")),
        P(("clip", "slab"), None),
        P(("clip", "slab")),
        P(("clip", "slab")),
        P(("clip", "slab")),
        P(("clip", "slab"), None),
        P(("clip", "slab")),
        P(("clip", "slab"), None),
        P(("clip", "slab")),
        P(),
    )
    fits = mesh.shape["clip"] == 16 and mesh.shape["slab"] == 2
    return jax.shard_map(
        per_device_fast if fits else per_device, mesh=mesh, in_specs=in_specs, out_specs=out_specs, check_vma=False
    )
```

```python
import functools
import math

import jax
import jax.numpy as jnp
from jax import lax
from jax.experimental import pallas as pl
from jax.experimental.pallas import tpu as pltpu
from jax.sharding import PartitionSpec as P

F32 = jnp.float32
BF = jnp.bfloat16
MESH = pl.DeviceIdType.MESH
SCALE = 1.0 / math.sqrt(32.0)
NT = (((1,), (1,)), ((), ()))
TN = (((0,), (0,)), ((), ()))
VM = pl.BlockSpec(memory_space=pltpu.VMEM)
HB = pl.BlockSpec(memory_space=pl.ANY)
UNROLL = 16
TABLE = 49


def dot(a, b, dims=(((1,), (0,)), ((), ()))):
    return lax.dot_general(a, b, dims, preferred_element_type=F32)


def tree(xs, op=lambda a, b: a + b):
    xs = list(xs)
    while len(xs) > 1:
        xs = [op(xs[i], xs[i + 1]) if i + 1 < len(xs) else xs[i] for i in range(0, len(xs), 2)]
    return xs[0]


def tile(ref, i):
    return ref[pl.ds(pl.multiple_of(i * 16, 16), 16), :]


def row(ref, i):
    return jnp.broadcast_to(ref[pl.ds(i, 1), :], (16, 128))


def pair_products(a_ref, a0, b_ref, b0):
    def body(d, acc):
        ad = tile(a_ref, a0 + d)
        return tuple(acc[q] + ad * row(b_ref, (b0 + d) * 16 + q) for q in range(16))

    return lax.fori_loop(
        0, 32, body, tuple(jnp.zeros((16, 128), F32) for _ in range(16)), unroll=UNROLL
    )


def weighted(ws, b_ref, b0, o_ref, o0, scale):
    def body(d, carry):
        parts = []
        for k in range(4):
            t = ws[4 * k] * row(b_ref, (b0 + d) * 16 + 4 * k)
            for q in range(4 * k + 1, 4 * k + 4):
                t = t + ws[q] * row(b_ref, (b0 + d) * 16 + q)
            parts.append(t)
        s = (parts[0] + parts[1]) + (parts[2] + parts[3])
        if scale is not None:
            s = s * scale
        o_ref[pl.ds(pl.multiple_of((o0 + d) * 16, 16), 16), :] = s.astype(BF).astype(F32)
        return carry

    lax.fori_loop(0, 32, body, 0, unroll=UNROLL)


class Place:
    def __init__(self):
        self.clip = lax.axis_index("clip")
        self.y = lax.axis_index("slab")
        self.c = self.clip % 2
        self.x = (self.clip // 2) % 2
        self.z = self.clip // 4
        self.rank8 = self.x * 4 + self.c * 2 + self.y
        base = self.x * 2 + self.c
        self.along_z = [(((self.z + d) % 4) * 4 + base, self.y) for d in (1, 2, 3)]
        self.over_x = (self.clip + 2 - 4 * self.x, self.y)
        self.over_y = (self.clip, 1 - self.y)
        self.over_core = (self.clip + 1 - 2 * self.c, self.y)

    def greet(self):
        barrier = pltpu.get_barrier_semaphore()
        others = self.along_z + [self.over_x, self.over_y, self.over_core]
        for other in others:
            pl.semaphore_signal(barrier, inc=1, device_id=other, device_id_type=MESH)

    def met(self):
        pl.semaphore_wait(pltpu.get_barrier_semaphore(), 6)


def remote(src, dst, ssem, rsem, to):
    return pltpu.make_async_remote_copy(
        src_ref=src, dst_ref=dst, send_sem=ssem, recv_sem=rsem, device_id=to, device_id_type=MESH
    )


class Gather:
    def __init__(self, place, pieces, ssem, rsem):
        self.copies = []
        z, x, c, y = place.z, place.x, place.c, place.y
        for k, (buf, c0, n, first_x, first) in enumerate(pieces):
            cols = pl.ds(c0, n)

            def cp(ix, s, to, k=k, buf=buf, cols=cols):
                ref = buf.at[ix + (slice(None), cols)]
                return remote(ref, ref, ssem.at[k, s], rsem.at[k, s], to)

            al = slice(None)
            mine = buf.at[z, x, c, y, :, cols]
            steps = [
                [
                    remote(
                        mine if first is None else first.at[:, cols],
                        mine,
                        ssem.at[k, d],
                        rsem.at[k, d],
                        place.along_z[d],
                    )
                    for d in range(3)
                ]
            ]
            if first_x:
                steps.append([cp((al, x, c, y), 3, place.over_x)])
                steps.append([cp((al, al, c, y), 4, place.over_y)])
            else:
                steps.append([cp((al, x, c, y), 3, place.over_y)])
                steps.append([cp((al, x, c, al), 4, place.over_x)])
            steps.append([cp((al, al, c, al), 5, place.over_core)])
            self.copies.append(steps)

    def start(self, k, s):
        for copy in self.copies[k][s]:
            copy.start()

    def advance(self, k, s):
        for copy in self.copies[k][s]:
            copy.wait_recv()
        if s < 3:
            self.start(k, s + 1)

    def close(self):
        for steps in self.copies:
            for step in steps:
                for copy in step:
                    copy.wait_send()


CH = 512
FJ = 512


def gelu_parts(a):
    z = jnp.abs(a) * 0.7071067811865476
    t = 1.0 / (1.0 + 0.3275911 * z)
    e = jnp.exp(a * a * -0.5)
    p = 0.5307027145 * t - 0.7265760135
    p = p * t + 0.7107068705
    p = p * t - 0.142248368
    p = p * t + 0.127414796
    tail = p * t * e
    return jnp.where(a >= 0, 1.0 - tail, tail), e * 0.3989422804014327


CH = 512
FJ = 512


PLAN_GATHER = (((0, 0), (1, 0)), (), ((2, 0),), (), ((3, 0),), ((0, 1), (1, 1)), ((4, 0),), ((2, 1), (5, 0)), ((6, 0),), ((3, 1), (1, 2), (0, 2), (1, 3), (0, 3)), ((4, 1), (7, 0)), ((6, 1),), ((2, 2),), (), ((2, 3), (3, 2), (5, 1)), ((8, 0),), ((3, 3), (4, 2)), (), ((4, 3), (5, 2), (9, 0)), (), ((5, 3), (7, 1)), (), ((6, 2), (8, 1), (10, 0)), (), ((6, 3),), (), ((9, 1),), (), (), (), ((7, 2),), (), (), ((7, 3),), ((8, 2),), ((10, 1),), ((8, 3),), (), (), (), (), (), ((9, 2),), ((10, 2),), ((9, 3),), ((10, 3),), ())


def spots(p):
    i, j = p // 4, p % 4
    return (i * 8 + (j + 2) % 8, i * 8 + (j + 6) % 8)


def gathered(ref, lo, hi):
    return jnp.concatenate([ref[pl.ds(lo, 64, stride=32), :], ref[pl.ds(hi, 64, stride=32), :]], axis=0)


def position_bias(tab_ref, bt_ref):
    for p in range(0, 16, 4):
        entry = lax.broadcasted_iota(jnp.int32, (TABLE, 512), 0)
        lane = lax.broadcasted_iota(jnp.int32, (TABLE, 512), 1)
        pi = lane // 128 + p
        qi = lane % 128
        index = (pi // 4 - qi // 4 + 3) * 7 + pi % 4 - qi % 4 + 3
        one = ((index == entry) & (qi < 16)).astype(F32)
        res = jnp.dot(
            tab_ref[...], one, precision=lax.Precision.HIGHEST, preferred_element_type=F32
        )
        for k in range(4):
            bt_ref[pl.ds(p + k, 16, stride=16), :] = res[:, k * 128 : (k + 1) * 128]


def small_block(place, small_refs, fc1b_ref, scr):
    scr[...] = jnp.zeros_like(scr)
    for k, ref in enumerate(small_refs):
        scr[k : k + 1, 0:16] = ref[...].astype(F32)
    lane = lax.broadcasted_iota(jnp.int32, (128, 128), 1)
    src = lax.broadcasted_iota(jnp.int32, (128, 128), 0)
    sel = ((lane == place.rank8 * 16 + src) & (src < 16)).astype(F32).astype(BF)
    vectors = dot(scr[...].astype(BF), sel)
    scr[0:1, 0:64] = fc1b_ref[...].astype(F32)
    half = ((lane == place.y * 64 + src) & (src < 64)).astype(F32).astype(BF)
    wide = dot(scr[0:1, :].astype(BF), half)
    r = lax.broadcasted_iota(jnp.int32, (16, 128), 0)
    return jnp.where(
        r < 8,
        vectors,
        jnp.where(r == 8 + place.x * 2 + place.c, jnp.broadcast_to(wide, (16, 128)), 0.0),
    ).astype(BF)


def k1_body(
    x_h, cot_h, mask_ref, wq_ref, wp_ref, w1_ref, w2_ref, s0, s1, s2, s3, s4, s5, s6, s7, fb_ref, tab_ref,
    out_h, mg_h, br_h, bhalo_ref, g1_h, g2_h, small_ref,
    wqb_h, wp_h, qkv_save, att_save, ctxt_h, normt_h, nt_h, rs_ref,
    ctx_ref, wpb, w1b, w2b, par_ref, x_ref, xs, big, cs_ref, a_ref, qb, halo, chalo, gains, scr,
    wqb, ctxt_ref, normt_ref, nt_ref, bt_ref, cot, hid_ref, pg_ref, sec_ref, br,
    ssem, rsem, hss, hrs, lsem, osem, csem,
):
    g_ref = big.at[pl.ds(0, 6144), :]
    ct_ref = big.at[pl.ds(6144, 2048), :]
    me = Place()
    z, x, c, y = me.z, me.x, me.c, me.y
    own = [
        pltpu.make_async_copy(src, buf.at[z, x, c, y], osem.at[i])
        for i, (src, buf) in enumerate(((wp_ref, wpb), (w1_ref, w1b), (w2_ref, w2b)))
    ]
    for cp in own:
        cp.start()
    xload = pltpu.make_async_copy(x_h, x_ref, osem.at[3])
    xload.start()
    cload = pltpu.make_async_copy(cot_h, cot, osem.at[4])
    cload.start()
    me.greet()
    for g in range(4):
        for k in range(3):
            wqb[z, x, c, y, :, 128 + g * 384 + k * 128 : 256 + g * 384 + k * 128] = wq_ref[
                :, k * 512 + g * 128 : k * 512 + g * 128 + 128
            ]
    wqb[z, x, c, y, :, 0:128] = small_block(me, (s0, s1, s2, s3, s4, s5, s6, s7), fb_ref, scr)
    pieces = [(wqb, 0, 256, True, None), (wqb, 256, 256, False, None)]
    pieces += [(wqb, 128 + g * 384, 384, g % 2 == 1, None) for g in (1, 2, 3)]
    pieces += [(wpb, 0, 256, False, wp_ref), (wpb, 256, 256, True, wp_ref)]
    pieces += [(w1b, 0, 1024, False, w1_ref), (w1b, 1024, 1024, True, w1_ref)]
    pieces += [(w2b, 0, 256, False, w2_ref), (w2b, 256, 256, True, w2_ref)]
    gat = Gather(me, pieces, ssem, rsem)
    me.met()
    for k in range(5):
        gat.start(k, 0)
    xhalo = remote(x_h.at[:, 0:16, :], halo, hss.at[4], hrs.at[4], me.over_y)
    xhalo.start()
    plan = [list(part) for part in PLAN_GATHER]

    def progress():
        for k, s in plan.pop(0):
            gat.advance(k, s)

    xload.wait()
    for b in range(8):
        for k in range(4):
            xs[k, b * 256 : b * 256 + 240, :] = x_ref[b, 16:256, k * 128 : k * 128 + 128].astype(F32)
    for k in range(5, 11):
        gat.start(k, 0)
    for cp in own:
        cp.wait()

    def norm_block(p):
        lo, hi = spots(p)
        turned = jnp.concatenate([gathered(xs.at[k], lo, hi).T for k in range(4)], axis=0)
        mean = jnp.mean(turned, 0, keepdims=True)
        cen = turned - mean
        rs = lax.rsqrt(jnp.mean(cen * cen, 0, keepdims=True) + 1e-6)
        big[p * 512 : (p + 1) * 512, :] = cen * rs
        rs_ref[p : p + 1, :] = rs

    progress()
    for p in range(16):
        if p == 8:
            xhalo.wait_recv()
            for b in range(8):
                for k in range(4):
                    xs[k, b * 256 + 240 : b * 256 + 256, :] = halo[
                        b, :, k * 128 : k * 128 + 128
                    ].astype(F32)
        norm_block(p)
        if p % 2 == 1:
            progress()
        if p == 5:
            position_bias(tab_ref, bt_ref)
    progress()
    for zz in range(4):
        total = jnp.sum(wqb[zz, :, :, :, :, 0:128].astype(F32).reshape(8, 16, 128), axis=0)
        par_ref[0:8, zz * 128 : (zz + 1) * 128] = total[0:8]
        for k in range(4):
            par_ref[8 + zz : 9 + zz, k * 128 : (k + 1) * 128] = total[8 + k : 9 + k]
    par_ref[12:16, :] = jnp.zeros((4, 512), F32)
    turned = par_ref[...].T
    for k in range(4):
        gains[k] = jnp.broadcast_to(turned[:, k : k + 1], (512, 128))

    def finish_norm(p, carry):
        cols = pl.ds(pl.multiple_of(p * 128, 128), 128)
        n = big[pl.ds(pl.multiple_of(p * 512, 512), 512), :]
        normt_ref[:, cols] = (n * gains[0] + gains[1]).astype(BF)
        nt_ref[:, cols] = n.astype(BF)
        return carry

    for t in range(4):
        lax.fori_loop(t * 4, t * 4 + 4, finish_norm, 0)
        progress()

    outs = []
    sends = []

    def out(src, dst, i):
        cp = pltpu.make_async_copy(src, dst, lsem.at[i])
        cp.start()
        outs.append(cp)

    out(normt_ref, normt_h, 8)
    out(nt_ref, nt_h, 9)
    save = None
    for g in range(4):
        w = wqb[:, :, :, :, :, 128 + g * 384 : 512 + g * 384].reshape(512, 384)
        wt = w.astype(F32).T.astype(BF)
        fs = slice(g * 128, (g + 1) * 128)
        if save is not None:
            save.wait()
        for t in range(2):
            res = dot(wt, normt_ref[:, t * 1024 : t * 1024 + 1024])
            for k in range(8):
                block = res[:, k * 128 : (k + 1) * 128]
                block = jnp.concatenate(
                    [block[0:128] + gains[2, fs, :], block[128:256], block[256:384] + gains[3, fs, :]],
                    axis=0,
                )
                g_ref[pl.ds(t * 8 + k, 384, stride=16), :] = block.astype(BF).astype(F32)
            if t == 0:
                progress()

        def keep(i, carry):
            rows = pl.ds(pl.multiple_of(i * 512, 512), 512)
            qb[rows, :] = g_ref[rows, :].astype(BF)
            return carry

        lax.fori_loop(0, 12, keep, 0)
        save = pltpu.make_async_copy(qb, qkv_save.at[g], lsem.at[g])
        save.start()
        if g == 3:
            out(wqb, wqb_h, 10)
        progress()

        def head(h, carry, g=g):
            acc = pair_products(g_ref, h * 32, g_ref, 128 + h * 32)
            bt = tile(bt_ref, g * 4 + h)
            s = [
                acc[q] * SCALE + jnp.broadcast_to(bt[:, q : q + 1], (16, 128)) for q in range(16)
            ]
            m = tree(s, jnp.maximum)
            e = [jnp.exp(v - m) for v in s]
            inv = 1.0 / tree(e)
            low = []
            for q in range(16):
                a = e[q] * inv
                a_ref[pl.ds(pl.multiple_of((g * 4 + h) * 256 + q * 16, 16), 16), :] = a
                low.append(a.astype(BF).astype(F32))
            weighted(low, g_ref, 256 + h * 32, ct_ref, h * 32, None)
            return carry

        for h in range(4):
            lax.fori_loop(h, h + 1, head, 0)
            progress()
        out(a_ref.at[pl.ds(g * 1024, 1024), :], att_save.at[pl.ds(g * 1024, 1024), :], 4 + g)
        for p in range(16):
            block = ct_ref[pl.ds(p, 128, stride=16), :]
            ctxt_ref[fs, p * 128 : (p + 1) * 128] = block.astype(BF)
            turned = block.T
            lo, hi = spots(p)
            cs_ref[pl.ds(lo, 64, stride=32), :] = turned[0:64]
            cs_ref[pl.ds(hi, 64, stride=32), :] = turned[64:128]
        for b in range(8):
            ctx_ref[b, 16:256, fs] = cs_ref[b * 256 : b * 256 + 240, :].astype(BF)
            chalo[g, b] = cs_ref[b * 256 + 240 : b * 256 + 256, :].astype(BF)
        send = remote(chalo.at[g], ctx_ref.at[:, 0:16, pl.ds(g * 128, 128)], hss.at[g], hrs.at[g], me.over_y)
        send.start()
        sends.append(send)
        out(ctxt_ref.at[pl.ds(g * 128, 128), :], ctxt_h.at[pl.ds(g * 128, 128), :], 11 + g)
        progress()
    out(wpb, wp_h, 15)
    cload.wait()
    wp, w1, w2 = wpb.reshape(512, 512), w1b.reshape(512, 2048), w2b.reshape(2048, 512)
    pb, g2, b2, fb2 = (par_ref[k : k + 1, :] for k in (4, 5, 6, 7))
    small_ref[...] = jnp.zeros_like(small_ref)
    rsel = (
        lax.broadcasted_iota(jnp.int32, (256, 32), 0) // 8
        == lax.broadcasted_iota(jnp.int32, (256, 32), 1)
    ).astype(F32).astype(BF)
    csel = lax.broadcasted_iota(jnp.int32, (256, 8), 0) % 8 == lax.broadcasted_iota(
        jnp.int32, (256, 8), 1
    )

    def mask_clip(b, carry):
        rows = pl.ds(pl.multiple_of(b * 256, 256), 256)
        spread = dot(rsel, mask_ref[b].astype(F32).astype(BF), NT)
        mark = jnp.sum(jnp.where(csel, spread, 0.0), 1, keepdims=True)
        inc = cot[rows, :].astype(F32) * mark
        cot[rows, :] = inc.astype(BF)
        small_ref[7:8, :] += jnp.sum(inc, 0, keepdims=True)
        return carry

    lax.fori_loop(0, 8, mask_clip, 0)
    for cp in sends:
        cp.wait()

    def ahead(i, carry):
        rows = pl.ds(pl.multiple_of(i * CH, CH), CH)
        clips = pl.ds(i * (CH // 256), CH // 256)
        mid = (
            x_ref[clips].reshape(CH, 512).astype(F32) + dot(ctx_ref[clips].reshape(CH, 512), wp[...]) + pb
        )
        for k in range(4):
            xs[k, rows, :] = mid[:, k * 128 : k * 128 + 128]
        cen = mid - jnp.mean(mid, 1, keepdims=True)
        rs = lax.rsqrt(jnp.mean(cen * cen, 1, keepdims=True) + 1e-6)
        sec = (cen * rs * g2 + b2).astype(BF)
        sec_ref[rows, :] = sec
        for j in range(2048 // FJ):
            cols = slice(j * FJ, (j + 1) * FJ)
            pre = dot(sec, w1[:, cols]) + par_ref[8 + j : 9 + j, :]
            cdf, pdf = gelu_parts(pre)
            hid_ref[rows, cols] = (pre * cdf).astype(BF)
            pg_ref[rows, cols] = (cdf + pre * pdf).astype(BF)
        return carry

    for i in range(2048 // CH):
        lax.fori_loop(i, i + 1, ahead, 0)
        progress()
    while plan:
        progress()

    def back_again(i, carry):
        rows = pl.ds(pl.multiple_of(i * CH, CH), CH)
        clips = pl.ds(i * (CH // 256), CH // 256)
        mid = jnp.concatenate([xs[k, rows, :] for k in range(4)], axis=1)
        cen = mid - jnp.mean(mid, 1, keepdims=True)
        rs = lax.rsqrt(jnp.mean(cen * cen, 1, keepdims=True) + 1e-6)
        n2 = cen * rs
        low = cot[rows, :]
        back = None
        for j in range(2048 // FJ):
            cols = slice(j * FJ, (j + 1) * FJ)
            hg = dot(low, w2[cols, :], NT)
            pg = (hg * pg_ref[rows, cols].astype(F32)).astype(BF)
            pg_ref[rows, cols] = pg
            small_ref[8 + j : 9 + j, :] += jnp.sum(pg.astype(F32), 0, keepdims=True)
            s = dot(pg, w1[:, cols], NT)
            back = s if back is None else back + s
        ctx_ref[clips] = (mid + dot(hid_ref[rows, :], w2[...]) + fb2).astype(BF).reshape(
            CH // 256, 256, 512
        )
        pltpu.make_async_copy(ctx_ref.at[clips], out_h.at[clips], csem.at[0, i]).start()
        small_ref[5:6, :] += jnp.sum(back * n2, 0, keepdims=True)
        small_ref[6:7, :] += jnp.sum(back, 0, keepdims=True)
        eg = back * g2
        r = (eg - jnp.mean(eg, 1, keepdims=True) - n2 * jnp.mean(eg * n2, 1, keepdims=True)) * rs
        mg = low.astype(F32) + r
        for k in range(4):
            xs[k, rows, :] = mg[:, k * 128 : k * 128 + 128]
        pltpu.make_async_copy(xs.at[:, rows, :], mg_h.at[:, rows, :], csem.at[1, i]).start()
        low_mg = mg.astype(BF)
        br[clips] = low_mg.reshape(CH // 256, 256, 512)
        pltpu.make_async_copy(br.at[clips], br_h.at[clips], csem.at[2, i]).start()
        small_ref[4:5, :] += jnp.sum(low_mg.astype(F32), 0, keepdims=True)
        return carry

    lax.fori_loop(0, 2048 // CH, back_again, 0)
    bhalo = remote(br.at[:, 0:16, :], bhalo_ref, hss.at[5], hrs.at[5], me.over_y)
    bhalo.start()
    save.wait()
    for cp in outs:
        cp.wait()
    turned = sec_ref[...].astype(F32).T.astype(BF)
    for j in range(8):
        cols = slice(j * 256, j * 256 + 256)
        normt_ref[:, cols] = dot(turned, pg_ref[:, cols]).astype(BF)
    last = [pltpu.make_async_copy(normt_ref, g1_h, csem.at[3, 0])]
    last[0].start()
    turned = cot[...].astype(F32).T.astype(BF)
    for j in range(8):
        cols = slice(j * 256, j * 256 + 256)
        x_ref[j] = dot(turned, hid_ref[:, cols]).T.astype(BF)
    last.append(pltpu.make_async_copy(x_ref, g2_h, csem.at[3, 1]))
    last[1].start()
    for i in range(2048 // CH):
        rows = pl.ds(i * CH, CH)
        clips = pl.ds(i * (CH // 256), CH // 256)
        pltpu.make_async_copy(ctx_ref.at[clips], out_h.at[clips], csem.at[0, i]).wait()
        pltpu.make_async_copy(xs.at[:, rows, :], mg_h.at[:, rows, :], csem.at[1, i]).wait()
        pltpu.make_async_copy(br.at[clips], br_h.at[clips], csem.at[2, i]).wait()
    for cp in last:
        cp.wait()
    bhalo.wait()
    xhalo.wait_send()
    gat.close()


def k1_call(x, cot, mask, wq, wp, w1, w2, smalls, fb, tab):
    S = jax.ShapeDtypeStruct
    lead = (4, 2, 2, 2)
    outs = [
        (S((8, 256, 512), BF), HB),
        (S((4, 2048, 128), F32), HB),
        (S((8, 256, 512), BF), HB),
        (S((8, 16, 512), BF), VM),
        (S((512, 2048), BF), HB),
        (S((8, 256, 512), BF), HB),
        (S((16, 512), F32), VM),
        (S(lead + (16, 1664), BF), HB),
        (S(lead + (16, 512), BF), HB),
        (S((4, 6144, 128), BF), HB),
        (S((4096, 128), F32), HB),
        (S((512, 2048), BF), HB),
        (S((512, 2048), BF), HB),
        (S((512, 2048), BF), HB),
        (S((16, 128), F32), VM),
    ]
    V = pltpu.VMEM
    D = pltpu.SemaphoreType.DMA
    return pl.pallas_call(
        k1_body,
        out_shape=[o[0] for o in outs],
        in_specs=[HB, HB] + [VM] * 15,
        out_specs=[o[1] for o in outs],
        scratch_shapes=[
            V((8, 256, 512), BF), V(lead + (16, 512), BF), V(lead + (16, 2048), BF),
            V(lead + (64, 512), BF), V((16, 512), F32),
            V((8, 256, 512), BF), V((4, 2048, 128), F32), V((8192, 128), F32),
            V((2048, 128), F32), V((4096, 128), F32), V((6144, 128), BF),
            V((8, 16, 512), BF), V((4, 8, 16, 128), BF), V((4, 512, 128), F32), V((16, 128), F32),
            V(lead + (16, 1664), BF), V((512, 2048), BF), V((512, 2048), BF), V((512, 2048), BF), V((256, 128), F32),
            V((2048, 512), BF), V((2048, 2048), BF), V((2048, 2048), BF), V((2048, 512), BF), V((8, 256, 512), BF),
            D((11, 6)), D((11, 6)), D((6,)), D((6,)), D((16,)), D((5,)), D((4, 4)),
        ],
        compiler_params=pltpu.CompilerParams(
            collective_id=1, has_side_effects=True, vmem_limit_bytes=62 << 20
        ),
        name="gather_attend_feed",
    )(x, cot, mask, wq, wp, w1, w2, *smalls, fb, tab)
PLAN_SCATTER = (((0, 0), (1, 0), (2, 0)), ((3, 0),), (), ((4, 0), (5, 0)), (), (), ((0, 1), (1, 1)), (), (), ((2, 1), (3, 1), (6, 0)), ((4, 1), (5, 1)), (), ((0, 2), (1, 2)), (), ((2, 2), (3, 2)), ((4, 2), (6, 1), (7, 0)), ((0, 3), (5, 2)), ((1, 3), (6, 2)), (), ((2, 3), (7, 1)), (), ((3, 3), (8, 0)), ((4, 3), (5, 3), (7, 2)), ((6, 3),), ((7, 3), (8, 1)), (), ((8, 2), (9, 0)), (), ((8, 3), (9, 1)), (), ((9, 2),), (), (), ((9, 3),))


class Scatter:
    def __init__(self, place, pieces, ssem, rsem):
        self.me = place
        self.pieces = pieces
        self.steps = []
        z, x, c, y = place.z, place.x, place.c, place.y
        al = slice(None)
        for k, (src, c0, n, first_y, own, s, r1, r2, r3, r4, done) in enumerate(pieces):
            cols = pl.ds(c0, n)

            def cp(a, b, i, to, k=k):
                return remote(a, b, ssem.at[k, i], rsem.at[k, i], to)

            steps = [[cp(src.at[:, :, 1 - c, :, :, cols], r1, 0, place.over_core)]]
            if first_y:
                steps.append([cp(s.at[:, :, 1 - y], r2, 1, place.over_y)])
                steps.append([cp(s.at[:, 1 - x, y], r3, 2, place.over_x)])
            else:
                steps.append([cp(s.at[:, 1 - x], r2, 1, place.over_x)])
                steps.append([cp(s.at[:, x, 1 - y], r3, 2, place.over_y)])
            steps.append(
                [
                    cp(s.at[(z + 1 + d) % 4, x, y], r4.at[d], 3 + d, place.along_z[d])
                    for d in range(3)
                ]
            )
            self.steps.append(steps)

    def start(self, k, i):
        for copy in self.steps[k][i]:
            copy.start()

    def advance(self, k, i):
        me = self.me
        z, x, c, y = me.z, me.x, me.c, me.y
        src, c0, n, first_y, own, s, r1, r2, r3, r4, done = self.pieces[k]
        cols = pl.ds(c0, n)
        for copy in self.steps[k][i]:
            copy.wait_recv()
        if i == 0:
            if own is not None:
                own.wait()

            def add(zz, carry):
                held = s[zz] if own is not None else src[zz, :, c, :, :, cols]
                s[zz] = (held.astype(F32) + r1[zz].astype(F32)).astype(BF)
                return carry

            lax.fori_loop(0, 4, add, 0)
        elif i == 1 and first_y:
            s[:, :, y] = (s[:, :, y].astype(F32) + r2[...].astype(F32)).astype(BF)
        elif i == 1:
            s[:, x] = (s[:, x].astype(F32) + r2[...].astype(F32)).astype(BF)
        elif i == 2:
            s[:, x, y] = (s[:, x, y].astype(F32) + r3[...].astype(F32)).astype(BF)
        else:
            done(tree([s[z, x, y].astype(F32)] + [r4[d].astype(F32) for d in range(3)]))
        if i < 3:
            self.start(k, i + 1)

    def close(self):
        for steps in self.steps:
            for step in steps:
                for copy in step:
                    copy.wait_send()


def k3_body(
    br_ref, bhalo, mg_h, g1_ref, g2_ref, small_ref, wqb_h, wp_h, qkv_save, att_save, ctxt_h, normt_h, nt_h, rs_ref,
    ig_ref, gq_ref, gp_ref, gf1_ref, gf2_ref, vec_ref,
    bs, bp, mg, wq, wp, qb, g_ref, dg, dc, a_ref, dqt, ctxt, normt, nt, ds_ref, low_ref,
    gacc, pgrad, qgrad, rhalo, rout, cells, ar, arr, arz,
    s4, r14, r24, r34, r44, sp, r1p, r2p, r3p, r4p, sq, r1q, r2q, r3q, r4q,
    ssem, rsem, hss, hrs, lsem, asems, aremr,
):
    me = Place()
    z, x, c, y = me.z, me.x, me.c, me.y
    me.greet()
    me.met()

    def local(src, dst, i):
        cp = pltpu.make_async_copy(src, dst, lsem.at[i])
        cp.start()
        return cp

    pieces = []
    owns = []
    for k, (src, rows, n) in enumerate(((g2_ref, 64, 256), (g1_ref, 16, 1024))):
        for half in range(2):
            j = k * 2 + half
            own = local(
                src.at[:, :, c, :, :, pl.ds(half * n, n)], s4[j], 10 + j
            )
            out = gf2_ref if k == 0 else gf1_ref

            def done(v, out=out, c0=half * n, n=n):
                out[:, c0 : c0 + n] = v

            pieces.append((src, half * n, n, half == 0, own, s4[j], r14[j], r24[j], r34[j], r44[j], done))
    for half in range(2):

        def done(v, c0=half * 256):
            gp_ref[:, c0 : c0 + 256] = v

        pieces.append(
            (pgrad, half * 256, 256, half == 0, None, sp.at[half], r1p.at[half], r2p.at[half], r3p.at[half], r4p.at[half], done)
        )
    for g in range(4):

        def done(v, g=g):
            for k in range(3):
                gq_ref[:, k * 512 + g * 128 : k * 512 + g * 128 + 128] = v[:, k * 128 : k * 128 + 128]

        pieces.append(
            (qgrad.at[g], 0, 384, g % 2 == 0, None, sq.at[g], r1q.at[g], r2q.at[g], r3q.at[g], r4q.at[g], done)
        )
    sca = Scatter(me, pieces, ssem, rsem)
    for k in range(4):
        sca.start(k, 0)
    load_c = local(ctxt_h, ctxt, 0)
    load_p = local(wp_h, wp, 1)
    load_q = local(qkv_save.at[0], qb, 2)
    load_a = local(att_save, a_ref, 3)
    load_n = local(normt_h, normt, 4)
    load_t = local(nt_h, nt, 5)
    load_w = local(wqb_h, wq, 6)
    load_m = local(mg_h, mg, 7)
    for b in range(8):
        for k in range(4):
            bs[k, b * 256 : b * 256 + 240, :] = br_ref[b, 16:256, k * 128 : k * 128 + 128].astype(F32)
    for b in range(8):
        for k in range(4):
            bs[k, b * 256 + 240 : b * 256 + 256, :] = bhalo[b, :, k * 128 : k * 128 + 128].astype(F32)
    for p in range(16):
        lo, hi = spots(p)
        for k in range(4):
            bp[p * 128 : p * 128 + 128, k * 128 : k * 128 + 128] = gathered(bs.at[k], lo, hi).astype(BF)
    plan = [list(part) for part in PLAN_SCATTER]

    def progress():
        if plan:
            for k, s in plan.pop(0):
                sca.advance(k, s)

    progress()
    load_c.wait()
    pgrad[...] = dot(ctxt[...], bp[...]).astype(BF).reshape(4, 2, 2, 2, 16, 512)
    sca.start(4, 0)
    sca.start(5, 0)
    progress()
    load_p.wait()
    load_a.wait()
    cells[...] = jnp.zeros_like(cells)
    lanes = lax.broadcasted_iota(jnp.int32, (16, 128), 1)
    for g in range(4):
        fs = slice(g * 128, (g + 1) * 128)

        def context_grad(t, carry, fs=fs):
            out = dot(wp[fs, :], bp[pl.ds(pl.multiple_of(t * 512, 512), 512), :], NT)
            for k in range(4):
                dc[pl.ds(t * 4 + k, 128, stride=16), :] = (
                    out[:, k * 128 : (k + 1) * 128].astype(BF).astype(F32)
                )
            return carry

        lax.fori_loop(0, 4, context_grad, 0)
        load_q.wait()

        def widen(i, carry):
            rows = pl.ds(pl.multiple_of(i * 512, 512), 512)
            g_ref[rows, :] = qb[rows, :].astype(F32)
            return carry

        lax.fori_loop(0, 12, widen, 0)
        if g < 3:
            load_q = local(qkv_save.at[g + 1], qb, 2)
        progress()

        def head(h, carry, g=g):
            da = pair_products(dc, h * 32, g_ref, 256 + h * 32)
            a0 = (g * 4 + h) * 16
            at = [tile(a_ref, a0 + q) for q in range(16)]
            tot = tree([da[q] * at[q] for q in range(16)])
            ds = []
            mine = lanes == g * 4 + h
            for q in range(16):
                low_ref[q * 16 : q * 16 + 16, :] = at[q].astype(BF).astype(F32)
                d = (at[q] * (da[q] - tot)).astype(BF).astype(F32)
                ds_ref[q * 16 : q * 16 + 16, :] = d
                ds.append(d)
                cell = jnp.sum(d, axis=1, keepdims=True)
                cells[q * 16 : q * 16 + 16, :] += jnp.where(mine, cell, 0.0)
            weighted(ds, g_ref, 128 + h * 32, dg, h * 32, SCALE)
            turned = [ds_ref[pl.ds(p, 16, stride=16), :] for p in range(16)]
            weighted(turned, g_ref, h * 32, dg, 128 + h * 32, SCALE)
            turned = [low_ref[pl.ds(p, 16, stride=16), :] for p in range(16)]
            weighted(turned, dc, h * 32, dg, 256 + h * 32, None)
            return carry

        for h in range(4):
            lax.fori_loop(h, h + 1, head, 0)
            progress()
        sums = jnp.zeros((384, 128), F32)
        for p in range(16):
            v = dg[pl.ds(p, 384, stride=16), :]
            sums = sums + v
            dqt[g * 384 : (g + 1) * 384, p * 128 : (p + 1) * 128] = v.astype(BF)
        ar[g, 2:3, :] = jnp.sum(sums[0:128].T, 0, keepdims=True)
        ar[g, 3:4, :] = jnp.sum(sums[256:384].T, 0, keepdims=True)
        if g == 0:
            load_n.wait()
        rows = slice(g * 384, g * 384 + 384)
        qgrad[g] = dot(normt[...], dqt[rows, :], NT).astype(BF).reshape(4, 2, 2, 2, 16, 384)
        sca.start(6 + g, 0)
        progress()
    load_w.wait()
    load_t.wait()
    wall = wq[:, :, :, :, :, 128:1664].reshape(512, 1536)
    gain = jnp.broadcast_to(wq_gain(wq), (512, 128))
    gacc[...] = jnp.zeros_like(gacc)

    def held(p):
        return (dg, p * 512) if p < 12 else (g_ref, (p - 12) * 512)

    for t in range(4):
        e4 = dot(wall, dqt[:, t * 512 : t * 512 + 512])
        for k in range(4):
            e = e4[:, k * 128 : (k + 1) * 128]
            ref, at = held(t * 4 + k)
            ref[at : at + 512, :] = e
        es = [e4[:, k * 128 : (k + 1) * 128] for k in range(4)]
        ns = [nt[:, t * 512 + k * 128 : t * 512 + k * 128 + 128].astype(F32) for k in range(4)]
        gacc[0] += tree([e * n for e, n in zip(es, ns)])
        gacc[1] += tree(es)
        progress()
    for zz in range(4):
        ls = slice(zz * 128, zz * 128 + 128)
        for k in range(2):
            ar[zz, k : k + 1, :] = jnp.sum(gacc[k, ls, :].T, 0, keepdims=True)
        ar[zz, 4:8, :] = small_ref[4:8, ls]
        for k in range(4):
            ar[zz, 8 + k : 9 + k, :] = small_ref[8 + zz : 9 + zz, k * 128 : k * 128 + 128]
        ar[zz, 12:16, :] = jnp.zeros((4, 128), F32)
    pair = lax.broadcasted_iota(jnp.int32, (256, 128), 0)
    entry = lax.broadcasted_iota(jnp.int32, (256, 128), 1)
    qi, pi = pair // 16, pair % 16
    index = (pi // 4 - qi // 4 + 3) * 7 + pi % 4 - qi % 4 + 3
    table = lax.dot_general(
        cells[...], (index == entry).astype(F32), TN,
        precision=lax.Precision.HIGHEST, preferred_element_type=F32,
    )
    ar[4] = table[0:16]
    progress()
    small = [
        remote(ar, arr.at[0], asems.at[0], aremr.at[0], me.over_core),
        remote(ar, arr.at[1], asems.at[1], aremr.at[1], me.over_x),
        remote(ar, arr.at[2], asems.at[2], aremr.at[2], me.over_y),
    ]
    small[0].start()

    def norm_back(p):
        ref, at = held(p)
        n = nt[:, p * 128 : p * 128 + 128].astype(F32)
        eg = ref[at : at + 512, :] * gain
        m2 = jnp.mean(eg * n, 0, keepdims=True)
        r = (eg - jnp.mean(eg, 0, keepdims=True) - n * m2) * rs_ref[p : p + 1, :]
        lo, hi = spots(p)
        for q in range(4):
            turned = r[q * 128 : q * 128 + 128].T
            bs[q, pl.ds(lo, 64, stride=32), :] = turned[0:64]
            bs[q, pl.ds(hi, 64, stride=32), :] = turned[64:128]

    for p in range(8, 12):
        norm_back(p)
    small[0].wait()
    ar[...] = ar[...] + arr[0]
    small[1].start()
    for p in range(12, 16):
        norm_back(p)
    for b in range(8):
        for k in range(4):
            rout[b, :, k * 128 : k * 128 + 128] = bs[k, b * 256 + 240 : b * 256 + 256, :].astype(BF)
    rh = remote(rout, rhalo, hss.at[1], hrs.at[1], me.over_y)
    rh.start()
    small[1].wait()
    ar[...] = ar[...] + arr[1]
    small[2].start()
    progress()
    for p in range(8):
        norm_back(p)
    load_m.wait()
    small[2].wait()
    ar[...] = ar[...] + arr[2]
    last = []
    for d in range(3):
        to = (z + 1 + d) % 4
        last.append(remote(ar.at[to], arz.at[z, 0], asems.at[3 + d], aremr.at[3 + d], me.along_z[d]))
        last.append(remote(ar.at[4], arz.at[z, 1], asems.at[6 + d], aremr.at[6 + d], me.along_z[d]))
    for cp in last:
        cp.start()
    arz[z, 0] = ar[z]
    arz[z, 1] = ar[4]
    progress()
    for b in range(8):
        for k in range(4):
            ls = slice(k * 128, k * 128 + 128)
            ig_ref[b, 16:256, ls] = (
                mg[k, b * 256 + 16 : b * 256 + 256, :] + bs[k, b * 256 : b * 256 + 240, :]
            ).astype(BF)
    rh.wait()
    for b in range(8):
        for k in range(4):
            ls = slice(k * 128, k * 128 + 128)
            ig_ref[b, 0:16, ls] = (
                mg[k, b * 256 : b * 256 + 16, :] + rhalo[b, :, ls].astype(F32)
            ).astype(BF)
    while plan:
        progress()
    for cp in last:
        cp.wait()
    total = (arz[0] + arz[1]) + (arz[2] + arz[3])
    mine = pltpu.roll(total[0], (8 - me.rank8) * 16 % 128, 1)
    ar[0] = total[0]
    fb = ar[0, pl.ds(8 + x * 2 + c, 1), :]
    vec_ref[0:8, :] = mine[0:8]
    vec_ref[8:9, :] = jnp.where(y == 0, fb, pltpu.roll(fb, 64, 1))
    vec_ref[9:16, :] = jnp.zeros((7, 128), F32)
    vec_ref[16:32, :] = total[1]
    sca.close()


def wq_gain(wq):
    parts = []
    for zz in range(4):
        total = jnp.sum(wq[zz, :, :, :, :, 0:128].astype(F32).reshape(8, 16, 128), axis=0)
        parts.append(total.T[:, 0:1])
    return jnp.concatenate(parts, 0)


def k3_call(br, bhalo, mg, g1, g2, small, wqb, wp, qs, asv, ctxt, normt, nt, rs):
    S = jax.ShapeDtypeStruct
    V = pltpu.VMEM
    lead = (4, 2, 2, 2)
    half = (4, 2, 2)
    outs = [S((8, 256, 512), BF), S((16, 1536), F32), S((16, 512), F32), S((16, 2048), F32), S((64, 512), F32)]
    outs += [S((32, 128), F32)]

    def four(shape):
        return [V(shape + (64, 256), BF)] * 2 + [V(shape + (16, 1024), BF)] * 2

    fours = [four(half), four(half), four((4, 2)), four((4,)), four((3,))]
    rest = []
    for count, n in ((2, 256), (4, 384)):
        for shape in (half, half, (4, 2), (4,), (3,)):
            rest.append(V((count,) + shape + (16, n), BF))
    scratch = [
        V((4, 2048, 128), F32), V((2048, 512), BF), V((4, 2048, 128), F32), V(lead + (16, 1664), BF),
        V((512, 512), BF), V((6144, 128), BF), V((6144, 128), F32), V((6144, 128), F32),
        V((2048, 128), F32), V((4096, 128), F32), V((1536, 2048), BF), V((512, 2048), BF),
        V((512, 2048), BF), V((512, 2048), BF), V((256, 128), F32), V((256, 128), F32),
        V((2, 512, 128), F32), V(lead + (16, 512), BF), V((4,) + lead + (16, 384), BF),
        V((8, 16, 512), BF), V((8, 16, 512), BF), V((256, 128), F32),
        V((5, 16, 128), F32), V((3, 5, 16, 128), F32), V((4, 2, 16, 128), F32),
    ]
    sems = [
        pltpu.SemaphoreType.DMA((10, 6)), pltpu.SemaphoreType.DMA((10, 6)),
        pltpu.SemaphoreType.DMA((2,)), pltpu.SemaphoreType.DMA((2,)), pltpu.SemaphoreType.DMA((14,)),
        pltpu.SemaphoreType.DMA((9,)), pltpu.SemaphoreType.DMA((9,)),
    ]

    def body(*refs):
        n = 14 + len(outs) + len(scratch)
        flat = refs[n : n + 20]
        groups = [flat[i * 4 : i * 4 + 4] for i in range(5)]
        k3_body(*refs[:n], *groups, *refs[n + 20 :])

    return pl.pallas_call(
        body,
        out_shape=outs,
        in_specs=[VM, VM, HB, HB, HB, VM, HB, HB, HB, HB, HB, HB, HB, VM],
        out_specs=[VM] * len(outs),
        scratch_shapes=scratch + sum(fours, []) + rest + sems,
        compiler_params=pltpu.CompilerParams(
            collective_id=2, has_side_effects=True, vmem_limit_bytes=62 << 20
        ),
        name="attend_back_scatter",
    )(br, bhalo, mg, g1, g2, small, wqb, wp, qs, asv, ctxt, normt, nt, rs)


def k4_body(out, ig, gq, gp, g1, g2, vec, out_o, ig_o, gq_o, gp_o, g1_o, g2_o, *small):
    out_o[...] = out[...]
    ig_o[...] = ig[...]

    @pl.when(pl.program_id(0) == 0)
    def _():
        for a, b in ((gq, gq_o), (gp, gp_o), (g1, g1_o), (g2, g2_o)):
            b[...] = a[...]
        for k in range(8):
            small[k][...] = vec[k : k + 1, 0:16]
        small[8][...] = vec[8:9, 0:64]
        small[9][...] = vec[16:32, 0:TABLE]


def k4_call(out, ig, gq, gp, g1, g2, vec):
    S = jax.ShapeDtypeStruct
    outs = [S(a.shape, a.dtype) for a in (out, ig, gq, gp, g1, g2)]
    outs += [S((1, 16), F32)] * 8 + [S((1, 64), F32), S((16, TABLE), F32)]
    step = pl.BlockSpec((2, 256, 512), lambda i: (i, 0, 0))

    def fixed(a):
        return pl.BlockSpec(a.shape, lambda i: (0, 0))

    return pl.pallas_call(
        k4_body,
        grid=(4,),
        out_shape=outs,
        in_specs=[step, step] + [fixed(a) for a in (gq, gp, g1, g2, vec)],
        out_specs=[step, step] + [fixed(a) for a in outs[2:]],
        compiler_params=pltpu.CompilerParams(vmem_limit_bytes=60 << 20),
        name="hand_over",
    )(out, ig, gq, gp, g1, g2, vec)


HEADS = 16
HEAD_DIM = 32
WIN = 4
SHIFT = 2
TABLE = 49


epsilon = 1e-06
highest = lax.Precision.HIGHEST


def from_behind(block, axis, distance):
    devices = range(lax.axis_size(axis))
    route = [((i - distance) % len(devices), i) for i in devices]
    return lax.ppermute(block, axis, route)


def normalize(values, gain_row, bias_row):
    average = jnp.mean(values, -1, keepdims=True)
    centred = values - average
    variance = jnp.mean(centred * centred, -1, keepdims=True)
    return centred * lax.rsqrt(variance + epsilon) * gain_row + bias_row


def exact_gelu(values):
    return jax.nn.gelu(values, approximate=False)


def table_onehot():
    positions = jnp.arange(WIN * WIN)
    row_of = positions // WIN
    column_of = positions % WIN
    table_index = (
        (row_of[:, None] - row_of[None, :] + WIN - 1) * (2 * WIN - 1)
        + column_of[:, None]
        - column_of[None, :]
        + WIN
        - 1
    )
    return (table_index.reshape(-1)[:, None] == jnp.arange(TABLE)[None, :]).astype(jnp.float32)


def to_windows(field_grid):
    clip_count, row_count, column_count, feature_width = field_grid.shape
    blocks = field_grid.reshape(
        clip_count, row_count // WIN, WIN, column_count // WIN, WIN, feature_width
    )
    return blocks.transpose(0, 1, 3, 2, 4, 5).reshape(-1, WIN * WIN, feature_width)


def from_windows(windows, clip_count, row_count, column_count):
    feature_width = windows.shape[-1]
    blocks = windows.reshape(
        clip_count, row_count // WIN, column_count // WIN, WIN, WIN, feature_width
    )
    return blocks.transpose(0, 1, 3, 2, 4, 5).reshape(
        clip_count, row_count, column_count, feature_width
    )


def times_transposed(left, right):
    return lax.dot_general(
        left, right, (((1,), (1,)), ((), ())), preferred_element_type=jnp.float32
    )


def outer_sum(left, right):
    return lax.dot_general(
        left, right, (((0,), (0,)), ((), ())), preferred_element_type=jnp.float32
    )


def per_device(
    inputs,
    grad_mask,
    cotangent,
    ln1_gain,
    ln1_bias,
    w_qkv,
    q_bias,
    v_bias,
    w_proj,
    proj_bias,
    ln2_gain,
    ln2_bias,
    w_fc1,
    fc1_bias,
    w_fc2,
    fc2_bias,
    pos_table,
):
    (
        gain_one,
        bias_one,
        qkv_full,
        qbias_full,
        vbias_full,
        proj_full,
        pbias_full,
        gain_two,
        bias_two,
        fc1_full,
        fc1b_full,
        fc2_full,
        fc2b_full,
    ) = (
        lax.all_gather(ln1_gain, ("clip", "slab"), axis=0, tiled=True),
        lax.all_gather(ln1_bias, ("clip", "slab"), axis=0, tiled=True),
        lax.all_gather(w_qkv, ("clip", "slab"), axis=0, tiled=True),
        lax.all_gather(q_bias, ("clip", "slab"), axis=0, tiled=True),
        lax.all_gather(v_bias, ("clip", "slab"), axis=0, tiled=True),
        lax.all_gather(w_proj, ("clip", "slab"), axis=0, tiled=True),
        lax.all_gather(proj_bias, ("clip", "slab"), axis=0, tiled=True),
        lax.all_gather(ln2_gain, ("clip", "slab"), axis=0, tiled=True),
        lax.all_gather(ln2_bias, ("clip", "slab"), axis=0, tiled=True),
        lax.all_gather(w_fc1, ("clip", "slab"), axis=0, tiled=True),
        lax.all_gather(fc1_bias, ("clip", "slab"), axis=0, tiled=True),
        lax.all_gather(w_fc2, ("clip", "slab"), axis=0, tiled=True),
        lax.all_gather(fc2_bias, ("clip", "slab"), axis=0, tiled=True),
    )
    clip_count, row_count, column_count, feature_width = inputs.shape
    score_scale = 1.0 / math.sqrt(HEAD_DIM)
    float_type = jnp.float32
    half_type = jnp.bfloat16
    ahead = from_behind(inputs[:, :SHIFT], "slab", -1)
    window_rows = jnp.concatenate([inputs[:, SHIFT:], ahead], axis=1).astype(float_type)
    normed, first_pull = jax.vjp(
        normalize, window_rows, gain_one.astype(float_type), bias_one.astype(float_type)
    )
    windows = to_windows(jnp.roll(normed.astype(half_type), -SHIFT, axis=2))
    window_count = windows.shape[0]
    token_count = window_count * WIN * WIN
    head_shape = (window_count, WIN * WIN, HEADS, HEAD_DIM)
    flat_windows = windows.reshape(token_count, feature_width)
    projected = jnp.dot(flat_windows, qkv_full, preferred_element_type=float_type)
    query_heads = (
        (projected[:, :feature_width] + qbias_full.astype(float_type))
        .astype(half_type)
        .reshape(head_shape)
    )
    key_heads = (
        projected[:, feature_width : 2 * feature_width].astype(half_type).reshape(head_shape)
    )
    value_heads = (
        (projected[:, 2 * feature_width :] + vbias_full.astype(float_type))
        .astype(half_type)
        .reshape(head_shape)
    )
    onehot = table_onehot()
    position_bias = (
        jnp.dot(onehot, pos_table, precision=highest)
        .reshape(WIN * WIN, WIN * WIN, HEADS)
        .transpose(2, 0, 1)
    )
    scores = (
        jnp.einsum("wqhc,wkhc->whqk", query_heads, key_heads, preferred_element_type=float_type)
        * score_scale
        + position_bias[None]
    )
    attention = jax.nn.softmax(scores, axis=-1)
    attention_low = attention.astype(half_type)
    context = jnp.einsum(
        "whqk,wkhc->wqhc", attention_low, value_heads, preferred_element_type=float_type
    )
    context = context.astype(half_type).reshape(window_count, WIN * WIN, feature_width)
    context_grid = jnp.roll(
        from_windows(context, clip_count, row_count, column_count), SHIFT, axis=2
    )
    returned = from_behind(context_grid[:, row_count - SHIFT :], "slab", 1)
    own_flat = jnp.concatenate([returned, context_grid[:, : row_count - SHIFT]], axis=1).reshape(
        -1, feature_width
    )
    input_flat = inputs.reshape(-1, feature_width).astype(float_type)
    middle = (
        input_flat
        + jnp.dot(own_flat, proj_full, preferred_element_type=float_type)
        + pbias_full.astype(float_type)
    )
    second, second_pull = jax.vjp(
        normalize, middle, gain_two.astype(float_type), bias_two.astype(float_type)
    )
    second_low = second.astype(half_type)
    pre_act = jnp.dot(second_low, fc1_full, preferred_element_type=float_type) + fc1b_full.astype(
        float_type
    )
    hidden, gelu_pull = jax.vjp(exact_gelu, pre_act)
    hidden_low = hidden.astype(half_type)
    output = (
        middle
        + jnp.dot(hidden_low, fc2_full, preferred_element_type=float_type)
        + fc2b_full.astype(float_type)
    )
    incoming = (cotangent.astype(float_type) * grad_mask.astype(float_type)[..., None]).reshape(
        -1, feature_width
    )
    incoming_low = incoming.astype(half_type)
    fc2_grad = outer_sum(hidden_low, incoming_low)
    fc2b_grad = jnp.sum(incoming, axis=0)
    hidden_grad = times_transposed(incoming_low, fc2_full)
    pre_grad = gelu_pull(hidden_grad)[0].astype(half_type)
    fc1_grad = outer_sum(second_low, pre_grad)
    fc1b_grad = jnp.sum(pre_grad.astype(float_type), axis=0)
    second_grad = times_transposed(pre_grad, fc1_full)
    middle_part, gain_two_grad, bias_two_grad = second_pull(second_grad)
    middle_grad = incoming + middle_part
    branch_low = middle_grad.astype(half_type)
    proj_grad = outer_sum(own_flat, branch_low)
    pbias_grad = jnp.sum(branch_low.astype(float_type), axis=0)
    context_grad = (
        times_transposed(branch_low, proj_full)
        .astype(half_type)
        .reshape(clip_count, row_count, column_count, feature_width)
    )
    sent_back = from_behind(context_grad[:, :SHIFT], "slab", -1)
    window_context_grad = jnp.concatenate([context_grad[:, SHIFT:], sent_back], axis=1)
    context_heads = to_windows(jnp.roll(window_context_grad, -SHIFT, axis=2)).reshape(head_shape)
    value_grad = jnp.einsum(
        "whqk,wqhc->wkhc", attention_low, context_heads, preferred_element_type=float_type
    ).astype(half_type)
    attention_grad = jnp.einsum(
        "wqhc,wkhc->whqk", context_heads, value_heads, preferred_element_type=float_type
    )
    score_grad = (
        attention * (attention_grad - jnp.sum(attention_grad * attention, -1, keepdims=True))
    ).astype(half_type)
    bias_cells = (
        jnp.sum(score_grad.astype(float_type), axis=0)
        .transpose(1, 2, 0)
        .reshape(WIN * WIN * WIN * WIN, HEADS)
    )
    table_grad = lax.dot_general(onehot, bias_cells, (((0,), (0,)), ((), ())), precision=highest)
    query_grad = (
        jnp.einsum("whqk,wkhc->wqhc", score_grad, key_heads, preferred_element_type=float_type)
        * score_scale
    ).astype(half_type)
    key_grad = (
        jnp.einsum("whqk,wqhc->wkhc", score_grad, query_heads, preferred_element_type=float_type)
        * score_scale
    ).astype(half_type)
    query_flat = query_grad.reshape(token_count, feature_width)
    value_flat = value_grad.reshape(token_count, feature_width)
    qkv_grad_low = jnp.concatenate(
        [query_flat, key_grad.reshape(token_count, feature_width), value_flat], axis=1
    )
    qkv_grad = outer_sum(flat_windows, qkv_grad_low)
    qbias_grad = jnp.sum(query_flat.astype(float_type), axis=0)
    vbias_grad = jnp.sum(value_flat.astype(float_type), axis=0)
    normed_grad = times_transposed(qkv_grad_low, qkv_full).reshape(
        window_count, WIN * WIN, feature_width
    )
    normed_grid_grad = jnp.roll(
        from_windows(normed_grad, clip_count, row_count, column_count), SHIFT, axis=2
    )
    rows_part, gain_one_grad, bias_one_grad = first_pull(normed_grid_grad)
    halo_back = from_behind(
        rows_part[:, row_count - SHIFT :].astype(jnp.bfloat16), "slab", 1
    ).astype(jnp.float32)
    input_grad = middle_grad.reshape(
        clip_count, row_count, column_count, feature_width
    ) + jnp.concatenate([halo_back, rows_part[:, : row_count - SHIFT]], axis=1)
    shares = (
        lax.psum_scatter(gain_one_grad, ("clip", "slab"), scatter_dimension=0, tiled=True),
        lax.psum_scatter(bias_one_grad, ("clip", "slab"), scatter_dimension=0, tiled=True),
        lax.psum_scatter(qkv_grad, ("clip", "slab"), scatter_dimension=0, tiled=True),
        lax.psum_scatter(qbias_grad, ("clip", "slab"), scatter_dimension=0, tiled=True),
        lax.psum_scatter(vbias_grad, ("clip", "slab"), scatter_dimension=0, tiled=True),
        lax.psum_scatter(proj_grad, ("clip", "slab"), scatter_dimension=0, tiled=True),
        lax.psum_scatter(pbias_grad, ("clip", "slab"), scatter_dimension=0, tiled=True),
        lax.psum_scatter(gain_two_grad, ("clip", "slab"), scatter_dimension=0, tiled=True),
        lax.psum_scatter(bias_two_grad, ("clip", "slab"), scatter_dimension=0, tiled=True),
        lax.psum_scatter(fc1_grad, ("clip", "slab"), scatter_dimension=0, tiled=True),
        lax.psum_scatter(fc1b_grad, ("clip", "slab"), scatter_dimension=0, tiled=True),
        lax.psum_scatter(fc2_grad, ("clip", "slab"), scatter_dimension=0, tiled=True),
        lax.psum_scatter(fc2b_grad, ("clip", "slab"), scatter_dimension=0, tiled=True),
    )
    table_total = lax.psum(table_grad, ("clip", "slab"))
    output = output.reshape(clip_count, row_count, column_count, feature_width).astype(half_type)
    return (
        output,
        input_grad.astype(half_type),
        shares[0],
        shares[1],
        shares[2],
        shares[3],
        shares[4],
        shares[5],
        shares[6],
        shares[7],
        shares[8],
        shares[9],
        shares[10],
        shares[11],
        shares[12],
        table_total,
    )


def per_device_fast(
    inputs,
    grad_mask,
    cotangent,
    ln1_gain,
    ln1_bias,
    w_qkv,
    q_bias,
    v_bias,
    w_proj,
    proj_bias,
    ln2_gain,
    ln2_bias,
    w_fc1,
    fc1_bias,
    w_fc2,
    fc2_bias,
    pos_table,
):
    smalls = [
        v.reshape(1, 16)
        for v in (ln1_gain, ln1_bias, q_bias, v_bias, proj_bias, ln2_gain, ln2_bias, fc2_bias)
    ]
    shape = inputs.shape
    x = inputs.reshape(8, 256, 512)
    output, mg, br, bhalo, g1, g2, small, wqb, wpb, qs, asv, ctxt, normt, nt, rs = k1_call(
        x, cotangent.reshape(2048, 512), grad_mask.transpose(0, 2, 1), w_qkv, w_proj, w_fc1, w_fc2,
        smalls, fc1_bias.reshape(1, 64), pos_table.T
    )
    lead = (4, 2, 2, 2)
    third = k3_call(
        br, bhalo, mg, g1.reshape(lead + (16, 2048)),
        g2.reshape(lead + (64, 512)), small, wqb, wpb.reshape(512, 512), qs, asv, ctxt, normt, nt, rs
    )
    output, input_grad, gq, gp, gf1, gf2, *vectors, fb, table = k4_call(output, *third)
    v = [r.reshape(16) for r in vectors]
    return (
        output.reshape(shape), input_grad.reshape(shape), v[0], v[1], gq, v[2], v[3], gp, v[4], v[5],
        v[6], gf1, fb.reshape(64), gf2, v[7], table.T,
    )


def solution(mesh):
    in_specs = (
        P("clip", "slab", None, None),
        P("clip", "slab", None),
        P("clip", "slab", None, None),
        P(("clip", "slab")),
        P(("clip", "slab")),
        P(("clip", "slab"), None),
        P(("clip", "slab")),
        P(("clip", "slab")),
        P(("clip", "slab"), None),
        P(("clip", "slab")),
        P(("clip", "slab")),
        P(("clip", "slab")),
        P(("clip", "slab"), None),
        P(("clip", "slab")),
        P(("clip", "slab"), None),
        P(("clip", "slab")),
        P(),
    )
    out_specs = (
        P("clip", "slab", None, None),
        P("clip", "slab", None, None),
        P(("clip", "slab")),
        P(("clip", "slab")),
        P(("clip", "slab"), None),
        P(("clip", "slab")),
        P(("clip", "slab")),
        P(("clip", "slab"), None),
        P(("clip", "slab")),
        P(("clip", "slab")),
        P(("clip", "slab")),
        P(("clip", "slab"), None),
        P(("clip", "slab")),
        P(("clip", "slab"), None),
        P(("clip", "slab")),
        P(),
    )
    fits = mesh.shape["clip"] == 16 and mesh.shape["slab"] == 2
    return jax.shard_map(
        per_device_fast if fits else per_device, mesh=mesh, in_specs=in_specs, out_specs=out_specs, check_vma=False
    )
```

```python
import functools
import math

import jax
import jax.numpy as jnp
from jax import lax
from jax.experimental import pallas as pl
from jax.experimental.pallas import tpu as pltpu
from jax.sharding import PartitionSpec as P

F32 = jnp.float32
BF = jnp.bfloat16
MESH = pl.DeviceIdType.MESH
SCALE = 1.0 / math.sqrt(32.0)
NT = (((1,), (1,)), ((), ()))
TN = (((0,), (0,)), ((), ()))
VM = pl.BlockSpec(memory_space=pltpu.VMEM)
HB = pl.BlockSpec(memory_space=pl.ANY)
UNROLL = 16
TABLE = 49


def dot(a, b, dims=(((1,), (0,)), ((), ()))):
    return lax.dot_general(a, b, dims, preferred_element_type=F32)


def tree(xs, op=lambda a, b: a + b):
    xs = list(xs)
    while len(xs) > 1:
        xs = [op(xs[i], xs[i + 1]) if i + 1 < len(xs) else xs[i] for i in range(0, len(xs), 2)]
    return xs[0]


def tile(ref, i):
    return ref[pl.ds(pl.multiple_of(i * 16, 16), 16), :]


def row(ref, i):
    return jnp.broadcast_to(ref[pl.ds(i, 1), :], (16, 128))


def pair_products(a_ref, a0, b_ref, b0):
    def body(d, acc):
        ad = tile(a_ref, a0 + d)
        return tuple(acc[q] + ad * row(b_ref, (b0 + d) * 16 + q) for q in range(16))

    return lax.fori_loop(
        0, 32, body, tuple(jnp.zeros((16, 128), F32) for _ in range(16)), unroll=UNROLL
    )


def weighted(ws, b_ref, b0, o_ref, o0, scale):
    def body(d, carry):
        parts = []
        for k in range(4):
            t = ws[4 * k] * row(b_ref, (b0 + d) * 16 + 4 * k)
            for q in range(4 * k + 1, 4 * k + 4):
                t = t + ws[q] * row(b_ref, (b0 + d) * 16 + q)
            parts.append(t)
        s = (parts[0] + parts[1]) + (parts[2] + parts[3])
        if scale is not None:
            s = s * scale
        o_ref[pl.ds(pl.multiple_of((o0 + d) * 16, 16), 16), :] = s.astype(BF).astype(F32)
        return carry

    lax.fori_loop(0, 32, body, 0, unroll=UNROLL)


class Place:
    def __init__(self):
        self.clip = lax.axis_index("clip")
        self.y = lax.axis_index("slab")
        self.c = self.clip % 2
        self.x = (self.clip // 2) % 2
        self.z = self.clip // 4
        self.rank8 = self.x * 4 + self.c * 2 + self.y
        base = self.x * 2 + self.c
        self.along_z = [(((self.z + d) % 4) * 4 + base, self.y) for d in (1, 2, 3)]
        self.over_x = (self.clip + 2 - 4 * self.x, self.y)
        self.over_y = (self.clip, 1 - self.y)
        self.over_core = (self.clip + 1 - 2 * self.c, self.y)

    def greet(self):
        barrier = pltpu.get_barrier_semaphore()
        others = self.along_z + [self.over_x, self.over_y, self.over_core]
        for other in others:
            pl.semaphore_signal(barrier, inc=1, device_id=other, device_id_type=MESH)

    def met(self):
        pl.semaphore_wait(pltpu.get_barrier_semaphore(), 6)


def remote(src, dst, ssem, rsem, to):
    return pltpu.make_async_remote_copy(
        src_ref=src, dst_ref=dst, send_sem=ssem, recv_sem=rsem, device_id=to, device_id_type=MESH
    )


class Gather:
    def __init__(self, place, pieces, ssem, rsem):
        self.copies = []
        z, x, c, y = place.z, place.x, place.c, place.y
        for k, (buf, c0, n, first_x, first) in enumerate(pieces):
            cols = pl.ds(c0, n)

            def cp(ix, s, to, k=k, buf=buf, cols=cols):
                ref = buf.at[ix + (slice(None), cols)]
                return remote(ref, ref, ssem.at[k, s], rsem.at[k, s], to)

            al = slice(None)
            mine = buf.at[z, x, c, y, :, cols]
            steps = [
                [
                    remote(
                        mine if first is None else first.at[:, cols],
                        mine,
                        ssem.at[k, d],
                        rsem.at[k, d],
                        place.along_z[d],
                    )
                    for d in range(3)
                ]
            ]
            if first_x:
                steps.append([cp((al, x, c, y), 3, place.over_x)])
                steps.append([cp((al, al, c, y), 4, place.over_y)])
            else:
                steps.append([cp((al, x, c, y), 3, place.over_y)])
                steps.append([cp((al, x, c, al), 4, place.over_x)])
            steps.append([cp((al, al, c, al), 5, place.over_core)])
            self.copies.append(steps)

    def start(self, k, s):
        for copy in self.copies[k][s]:
            copy.start()

    def advance(self, k, s):
        for copy in self.copies[k][s]:
            copy.wait_recv()
        if s < 3:
            self.start(k, s + 1)

    def close(self):
        for steps in self.copies:
            for step in steps:
                for copy in step:
                    copy.wait_send()


CH = 512
FJ = 512


def gelu_parts(a):
    t = 1.0 / (1.0 + 0.2316418882 * jnp.abs(a))
    e = jnp.exp2(a * a * -0.7213475204444817)
    p = 0.5307027145 * t - 0.7265760135
    p = p * t + 0.7107068705
    p = p * t - 0.142248368
    p = p * t + 0.127414796
    tail = p * t * e
    return jnp.where(a >= 0, 1.0 - tail, tail), e * 0.3989422804014327


CH = 512
FJ = 512


PLAN_GATHER = (((0, 0), (1, 0)), (), ((2, 0),), (), ((3, 0),), ((0, 1), (1, 1)), ((4, 0),), ((2, 1), (5, 0)), ((6, 0),), ((3, 1), (1, 2), (0, 2), (1, 3), (0, 3)), ((4, 1), (7, 0)), ((6, 1),), ((2, 2),), (), ((2, 3), (3, 2), (5, 1)), ((8, 0),), ((3, 3), (4, 2)), (), ((4, 3), (5, 2), (9, 0)), (), ((5, 3), (7, 1)), (), ((6, 2), (8, 1), (10, 0)), (), ((6, 3),), (), ((9, 1),), (), (), (), ((7, 2),), (), (), ((7, 3),), ((8, 2),), ((10, 1),), ((8, 3),), (), (), (), (), (), ((9, 2),), ((10, 2),), ((9, 3),), ((10, 3),), ())


def spots(p):
    i, j = p // 4, p % 4
    return (i * 8 + (j + 2) % 8, i * 8 + (j + 6) % 8)


def gathered(ref, lo, hi):
    return jnp.concatenate([ref[pl.ds(lo, 64, stride=32), :], ref[pl.ds(hi, 64, stride=32), :]], axis=0)


def position_bias(tab_ref, bt_ref):
    for p in range(0, 16, 4):
        entry = lax.broadcasted_iota(jnp.int32, (TABLE, 512), 0)
        lane = lax.broadcasted_iota(jnp.int32, (TABLE, 512), 1)
        pi = lane // 128 + p
        qi = lane % 128
        index = (pi // 4 - qi // 4 + 3) * 7 + pi % 4 - qi % 4 + 3
        one = ((index == entry) & (qi < 16)).astype(F32)
        res = jnp.dot(
            tab_ref[...], one, precision=lax.Precision.HIGHEST, preferred_element_type=F32
        )
        for k in range(4):
            bt_ref[pl.ds(p + k, 16, stride=16), :] = res[:, k * 128 : (k + 1) * 128]


def small_block(place, small_refs, fc1b_ref, scr):
    scr[...] = jnp.zeros_like(scr)
    for k, ref in enumerate(small_refs):
        scr[k : k + 1, 0:16] = ref[...].astype(F32)
    lane = lax.broadcasted_iota(jnp.int32, (128, 128), 1)
    src = lax.broadcasted_iota(jnp.int32, (128, 128), 0)
    sel = ((lane == place.rank8 * 16 + src) & (src < 16)).astype(F32).astype(BF)
    vectors = dot(scr[...].astype(BF), sel)
    scr[0:1, 0:64] = fc1b_ref[...].astype(F32)
    half = ((lane == place.y * 64 + src) & (src < 64)).astype(F32).astype(BF)
    wide = dot(scr[0:1, :].astype(BF), half)
    r = lax.broadcasted_iota(jnp.int32, (16, 128), 0)
    return jnp.where(
        r < 8,
        vectors,
        jnp.where(r == 8 + place.x * 2 + place.c, jnp.broadcast_to(wide, (16, 128)), 0.0),
    ).astype(BF)


def k1_body(
    x_h, cot_h, mask_ref, wq_ref, wp_ref, w1_ref, w2_ref, s0, s1, s2, s3, s4, s5, s6, s7, fb_ref, tab_ref,
    out_h, mg_h, br_h, bhalo_ref, g1_h, g2_h, small_ref,
    wqb_h, wp_h, qkv_save, att_save, ctxt_h, normt_h, nt_h, rs_ref,
    ctx_ref, wpb, w1b, w2b, par_ref, x_ref, xs, big, cs_ref, a_ref, qb, halo, chalo, gains, scr,
    wqb, ctxt_ref, normt_ref, nt_ref, bt_ref, cot, hid_ref, pg_ref, sec_ref, br,
    ssem, rsem, hss, hrs, lsem, osem, csem,
):
    g_ref = big.at[pl.ds(0, 6144), :]
    ct_ref = big.at[pl.ds(6144, 2048), :]
    me = Place()
    z, x, c, y = me.z, me.x, me.c, me.y
    own = [
        pltpu.make_async_copy(src, buf.at[z, x, c, y], osem.at[i])
        for i, (src, buf) in enumerate(((wp_ref, wpb), (w1_ref, w1b), (w2_ref, w2b)))
    ]
    for cp in own:
        cp.start()
    xload = pltpu.make_async_copy(x_h, x_ref, osem.at[3])
    xload.start()
    cload = pltpu.make_async_copy(cot_h, cot, osem.at[4])
    cload.start()
    me.greet()
    for g in range(4):
        for k in range(3):
            wqb[z, x, c, y, :, 128 + g * 384 + k * 128 : 256 + g * 384 + k * 128] = wq_ref[
                :, k * 512 + g * 128 : k * 512 + g * 128 + 128
            ]
    wqb[z, x, c, y, :, 0:128] = small_block(me, (s0, s1, s2, s3, s4, s5, s6, s7), fb_ref, scr)
    pieces = [(wqb, 0, 256, True, None), (wqb, 256, 256, False, None)]
    pieces += [(wqb, 128 + g * 384, 384, g % 2 == 1, None) for g in (1, 2, 3)]
    pieces += [(wpb, 0, 256, False, wp_ref), (wpb, 256, 256, True, wp_ref)]
    pieces += [(w1b, 0, 1024, False, w1_ref), (w1b, 1024, 1024, True, w1_ref)]
    pieces += [(w2b, 0, 256, False, w2_ref), (w2b, 256, 256, True, w2_ref)]
    gat = Gather(me, pieces, ssem, rsem)
    me.met()
    for k in range(5):
        gat.start(k, 0)
    xhalo = remote(x_h.at[:, 0:16, :], halo, hss.at[4], hrs.at[4], me.over_y)
    xhalo.start()
    plan = [list(part) for part in PLAN_GATHER]

    def progress():
        for k, s in plan.pop(0):
            gat.advance(k, s)

    xload.wait()
    for b in range(8):
        for k in range(4):
            xs[k, b * 256 : b * 256 + 240, :] = x_ref[b, 16:256, k * 128 : k * 128 + 128].astype(F32)
    for k in range(5, 11):
        gat.start(k, 0)
    for cp in own:
        cp.wait()

    def norm_block(p):
        lo, hi = spots(p)
        turned = jnp.concatenate([gathered(xs.at[k], lo, hi).T for k in range(4)], axis=0)
        mean = jnp.mean(turned, 0, keepdims=True)
        cen = turned - mean
        rs = lax.rsqrt(jnp.mean(cen * cen, 0, keepdims=True) + 1e-6)
        big[p * 512 : (p + 1) * 512, :] = cen * rs
        rs_ref[p : p + 1, :] = rs

    progress()
    for p in range(16):
        if p == 8:
            xhalo.wait_recv()
            for b in range(8):
                for k in range(4):
                    xs[k, b * 256 + 240 : b * 256 + 256, :] = halo[
                        b, :, k * 128 : k * 128 + 128
                    ].astype(F32)
        norm_block(p)
        if p % 2 == 1:
            progress()
        if p == 5:
            position_bias(tab_ref, bt_ref)
    progress()
    for zz in range(4):
        total = jnp.sum(wqb[zz, :, :, :, :, 0:128].astype(F32).reshape(8, 16, 128), axis=0)
        par_ref[0:8, zz * 128 : (zz + 1) * 128] = total[0:8]
        for k in range(4):
            par_ref[8 + zz : 9 + zz, k * 128 : (k + 1) * 128] = total[8 + k : 9 + k]
    par_ref[12:16, :] = jnp.zeros((4, 512), F32)
    turned = par_ref[...].T
    for k in range(4):
        gains[k] = jnp.broadcast_to(turned[:, k : k + 1], (512, 128))

    def finish_norm(p, carry):
        cols = pl.ds(pl.multiple_of(p * 128, 128), 128)
        n = big[pl.ds(pl.multiple_of(p * 512, 512), 512), :]
        normt_ref[:, cols] = (n * gains[0] + gains[1]).astype(BF)
        nt_ref[:, cols] = n.astype(BF)
        return carry

    for t in range(4):
        lax.fori_loop(t * 4, t * 4 + 4, finish_norm, 0)
        progress()

    outs = []
    sends = []

    def out(src, dst, i):
        cp = pltpu.make_async_copy(src, dst, lsem.at[i])
        cp.start()
        outs.append(cp)

    out(normt_ref, normt_h, 8)
    out(nt_ref, nt_h, 9)
    save = None
    for g in range(4):
        w = wqb[:, :, :, :, :, 128 + g * 384 : 512 + g * 384].reshape(512, 384)
        wt = w.astype(F32).T.astype(BF)
        fs = slice(g * 128, (g + 1) * 128)
        if save is not None:
            save.wait()
        for t in range(2):
            res = dot(wt, normt_ref[:, t * 1024 : t * 1024 + 1024])
            for k in range(8):
                block = res[:, k * 128 : (k + 1) * 128]
                block = jnp.concatenate(
                    [block[0:128] + gains[2, fs, :], block[128:256], block[256:384] + gains[3, fs, :]],
                    axis=0,
                )
                g_ref[pl.ds(t * 8 + k, 384, stride=16), :] = block.astype(BF).astype(F32)
            if t == 0:
                progress()

        def keep(i, carry):
            rows = pl.ds(pl.multiple_of(i * 512, 512), 512)
            qb[rows, :] = g_ref[rows, :].astype(BF)
            return carry

        lax.fori_loop(0, 12, keep, 0)
        save = pltpu.make_async_copy(qb, qkv_save.at[g], lsem.at[g])
        save.start()
        if g == 3:
            out(wqb, wqb_h, 10)
        progress()

        def head(h, carry, g=g):
            acc = pair_products(g_ref, h * 32, g_ref, 128 + h * 32)
            bt = tile(bt_ref, g * 4 + h)
            s = [
                acc[q] * SCALE + jnp.broadcast_to(bt[:, q : q + 1], (16, 128)) for q in range(16)
            ]
            m = tree(s, jnp.maximum)
            e = [jnp.exp(v - m) for v in s]
            inv = 1.0 / tree(e)
            low = []
            for q in range(16):
                a = e[q] * inv
                a_ref[pl.ds(pl.multiple_of((g * 4 + h) * 256 + q * 16, 16), 16), :] = a
                low.append(a.astype(BF).astype(F32))
            weighted(low, g_ref, 256 + h * 32, ct_ref, h * 32, None)
            return carry

        for h in range(4):
            lax.fori_loop(h, h + 1, head, 0)
            progress()
        out(a_ref.at[pl.ds(g * 1024, 1024), :], att_save.at[pl.ds(g * 1024, 1024), :], 4 + g)
        for p in range(16):
            block = ct_ref[pl.ds(p, 128, stride=16), :]
            ctxt_ref[fs, p * 128 : (p + 1) * 128] = block.astype(BF)
            turned = block.T
            lo, hi = spots(p)
            cs_ref[pl.ds(lo, 64, stride=32), :] = turned[0:64]
            cs_ref[pl.ds(hi, 64, stride=32), :] = turned[64:128]
        for b in range(8):
            ctx_ref[b, 16:256, fs] = cs_ref[b * 256 : b * 256 + 240, :].astype(BF)
            chalo[g, b] = cs_ref[b * 256 + 240 : b * 256 + 256, :].astype(BF)
        send = remote(chalo.at[g], ctx_ref.at[:, 0:16, pl.ds(g * 128, 128)], hss.at[g], hrs.at[g], me.over_y)
        send.start()
        sends.append(send)
        out(ctxt_ref.at[pl.ds(g * 128, 128), :], ctxt_h.at[pl.ds(g * 128, 128), :], 11 + g)
        progress()
    out(wpb, wp_h, 15)
    cload.wait()
    wp, w1, w2 = wpb.reshape(512, 512), w1b.reshape(512, 2048), w2b.reshape(2048, 512)
    pb, g2, b2, fb2 = (par_ref[k : k + 1, :] for k in (4, 5, 6, 7))
    small_ref[...] = jnp.zeros_like(small_ref)
    rsel = (
        lax.broadcasted_iota(jnp.int32, (256, 32), 0) // 8
        == lax.broadcasted_iota(jnp.int32, (256, 32), 1)
    ).astype(F32).astype(BF)
    csel = lax.broadcasted_iota(jnp.int32, (256, 8), 0) % 8 == lax.broadcasted_iota(
        jnp.int32, (256, 8), 1
    )

    def mask_clip(b, carry):
        rows = pl.ds(pl.multiple_of(b * 256, 256), 256)
        spread = dot(rsel, mask_ref[b].astype(F32).astype(BF), NT)
        mark = jnp.sum(jnp.where(csel, spread, 0.0), 1, keepdims=True)
        inc = cot[rows, :].astype(F32) * mark
        cot[rows, :] = inc.astype(BF)
        small_ref[7:8, :] += jnp.sum(inc, 0, keepdims=True)
        return carry

    lax.fori_loop(0, 8, mask_clip, 0)
    for cp in sends:
        cp.wait()

    def ahead(i, carry):
        rows = pl.ds(pl.multiple_of(i * CH, CH), CH)
        clips = pl.ds(i * (CH // 256), CH // 256)
        mid = (
            x_ref[clips].reshape(CH, 512).astype(F32) + dot(ctx_ref[clips].reshape(CH, 512), wp[...]) + pb
        )
        for k in range(4):
            xs[k, rows, :] = mid[:, k * 128 : k * 128 + 128]
        cen = mid - jnp.mean(mid, 1, keepdims=True)
        rs = lax.rsqrt(jnp.mean(cen * cen, 1, keepdims=True) + 1e-6)
        sec = (cen * rs * g2 + b2).astype(BF)
        sec_ref[rows, :] = sec
        for j in range(2048 // FJ):
            cols = slice(j * FJ, (j + 1) * FJ)
            pre = dot(sec, w1[:, cols]) + par_ref[8 + j : 9 + j, :]
            cdf, pdf = gelu_parts(pre)
            hid_ref[rows, cols] = (pre * cdf).astype(BF)
            pg_ref[rows, cols] = (cdf + pre * pdf).astype(BF)
        return carry

    for i in range(2048 // CH):
        lax.fori_loop(i, i + 1, ahead, 0)
        progress()
    while plan:
        progress()

    def back_again(i, carry):
        rows = pl.ds(pl.multiple_of(i * CH, CH), CH)
        clips = pl.ds(i * (CH // 256), CH // 256)
        mid = jnp.concatenate([xs[k, rows, :] for k in range(4)], axis=1)
        cen = mid - jnp.mean(mid, 1, keepdims=True)
        rs = lax.rsqrt(jnp.mean(cen * cen, 1, keepdims=True) + 1e-6)
        n2 = cen * rs
        low = cot[rows, :]
        back = None
        for j in range(2048 // FJ):
            cols = slice(j * FJ, (j + 1) * FJ)
            hg = dot(low, w2[cols, :], NT)
            pg = (hg * pg_ref[rows, cols].astype(F32)).astype(BF)
            pg_ref[rows, cols] = pg
            small_ref[8 + j : 9 + j, :] += jnp.sum(pg.astype(F32), 0, keepdims=True)
            s = dot(pg, w1[:, cols], NT)
            back = s if back is None else back + s
        ctx_ref[clips] = (mid + dot(hid_ref[rows, :], w2[...]) + fb2).astype(BF).reshape(
            CH // 256, 256, 512
        )
        pltpu.make_async_copy(ctx_ref.at[clips], out_h.at[clips], csem.at[0, i]).start()
        small_ref[5:6, :] += jnp.sum(back * n2, 0, keepdims=True)
        small_ref[6:7, :] += jnp.sum(back, 0, keepdims=True)
        eg = back * g2
        r = (eg - jnp.mean(eg, 1, keepdims=True) - n2 * jnp.mean(eg * n2, 1, keepdims=True)) * rs
        mg = low.astype(F32) + r
        for k in range(4):
            xs[k, rows, :] = mg[:, k * 128 : k * 128 + 128]
        pltpu.make_async_copy(xs.at[:, rows, :], mg_h.at[:, rows, :], csem.at[1, i]).start()
        low_mg = mg.astype(BF)
        br[clips] = low_mg.reshape(CH // 256, 256, 512)
        pltpu.make_async_copy(br.at[clips], br_h.at[clips], csem.at[2, i]).start()
        small_ref[4:5, :] += jnp.sum(low_mg.astype(F32), 0, keepdims=True)
        return carry

    lax.fori_loop(0, 2048 // CH, back_again, 0)
    bhalo = remote(br.at[:, 0:16, :], bhalo_ref, hss.at[5], hrs.at[5], me.over_y)
    bhalo.start()
    save.wait()
    for cp in outs:
        cp.wait()
    turned = sec_ref[...].astype(F32).T.astype(BF)
    for j in range(8):
        cols = slice(j * 256, j * 256 + 256)
        normt_ref[:, cols] = dot(turned, pg_ref[:, cols]).astype(BF)
    last = [pltpu.make_async_copy(normt_ref, g1_h, csem.at[3, 0])]
    last[0].start()
    turned = cot[...].astype(F32).T.astype(BF)
    for j in range(8):
        cols = slice(j * 256, j * 256 + 256)
        x_ref[j] = dot(turned, hid_ref[:, cols]).T.astype(BF)
    last.append(pltpu.make_async_copy(x_ref, g2_h, csem.at[3, 1]))
    last[1].start()
    for i in range(2048 // CH):
        rows = pl.ds(i * CH, CH)
        clips = pl.ds(i * (CH // 256), CH // 256)
        pltpu.make_async_copy(ctx_ref.at[clips], out_h.at[clips], csem.at[0, i]).wait()
        pltpu.make_async_copy(xs.at[:, rows, :], mg_h.at[:, rows, :], csem.at[1, i]).wait()
        pltpu.make_async_copy(br.at[clips], br_h.at[clips], csem.at[2, i]).wait()
    for cp in last:
        cp.wait()
    bhalo.wait()
    xhalo.wait_send()
    gat.close()


def k1_call(x, cot, mask, wq, wp, w1, w2, smalls, fb, tab):
    S = jax.ShapeDtypeStruct
    lead = (4, 2, 2, 2)
    outs = [
        (S((8, 256, 512), BF), HB),
        (S((4, 2048, 128), F32), HB),
        (S((8, 256, 512), BF), HB),
        (S((8, 16, 512), BF), VM),
        (S((512, 2048), BF), HB),
        (S((8, 256, 512), BF), HB),
        (S((16, 512), F32), VM),
        (S(lead + (16, 1664), BF), HB),
        (S(lead + (16, 512), BF), HB),
        (S((4, 6144, 128), BF), HB),
        (S((4096, 128), F32), HB),
        (S((512, 2048), BF), HB),
        (S((512, 2048), BF), HB),
        (S((512, 2048), BF), HB),
        (S((16, 128), F32), VM),
    ]
    V = pltpu.VMEM
    D = pltpu.SemaphoreType.DMA
    return pl.pallas_call(
        k1_body,
        out_shape=[o[0] for o in outs],
        in_specs=[HB, HB] + [VM] * 15,
        out_specs=[o[1] for o in outs],
        scratch_shapes=[
            V((8, 256, 512), BF), V(lead + (16, 512), BF), V(lead + (16, 2048), BF),
            V(lead + (64, 512), BF), V((16, 512), F32),
            V((8, 256, 512), BF), V((4, 2048, 128), F32), V((8192, 128), F32),
            V((2048, 128), F32), V((4096, 128), F32), V((6144, 128), BF),
            V((8, 16, 512), BF), V((4, 8, 16, 128), BF), V((4, 512, 128), F32), V((16, 128), F32),
            V(lead + (16, 1664), BF), V((512, 2048), BF), V((512, 2048), BF), V((512, 2048), BF), V((256, 128), F32),
            V((2048, 512), BF), V((2048, 2048), BF), V((2048, 2048), BF), V((2048, 512), BF), V((8, 256, 512), BF),
            D((11, 6)), D((11, 6)), D((6,)), D((6,)), D((16,)), D((5,)), D((4, 4)),
        ],
        compiler_params=pltpu.CompilerParams(
            collective_id=1, has_side_effects=True, vmem_limit_bytes=62 << 20
        ),
        name="gather_attend_feed",
    )(x, cot, mask, wq, wp, w1, w2, *smalls, fb, tab)
PLAN_SCATTER = (((0, 0), (1, 0), (2, 0)), ((3, 0),), (), ((4, 0), (5, 0)), (), (), ((0, 1), (1, 1)), (), (), ((2, 1), (3, 1), (6, 0)), ((4, 1), (5, 1)), (), ((0, 2), (1, 2)), (), ((2, 2), (3, 2)), ((4, 2), (6, 1), (7, 0)), ((0, 3), (5, 2)), ((1, 3), (6, 2)), (), ((2, 3), (7, 1)), (), ((3, 3), (8, 0)), ((4, 3), (5, 3), (7, 2)), ((6, 3),), ((7, 3), (8, 1)), (), ((8, 2), (9, 0)), (), ((8, 3), (9, 1)), (), ((9, 2),), (), (), ((9, 3),))


class Scatter:
    def __init__(self, place, pieces, ssem, rsem):
        self.me = place
        self.pieces = pieces
        self.steps = []
        z, x, c, y = place.z, place.x, place.c, place.y
        al = slice(None)
        for k, (src, c0, n, first_y, own, s, r1, r2, r3, r4, done) in enumerate(pieces):
            cols = pl.ds(c0, n)

            def cp(a, b, i, to, k=k):
                return remote(a, b, ssem.at[k, i], rsem.at[k, i], to)

            steps = [[cp(src.at[:, :, 1 - c, :, :, cols], r1, 0, place.over_core)]]
            if first_y:
                steps.append([cp(s.at[:, :, 1 - y], r2, 1, place.over_y)])
                steps.append([cp(s.at[:, 1 - x, y], r3, 2, place.over_x)])
            else:
                steps.append([cp(s.at[:, 1 - x], r2, 1, place.over_x)])
                steps.append([cp(s.at[:, x, 1 - y], r3, 2, place.over_y)])
            steps.append(
                [
                    cp(s.at[(z + 1 + d) % 4, x, y], r4.at[d], 3 + d, place.along_z[d])
                    for d in range(3)
                ]
            )
            self.steps.append(steps)

    def start(self, k, i):
        for copy in self.steps[k][i]:
            copy.start()

    def advance(self, k, i):
        me = self.me
        z, x, c, y = me.z, me.x, me.c, me.y
        src, c0, n, first_y, own, s, r1, r2, r3, r4, done = self.pieces[k]
        cols = pl.ds(c0, n)
        for copy in self.steps[k][i]:
            copy.wait_recv()
        if i == 0:
            if own is not None:
                own.wait()

            def add(zz, carry):
                held = s[zz] if own is not None else src[zz, :, c, :, :, cols]
                s[zz] = (held.astype(F32) + r1[zz].astype(F32)).astype(BF)
                return carry

            lax.fori_loop(0, 4, add, 0)
        elif i == 1 and first_y:
            s[:, :, y] = (s[:, :, y].astype(F32) + r2[...].astype(F32)).astype(BF)
        elif i == 1:
            s[:, x] = (s[:, x].astype(F32) + r2[...].astype(F32)).astype(BF)
        elif i == 2:
            s[:, x, y] = (s[:, x, y].astype(F32) + r3[...].astype(F32)).astype(BF)
        else:
            done(tree([s[z, x, y].astype(F32)] + [r4[d].astype(F32) for d in range(3)]))
        if i < 3:
            self.start(k, i + 1)

    def close(self):
        for steps in self.steps:
            for step in steps:
                for copy in step:
                    copy.wait_send()


def k3_body(
    br_ref, bhalo, mg_h, g1_ref, g2_ref, small_ref, wqb_h, wp_h, qkv_save, att_save, ctxt_h, normt_h, nt_h, rs_ref,
    ig_ref, gq_ref, gp_ref, gf1_ref, gf2_ref, vec_ref,
    bs, bp, mg, wq, wp, qb, g_ref, dg, dc, a_ref, dqt, ctxt, normt, nt, ds_ref, low_ref,
    gacc, pgrad, qgrad, rhalo, rout, cells, ar, arr, arz,
    s4, r14, r24, r34, r44, sp, r1p, r2p, r3p, r4p, sq, r1q, r2q, r3q, r4q,
    ssem, rsem, hss, hrs, lsem, asems, aremr,
):
    me = Place()
    z, x, c, y = me.z, me.x, me.c, me.y
    me.greet()
    me.met()

    def local(src, dst, i):
        cp = pltpu.make_async_copy(src, dst, lsem.at[i])
        cp.start()
        return cp

    pieces = []
    owns = []
    for k, (src, rows, n) in enumerate(((g2_ref, 64, 256), (g1_ref, 16, 1024))):
        for half in range(2):
            j = k * 2 + half
            own = local(
                src.at[:, :, c, :, :, pl.ds(half * n, n)], s4[j], 10 + j
            )
            out = gf2_ref if k == 0 else gf1_ref

            def done(v, out=out, c0=half * n, n=n):
                out[:, c0 : c0 + n] = v

            pieces.append((src, half * n, n, half == 0, own, s4[j], r14[j], r24[j], r34[j], r44[j], done))
    for half in range(2):

        def done(v, c0=half * 256):
            gp_ref[:, c0 : c0 + 256] = v

        pieces.append(
            (pgrad, half * 256, 256, half == 0, None, sp.at[half], r1p.at[half], r2p.at[half], r3p.at[half], r4p.at[half], done)
        )
    for g in range(4):

        def done(v, g=g):
            for k in range(3):
                gq_ref[:, k * 512 + g * 128 : k * 512 + g * 128 + 128] = v[:, k * 128 : k * 128 + 128]

        pieces.append(
            (qgrad.at[g], 0, 384, g % 2 == 0, None, sq.at[g], r1q.at[g], r2q.at[g], r3q.at[g], r4q.at[g], done)
        )
    sca = Scatter(me, pieces, ssem, rsem)
    for k in range(4):
        sca.start(k, 0)
    load_c = local(ctxt_h, ctxt, 0)
    load_p = local(wp_h, wp, 1)
    load_q = local(qkv_save.at[0], qb, 2)
    load_a = local(att_save, a_ref, 3)
    load_n = local(normt_h, normt, 4)
    load_t = local(nt_h, nt, 5)
    load_w = local(wqb_h, wq, 6)
    load_m = local(mg_h, mg, 7)
    for b in range(8):
        for k in range(4):
            bs[k, b * 256 : b * 256 + 240, :] = br_ref[b, 16:256, k * 128 : k * 128 + 128].astype(F32)
    for b in range(8):
        for k in range(4):
            bs[k, b * 256 + 240 : b * 256 + 256, :] = bhalo[b, :, k * 128 : k * 128 + 128].astype(F32)
    for p in range(16):
        lo, hi = spots(p)
        for k in range(4):
            bp[p * 128 : p * 128 + 128, k * 128 : k * 128 + 128] = gathered(bs.at[k], lo, hi).astype(BF)
    plan = [list(part) for part in PLAN_SCATTER]

    def progress():
        if plan:
            for k, s in plan.pop(0):
                sca.advance(k, s)

    progress()
    load_c.wait()
    pgrad[...] = dot(ctxt[...], bp[...]).astype(BF).reshape(4, 2, 2, 2, 16, 512)
    sca.start(4, 0)
    sca.start(5, 0)
    progress()
    load_p.wait()
    load_a.wait()
    cells[...] = jnp.zeros_like(cells)
    lanes = lax.broadcasted_iota(jnp.int32, (16, 128), 1)
    for g in range(4):
        fs = slice(g * 128, (g + 1) * 128)

        def context_grad(t, carry, fs=fs):
            out = dot(wp[fs, :], bp[pl.ds(pl.multiple_of(t * 512, 512), 512), :], NT)
            for k in range(4):
                dc[pl.ds(t * 4 + k, 128, stride=16), :] = (
                    out[:, k * 128 : (k + 1) * 128].astype(BF).astype(F32)
                )
            return carry

        lax.fori_loop(0, 4, context_grad, 0)
        load_q.wait()

        def widen(i, carry):
            rows = pl.ds(pl.multiple_of(i * 512, 512), 512)
            g_ref[rows, :] = qb[rows, :].astype(F32)
            return carry

        lax.fori_loop(0, 12, widen, 0)
        if g < 3:
            load_q = local(qkv_save.at[g + 1], qb, 2)
        progress()

        def head(h, carry, g=g):
            da = pair_products(dc, h * 32, g_ref, 256 + h * 32)
            a0 = (g * 4 + h) * 16
            at = [tile(a_ref, a0 + q) for q in range(16)]
            tot = tree([da[q] * at[q] for q in range(16)])
            ds = []
            mine = lanes == g * 4 + h
            for q in range(16):
                low_ref[q * 16 : q * 16 + 16, :] = at[q].astype(BF).astype(F32)
                d = (at[q] * (da[q] - tot)).astype(BF).astype(F32)
                ds_ref[q * 16 : q * 16 + 16, :] = d
                ds.append(d)
                cell = jnp.sum(d, axis=1, keepdims=True)
                cells[q * 16 : q * 16 + 16, :] += jnp.where(mine, cell, 0.0)
            weighted(ds, g_ref, 128 + h * 32, dg, h * 32, SCALE)
            turned = [ds_ref[pl.ds(p, 16, stride=16), :] for p in range(16)]
            weighted(turned, g_ref, h * 32, dg, 128 + h * 32, SCALE)
            turned = [low_ref[pl.ds(p, 16, stride=16), :] for p in range(16)]
            weighted(turned, dc, h * 32, dg, 256 + h * 32, None)
            return carry

        for h in range(4):
            lax.fori_loop(h, h + 1, head, 0)
            progress()
        sums = jnp.zeros((384, 128), F32)
        for p in range(16):
            v = dg[pl.ds(p, 384, stride=16), :]
            sums = sums + v
            dqt[g * 384 : (g + 1) * 384, p * 128 : (p + 1) * 128] = v.astype(BF)
        ar[g, 2:3, :] = jnp.sum(sums[0:128].T, 0, keepdims=True)
        ar[g, 3:4, :] = jnp.sum(sums[256:384].T, 0, keepdims=True)
        if g == 0:
            load_n.wait()
        rows = slice(g * 384, g * 384 + 384)
        qgrad[g] = dot(normt[...], dqt[rows, :], NT).astype(BF).reshape(4, 2, 2, 2, 16, 384)
        sca.start(6 + g, 0)
        progress()
    load_w.wait()
    load_t.wait()
    wall = wq[:, :, :, :, :, 128:1664].reshape(512, 1536)
    gain = jnp.broadcast_to(wq_gain(wq), (512, 128))
    gacc[...] = jnp.zeros_like(gacc)

    def held(p):
        return (dg, p * 512) if p < 12 else (g_ref, (p - 12) * 512)

    for t in range(4):
        e4 = dot(wall, dqt[:, t * 512 : t * 512 + 512])
        for k in range(4):
            e = e4[:, k * 128 : (k + 1) * 128]
            ref, at = held(t * 4 + k)
            ref[at : at + 512, :] = e
        es = [e4[:, k * 128 : (k + 1) * 128] for k in range(4)]
        ns = [nt[:, t * 512 + k * 128 : t * 512 + k * 128 + 128].astype(F32) for k in range(4)]
        gacc[0] += tree([e * n for e, n in zip(es, ns)])
        gacc[1] += tree(es)
        progress()
    for zz in range(4):
        ls = slice(zz * 128, zz * 128 + 128)
        for k in range(2):
            ar[zz, k : k + 1, :] = jnp.sum(gacc[k, ls, :].T, 0, keepdims=True)
        ar[zz, 4:8, :] = small_ref[4:8, ls]
        for k in range(4):
            ar[zz, 8 + k : 9 + k, :] = small_ref[8 + zz : 9 + zz, k * 128 : k * 128 + 128]
        ar[zz, 12:16, :] = jnp.zeros((4, 128), F32)
    pair = lax.broadcasted_iota(jnp.int32, (256, 128), 0)
    entry = lax.broadcasted_iota(jnp.int32, (256, 128), 1)
    qi, pi = pair // 16, pair % 16
    index = (pi // 4 - qi // 4 + 3) * 7 + pi % 4 - qi % 4 + 3
    table = lax.dot_general(
        cells[...], (index == entry).astype(F32), TN,
        precision=lax.Precision.HIGHEST, preferred_element_type=F32,
    )
    ar[4] = table[0:16]
    progress()
    small = [
        remote(ar, arr.at[0], asems.at[0], aremr.at[0], me.over_core),
        remote(ar, arr.at[1], asems.at[1], aremr.at[1], me.over_y),
        remote(ar, arr.at[2], asems.at[2], aremr.at[2], me.over_x),
    ]
    small[0].start()

    def norm_back(p):
        ref, at = held(p)
        n = nt[:, p * 128 : p * 128 + 128].astype(F32)
        eg = ref[at : at + 512, :] * gain
        m2 = jnp.mean(eg * n, 0, keepdims=True)
        r = (eg - jnp.mean(eg, 0, keepdims=True) - n * m2) * rs_ref[p : p + 1, :]
        lo, hi = spots(p)
        for q in range(4):
            turned = r[q * 128 : q * 128 + 128].T
            bs[q, pl.ds(lo, 64, stride=32), :] = turned[0:64]
            bs[q, pl.ds(hi, 64, stride=32), :] = turned[64:128]

    for p in range(8, 12):
        norm_back(p)
    small[0].wait()
    ar[...] = ar[...] + arr[0]
    small[1].start()
    for p in range(12, 16):
        norm_back(p)
    for b in range(8):
        for k in range(4):
            rout[b, :, k * 128 : k * 128 + 128] = bs[k, b * 256 + 240 : b * 256 + 256, :].astype(BF)
    rh = remote(rout, rhalo, hss.at[1], hrs.at[1], me.over_y)
    rh.start()
    small[1].wait()
    ar[...] = ar[...] + arr[1]
    small[2].start()
    progress()
    for p in range(8):
        norm_back(p)
    load_m.wait()
    small[2].wait()
    ar[...] = ar[...] + arr[2]
    last = []
    for d in range(3):
        to = (z + 1 + d) % 4
        last.append(remote(ar.at[to], arz.at[z, 0], asems.at[3 + d], aremr.at[3 + d], me.along_z[d]))
        last.append(remote(ar.at[4], arz.at[z, 1], asems.at[6 + d], aremr.at[6 + d], me.along_z[d]))
    for cp in last:
        cp.start()
    arz[z, 0] = ar[z]
    arz[z, 1] = ar[4]
    progress()
    for b in range(8):
        for k in range(4):
            ls = slice(k * 128, k * 128 + 128)
            ig_ref[b, 16:256, ls] = (
                mg[k, b * 256 + 16 : b * 256 + 256, :] + bs[k, b * 256 : b * 256 + 240, :]
            ).astype(BF)
    rh.wait()
    for b in range(8):
        for k in range(4):
            ls = slice(k * 128, k * 128 + 128)
            ig_ref[b, 0:16, ls] = (
                mg[k, b * 256 : b * 256 + 16, :] + rhalo[b, :, ls].astype(F32)
            ).astype(BF)
    while plan:
        progress()
    for cp in last:
        cp.wait()
    total = (arz[0] + arz[1]) + (arz[2] + arz[3])
    mine = pltpu.roll(total[0], (8 - me.rank8) * 16 % 128, 1)
    ar[0] = total[0]
    fb = ar[0, pl.ds(8 + x * 2 + c, 1), :]
    vec_ref[0:8, :] = mine[0:8]
    vec_ref[8:9, :] = jnp.where(y == 0, fb, pltpu.roll(fb, 64, 1))
    vec_ref[9:16, :] = jnp.zeros((7, 128), F32)
    vec_ref[16:32, :] = total[1]
    sca.close()


def wq_gain(wq):
    parts = []
    for zz in range(4):
        total = jnp.sum(wq[zz, :, :, :, :, 0:128].astype(F32).reshape(8, 16, 128), axis=0)
        parts.append(total.T[:, 0:1])
    return jnp.concatenate(parts, 0)


def k3_call(br, bhalo, mg, g1, g2, small, wqb, wp, qs, asv, ctxt, normt, nt, rs):
    S = jax.ShapeDtypeStruct
    V = pltpu.VMEM
    lead = (4, 2, 2, 2)
    half = (4, 2, 2)
    outs = [S((8, 256, 512), BF), S((16, 1536), F32), S((16, 512), F32), S((16, 2048), F32), S((64, 512), F32)]
    outs += [S((32, 128), F32)]

    def four(shape):
        return [V(shape + (64, 256), BF)] * 2 + [V(shape + (16, 1024), BF)] * 2

    fours = [four(half), four(half), four((4, 2)), four((4,)), four((3,))]
    rest = []
    for count, n in ((2, 256), (4, 384)):
        for shape in (half, half, (4, 2), (4,), (3,)):
            rest.append(V((count,) + shape + (16, n), BF))
    scratch = [
        V((4, 2048, 128), F32), V((2048, 512), BF), V((4, 2048, 128), F32), V(lead + (16, 1664), BF),
        V((512, 512), BF), V((6144, 128), BF), V((6144, 128), F32), V((6144, 128), F32),
        V((2048, 128), F32), V((4096, 128), F32), V((1536, 2048), BF), V((512, 2048), BF),
        V((512, 2048), BF), V((512, 2048), BF), V((256, 128), F32), V((256, 128), F32),
        V((2, 512, 128), F32), V(lead + (16, 512), BF), V((4,) + lead + (16, 384), BF),
        V((8, 16, 512), BF), V((8, 16, 512), BF), V((256, 128), F32),
        V((5, 16, 128), F32), V((3, 5, 16, 128), F32), V((4, 2, 16, 128), F32),
    ]
    sems = [
        pltpu.SemaphoreType.DMA((10, 6)), pltpu.SemaphoreType.DMA((10, 6)),
        pltpu.SemaphoreType.DMA((2,)), pltpu.SemaphoreType.DMA((2,)), pltpu.SemaphoreType.DMA((14,)),
        pltpu.SemaphoreType.DMA((9,)), pltpu.SemaphoreType.DMA((9,)),
    ]

    def body(*refs):
        n = 14 + len(outs) + len(scratch)
        flat = refs[n : n + 20]
        groups = [flat[i * 4 : i * 4 + 4] for i in range(5)]
        k3_body(*refs[:n], *groups, *refs[n + 20 :])

    return pl.pallas_call(
        body,
        out_shape=outs,
        in_specs=[VM, VM, HB, HB, HB, VM, HB, HB, HB, HB, HB, HB, HB, VM],
        out_specs=[VM] * len(outs),
        scratch_shapes=scratch + sum(fours, []) + rest + sems,
        compiler_params=pltpu.CompilerParams(
            collective_id=2, has_side_effects=True, vmem_limit_bytes=62 << 20
        ),
        name="attend_back_scatter",
    )(br, bhalo, mg, g1, g2, small, wqb, wp, qs, asv, ctxt, normt, nt, rs)


def k4_body(out, ig, gq, gp, g1, g2, vec, out_o, ig_o, gq_o, gp_o, g1_o, g2_o, *small):
    out_o[...] = out[...]
    ig_o[...] = ig[...]

    @pl.when(pl.program_id(0) == 0)
    def _():
        for a, b in ((gq, gq_o), (gp, gp_o), (g1, g1_o), (g2, g2_o)):
            b[...] = a[...]
        for k in range(8):
            small[k][...] = vec[k : k + 1, 0:16]
        small[8][...] = vec[8:9, 0:64]
        small[9][...] = vec[16:32, 0:TABLE]


def k4_call(out, ig, gq, gp, g1, g2, vec):
    S = jax.ShapeDtypeStruct
    outs = [S(a.shape, a.dtype) for a in (out, ig, gq, gp, g1, g2)]
    outs += [S((1, 16), F32)] * 8 + [S((1, 64), F32), S((16, TABLE), F32)]
    step = pl.BlockSpec((2, 256, 512), lambda i: (i, 0, 0))

    def fixed(a):
        return pl.BlockSpec(a.shape, lambda i: (0, 0))

    return pl.pallas_call(
        k4_body,
        grid=(4,),
        out_shape=outs,
        in_specs=[step, step] + [fixed(a) for a in (gq, gp, g1, g2, vec)],
        out_specs=[step, step] + [fixed(a) for a in outs[2:]],
        compiler_params=pltpu.CompilerParams(vmem_limit_bytes=60 << 20),
        name="hand_over",
    )(out, ig, gq, gp, g1, g2, vec)


HEADS = 16
HEAD_DIM = 32
WIN = 4
SHIFT = 2
TABLE = 49


epsilon = 1e-06
highest = lax.Precision.HIGHEST


def from_behind(block, axis, distance):
    devices = range(lax.axis_size(axis))
    route = [((i - distance) % len(devices), i) for i in devices]
    return lax.ppermute(block, axis, route)


def normalize(values, gain_row, bias_row):
    average = jnp.mean(values, -1, keepdims=True)
    centred = values - average
    variance = jnp.mean(centred * centred, -1, keepdims=True)
    return centred * lax.rsqrt(variance + epsilon) * gain_row + bias_row


def exact_gelu(values):
    return jax.nn.gelu(values, approximate=False)


def table_onehot():
    positions = jnp.arange(WIN * WIN)
    row_of = positions // WIN
    column_of = positions % WIN
    table_index = (
        (row_of[:, None] - row_of[None, :] + WIN - 1) * (2 * WIN - 1)
        + column_of[:, None]
        - column_of[None, :]
        + WIN
        - 1
    )
    return (table_index.reshape(-1)[:, None] == jnp.arange(TABLE)[None, :]).astype(jnp.float32)


def to_windows(field_grid):
    clip_count, row_count, column_count, feature_width = field_grid.shape
    blocks = field_grid.reshape(
        clip_count, row_count // WIN, WIN, column_count // WIN, WIN, feature_width
    )
    return blocks.transpose(0, 1, 3, 2, 4, 5).reshape(-1, WIN * WIN, feature_width)


def from_windows(windows, clip_count, row_count, column_count):
    feature_width = windows.shape[-1]
    blocks = windows.reshape(
        clip_count, row_count // WIN, column_count // WIN, WIN, WIN, feature_width
    )
    return blocks.transpose(0, 1, 3, 2, 4, 5).reshape(
        clip_count, row_count, column_count, feature_width
    )


def times_transposed(left, right):
    return lax.dot_general(
        left, right, (((1,), (1,)), ((), ())), preferred_element_type=jnp.float32
    )


def outer_sum(left, right):
    return lax.dot_general(
        left, right, (((0,), (0,)), ((), ())), preferred_element_type=jnp.float32
    )


def per_device(
    inputs,
    grad_mask,
    cotangent,
    ln1_gain,
    ln1_bias,
    w_qkv,
    q_bias,
    v_bias,
    w_proj,
    proj_bias,
    ln2_gain,
    ln2_bias,
    w_fc1,
    fc1_bias,
    w_fc2,
    fc2_bias,
    pos_table,
):
    (
        gain_one,
        bias_one,
        qkv_full,
        qbias_full,
        vbias_full,
        proj_full,
        pbias_full,
        gain_two,
        bias_two,
        fc1_full,
        fc1b_full,
        fc2_full,
        fc2b_full,
    ) = (
        lax.all_gather(ln1_gain, ("clip", "slab"), axis=0, tiled=True),
        lax.all_gather(ln1_bias, ("clip", "slab"), axis=0, tiled=True),
        lax.all_gather(w_qkv, ("clip", "slab"), axis=0, tiled=True),
        lax.all_gather(q_bias, ("clip", "slab"), axis=0, tiled=True),
        lax.all_gather(v_bias, ("clip", "slab"), axis=0, tiled=True),
        lax.all_gather(w_proj, ("clip", "slab"), axis=0, tiled=True),
        lax.all_gather(proj_bias, ("clip", "slab"), axis=0, tiled=True),
        lax.all_gather(ln2_gain, ("clip", "slab"), axis=0, tiled=True),
        lax.all_gather(ln2_bias, ("clip", "slab"), axis=0, tiled=True),
        lax.all_gather(w_fc1, ("clip", "slab"), axis=0, tiled=True),
        lax.all_gather(fc1_bias, ("clip", "slab"), axis=0, tiled=True),
        lax.all_gather(w_fc2, ("clip", "slab"), axis=0, tiled=True),
        lax.all_gather(fc2_bias, ("clip", "slab"), axis=0, tiled=True),
    )
    clip_count, row_count, column_count, feature_width = inputs.shape
    score_scale = 1.0 / math.sqrt(HEAD_DIM)
    float_type = jnp.float32
    half_type = jnp.bfloat16
    ahead = from_behind(inputs[:, :SHIFT], "slab", -1)
    window_rows = jnp.concatenate([inputs[:, SHIFT:], ahead], axis=1).astype(float_type)
    normed, first_pull = jax.vjp(
        normalize, window_rows, gain_one.astype(float_type), bias_one.astype(float_type)
    )
    windows = to_windows(jnp.roll(normed.astype(half_type), -SHIFT, axis=2))
    window_count = windows.shape[0]
    token_count = window_count * WIN * WIN
    head_shape = (window_count, WIN * WIN, HEADS, HEAD_DIM)
    flat_windows = windows.reshape(token_count, feature_width)
    projected = jnp.dot(flat_windows, qkv_full, preferred_element_type=float_type)
    query_heads = (
        (projected[:, :feature_width] + qbias_full.astype(float_type))
        .astype(half_type)
        .reshape(head_shape)
    )
    key_heads = (
        projected[:, feature_width : 2 * feature_width].astype(half_type).reshape(head_shape)
    )
    value_heads = (
        (projected[:, 2 * feature_width :] + vbias_full.astype(float_type))
        .astype(half_type)
        .reshape(head_shape)
    )
    onehot = table_onehot()
    position_bias = (
        jnp.dot(onehot, pos_table, precision=highest)
        .reshape(WIN * WIN, WIN * WIN, HEADS)
        .transpose(2, 0, 1)
    )
    scores = (
        jnp.einsum("wqhc,wkhc->whqk", query_heads, key_heads, preferred_element_type=float_type)
        * score_scale
        + position_bias[None]
    )
    attention = jax.nn.softmax(scores, axis=-1)
    attention_low = attention.astype(half_type)
    context = jnp.einsum(
        "whqk,wkhc->wqhc", attention_low, value_heads, preferred_element_type=float_type
    )
    context = context.astype(half_type).reshape(window_count, WIN * WIN, feature_width)
    context_grid = jnp.roll(
        from_windows(context, clip_count, row_count, column_count), SHIFT, axis=2
    )
    returned = from_behind(context_grid[:, row_count - SHIFT :], "slab", 1)
    own_flat = jnp.concatenate([returned, context_grid[:, : row_count - SHIFT]], axis=1).reshape(
        -1, feature_width
    )
    input_flat = inputs.reshape(-1, feature_width).astype(float_type)
    middle = (
        input_flat
        + jnp.dot(own_flat, proj_full, preferred_element_type=float_type)
        + pbias_full.astype(float_type)
    )
    second, second_pull = jax.vjp(
        normalize, middle, gain_two.astype(float_type), bias_two.astype(float_type)
    )
    second_low = second.astype(half_type)
    pre_act = jnp.dot(second_low, fc1_full, preferred_element_type=float_type) + fc1b_full.astype(
        float_type
    )
    hidden, gelu_pull = jax.vjp(exact_gelu, pre_act)
    hidden_low = hidden.astype(half_type)
    output = (
        middle
        + jnp.dot(hidden_low, fc2_full, preferred_element_type=float_type)
        + fc2b_full.astype(float_type)
    )
    incoming = (cotangent.astype(float_type) * grad_mask.astype(float_type)[..., None]).reshape(
        -1, feature_width
    )
    incoming_low = incoming.astype(half_type)
    fc2_grad = outer_sum(hidden_low, incoming_low)
    fc2b_grad = jnp.sum(incoming, axis=0)
    hidden_grad = times_transposed(incoming_low, fc2_full)
    pre_grad = gelu_pull(hidden_grad)[0].astype(half_type)
    fc1_grad = outer_sum(second_low, pre_grad)
    fc1b_grad = jnp.sum(pre_grad.astype(float_type), axis=0)
    second_grad = times_transposed(pre_grad, fc1_full)
    middle_part, gain_two_grad, bias_two_grad = second_pull(second_grad)
    middle_grad = incoming + middle_part
    branch_low = middle_grad.astype(half_type)
    proj_grad = outer_sum(own_flat, branch_low)
    pbias_grad = jnp.sum(branch_low.astype(float_type), axis=0)
    context_grad = (
        times_transposed(branch_low, proj_full)
        .astype(half_type)
        .reshape(clip_count, row_count, column_count, feature_width)
    )
    sent_back = from_behind(context_grad[:, :SHIFT], "slab", -1)
    window_context_grad = jnp.concatenate([context_grad[:, SHIFT:], sent_back], axis=1)
    context_heads = to_windows(jnp.roll(window_context_grad, -SHIFT, axis=2)).reshape(head_shape)
    value_grad = jnp.einsum(
        "whqk,wqhc->wkhc", attention_low, context_heads, preferred_element_type=float_type
    ).astype(half_type)
    attention_grad = jnp.einsum(
        "wqhc,wkhc->whqk", context_heads, value_heads, preferred_element_type=float_type
    )
    score_grad = (
        attention * (attention_grad - jnp.sum(attention_grad * attention, -1, keepdims=True))
    ).astype(half_type)
    bias_cells = (
        jnp.sum(score_grad.astype(float_type), axis=0)
        .transpose(1, 2, 0)
        .reshape(WIN * WIN * WIN * WIN, HEADS)
    )
    table_grad = lax.dot_general(onehot, bias_cells, (((0,), (0,)), ((), ())), precision=highest)
    query_grad = (
        jnp.einsum("whqk,wkhc->wqhc", score_grad, key_heads, preferred_element_type=float_type)
        * score_scale
    ).astype(half_type)
    key_grad = (
        jnp.einsum("whqk,wqhc->wkhc", score_grad, query_heads, preferred_element_type=float_type)
        * score_scale
    ).astype(half_type)
    query_flat = query_grad.reshape(token_count, feature_width)
    value_flat = value_grad.reshape(token_count, feature_width)
    qkv_grad_low = jnp.concatenate(
        [query_flat, key_grad.reshape(token_count, feature_width), value_flat], axis=1
    )
    qkv_grad = outer_sum(flat_windows, qkv_grad_low)
    qbias_grad = jnp.sum(query_flat.astype(float_type), axis=0)
    vbias_grad = jnp.sum(value_flat.astype(float_type), axis=0)
    normed_grad = times_transposed(qkv_grad_low, qkv_full).reshape(
        window_count, WIN * WIN, feature_width
    )
    normed_grid_grad = jnp.roll(
        from_windows(normed_grad, clip_count, row_count, column_count), SHIFT, axis=2
    )
    rows_part, gain_one_grad, bias_one_grad = first_pull(normed_grid_grad)
    halo_back = from_behind(
        rows_part[:, row_count - SHIFT :].astype(jnp.bfloat16), "slab", 1
    ).astype(jnp.float32)
    input_grad = middle_grad.reshape(
        clip_count, row_count, column_count, feature_width
    ) + jnp.concatenate([halo_back, rows_part[:, : row_count - SHIFT]], axis=1)
    shares = (
        lax.psum_scatter(gain_one_grad, ("clip", "slab"), scatter_dimension=0, tiled=True),
        lax.psum_scatter(bias_one_grad, ("clip", "slab"), scatter_dimension=0, tiled=True),
        lax.psum_scatter(qkv_grad, ("clip", "slab"), scatter_dimension=0, tiled=True),
        lax.psum_scatter(qbias_grad, ("clip", "slab"), scatter_dimension=0, tiled=True),
        lax.psum_scatter(vbias_grad, ("clip", "slab"), scatter_dimension=0, tiled=True),
        lax.psum_scatter(proj_grad, ("clip", "slab"), scatter_dimension=0, tiled=True),
        lax.psum_scatter(pbias_grad, ("clip", "slab"), scatter_dimension=0, tiled=True),
        lax.psum_scatter(gain_two_grad, ("clip", "slab"), scatter_dimension=0, tiled=True),
        lax.psum_scatter(bias_two_grad, ("clip", "slab"), scatter_dimension=0, tiled=True),
        lax.psum_scatter(fc1_grad, ("clip", "slab"), scatter_dimension=0, tiled=True),
        lax.psum_scatter(fc1b_grad, ("clip", "slab"), scatter_dimension=0, tiled=True),
        lax.psum_scatter(fc2_grad, ("clip", "slab"), scatter_dimension=0, tiled=True),
        lax.psum_scatter(fc2b_grad, ("clip", "slab"), scatter_dimension=0, tiled=True),
    )
    table_total = lax.psum(table_grad, ("clip", "slab"))
    output = output.reshape(clip_count, row_count, column_count, feature_width).astype(half_type)
    return (
        output,
        input_grad.astype(half_type),
        shares[0],
        shares[1],
        shares[2],
        shares[3],
        shares[4],
        shares[5],
        shares[6],
        shares[7],
        shares[8],
        shares[9],
        shares[10],
        shares[11],
        shares[12],
        table_total,
    )


def per_device_fast(
    inputs,
    grad_mask,
    cotangent,
    ln1_gain,
    ln1_bias,
    w_qkv,
    q_bias,
    v_bias,
    w_proj,
    proj_bias,
    ln2_gain,
    ln2_bias,
    w_fc1,
    fc1_bias,
    w_fc2,
    fc2_bias,
    pos_table,
):
    smalls = [
        v.reshape(1, 16)
        for v in (ln1_gain, ln1_bias, q_bias, v_bias, proj_bias, ln2_gain, ln2_bias, fc2_bias)
    ]
    shape = inputs.shape
    x = inputs.reshape(8, 256, 512)
    output, mg, br, bhalo, g1, g2, small, wqb, wpb, qs, asv, ctxt, normt, nt, rs = k1_call(
        x, cotangent.reshape(2048, 512), grad_mask.transpose(0, 2, 1), w_qkv, w_proj, w_fc1, w_fc2,
        smalls, fc1_bias.reshape(1, 64), pos_table.T
    )
    lead = (4, 2, 2, 2)
    third = k3_call(
        br, bhalo, mg, g1.reshape(lead + (16, 2048)),
        g2.reshape(lead + (64, 512)), small, wqb, wpb.reshape(512, 512), qs, asv, ctxt, normt, nt, rs
    )
    output, input_grad, gq, gp, gf1, gf2, *vectors, fb, table = k4_call(output, *third)
    v = [r.reshape(16) for r in vectors]
    return (
        output.reshape(shape), input_grad.reshape(shape), v[0], v[1], gq, v[2], v[3], gp, v[4], v[5],
        v[6], gf1, fb.reshape(64), gf2, v[7], table.T,
    )


def solution(mesh):
    in_specs = (
        P("clip", "slab", None, None),
        P("clip", "slab", None),
        P("clip", "slab", None, None),
        P(("clip", "slab")),
        P(("clip", "slab")),
        P(("clip", "slab"), None),
        P(("clip", "slab")),
        P(("clip", "slab")),
        P(("clip", "slab"), None),
        P(("clip", "slab")),
        P(("clip", "slab")),
        P(("clip", "slab")),
        P(("clip", "slab"), None),
        P(("clip", "slab")),
        P(("clip", "slab"), None),
        P(("clip", "slab")),
        P(),
    )
    out_specs = (
        P("clip", "slab", None, None),
        P("clip", "slab", None, None),
        P(("clip", "slab")),
        P(("clip", "slab")),
        P(("clip", "slab"), None),
        P(("clip", "slab")),
        P(("clip", "slab")),
        P(("clip", "slab"), None),
        P(("clip", "slab")),
        P(("clip", "slab")),
        P(("clip", "slab")),
        P(("clip", "slab"), None),
        P(("clip", "slab")),
        P(("clip", "slab"), None),
        P(("clip", "slab")),
        P(),
    )
    fits = mesh.shape["clip"] == 16 and mesh.shape["slab"] == 2
    return jax.shard_map(
        per_device_fast if fits else per_device, mesh=mesh, in_specs=in_specs, out_specs=out_specs, check_vma=False
    )
```
